128 devices in a mesh: blk: 8 (over y_hi, x), tp: 16 (over z, y_lo, core).
Axes of the slice: x: 4, y: 4 (y_hi: 2, y_lo: 2; y = y_hi * 2 + y_lo), z: 4, core: 2. Of those that a mesh axis runs over, the one named last changes fastest.
Arguments:
- tokens: bfloat16 [4096, 8192], P('blk')
- segment_ids: int32 [8, 512], P('blk'), may hold values from 0 to 3, never falling along the last dimension, each value on 1 to 256 neighbouring positions
- q_weight: bfloat16 [8192, 8192], P('blk', 'tp'), may hold values from -0.0625 to 0.0625
- key_value_weight: bfloat16 [8192, 2048], P('blk', 'tp'), may hold values from -0.0625 to 0.0625
- o_weight: bfloat16 [8192, 8192], P('blk', 'tp'), may hold values from -0.0625 to 0.0625
- cotangent: bfloat16 [4096, 8192], P('blk'), may hold values from -6 to 6
Outputs:
- mixed: bfloat16 [4096, 8192], P('blk')
- d_tokens: bfloat16 [4096, 8192], P('blk', 'tp')
- q_grad: bfloat16 [8192, 8192], P('blk', 'tp')
- key_value_gradient: bfloat16 [8192, 2048], P('blk', 'tp')
- o_grad: bfloat16 [8192, 8192], P('blk', 'tp')
The draws below stay inside these ranges and needn't reach their ends.
Inputs may be any that keep to these rules, and one draw needn't show every extreme that they name: `segment_ids`: in each micro-batch the document numbers never fall; each document has 1 to 256 tokens, one exactly 256.
All inputs are finite; a program needn't handle non-finite values.
Results may differ from the reference program's by a relative error of at most 0.025.
Values may be sent and summed in bfloat16 or wider, within the bound.
A program may use at most 256 MiB of HBM per device.

```python
import math
import jax
import jax.numpy as jnp
import numpy as np
from jax import lax

MODEL_WIDTH = 8192
QUERY_HEADS = 64
KEY_VALUE_HEADS = 8
HEAD_SIZE = 128
BATCH_TOKENS = 512
SEGS = 4
SEG_MOST = 256
GROUPS = 8
TOKENS = 4096
QPD = 4
KVD = 64
N_BLK = 8
N_TP = 16


def draw_tokens(key, part):
    key = jax.random.fold_in(key, 11)
    base = jax.random.normal(jax.random.fold_in(key, 1), (TOKENS, MODEL_WIDTH), jnp.float32)
    base = jnp.clip(base, -5.0, 5.0)
    return base.astype(jnp.bfloat16)


def steps_of(key, shape, pieces, smallest, high):
    def one(axis_at, shards_of):
        heights = jax.random.uniform(jax.random.fold_in(jax.random.fold_in(key, 6), axis_at), (shards_of,), jnp.float32, smallest / len(pieces), high / len(pieces))
        return jnp.repeat(jnp.exp(heights), shape[axis_at] // shards_of).reshape((-1,) + (1,) * (len(shape) - axis_at - 1))

    factor_of = one(*pieces[0])
    for cut in pieces[1:]:
        factor_of = factor_of * one(*cut)
    return factor_of


def split_up(amount, total, limit, slope):
    weights = [(1 << 20) // math.isqrt(rank ** slope) + 1 for rank in range(2, amount + 1)]
    spare, holding = total - limit - (amount - 1), [1] * (amount - 1)
    while spare > 0:
        free = [i for i in range(amount - 1) if holding[i] < limit]
        mass, left = sum([weights[i] for i in free]), spare
        for i in free:
            extra = min(limit - holding[i], max(1, left * weights[i] // mass), spare)
            holding[i] = holding[i] + extra
            spare = spare - extra
    return np.array([limit] + holding)


def ragged(rng, amount, total, bound, lean):
    if amount == 2:
        one = jax.random.randint(rng, (), max(1, total - bound), min(bound, total - 1) + 1)
        return jnp.stack([one, total - one])
    tallies = jnp.asarray(split_up(amount, total, bound, lean), jnp.int32)
    twos = (amount - 1) // 2
    giver, taker = tallies[1:1 + 2 * twos:2], tallies[2:2 + 2 * twos:2]
    margin = jnp.minimum(giver - 1, bound - taker)
    shifted = jax.random.randint(jax.random.fold_in(rng, 1), (twos,), 0, 1 << 20) % (margin + 1)
    tallies = tallies.at[1:1 + 2 * twos:2].set(giver - shifted).at[2:2 + 2 * twos:2].set(taker + shifted)
    return tallies[jax.random.permutation(jax.random.fold_in(rng, 2), amount)]


def bell_draw(stream_key, extent, scale, limit, pieces=(), kind=jnp.bfloat16):
    drawn = jax.random.normal(stream_key, extent, jnp.float32) * scale
    if len(pieces) > 0:
        drawn = steps_of(stream_key, extent, pieces, -0.22, 0.18) * drawn
    return jnp.clip(drawn, min=-limit, max=limit).astype(kind)


def setup_inputs(seed: int = 0) -> dict:
    splits = jax.random.split(jax.random.key(seed), 7)
    return {
        "tokens": draw_tokens(jax.random.fold_in(splits[6], 71), 0),
        "segment_ids": jax.vmap(lambda own: jnp.searchsorted(jnp.cumsum(ragged(own, SEGS, BATCH_TOKENS, SEG_MOST, 1)), jnp.arange(BATCH_TOKENS), side="right"))(jax.random.split(splits[1], GROUPS)).reshape((GROUPS, BATCH_TOKENS)).astype(jnp.int32),
        "q_weight": bell_draw(splits[2], (MODEL_WIDTH, QUERY_HEADS * HEAD_SIZE), MODEL_WIDTH ** -0.5, 0.0625, ((0, 8), (1, 16))),
        "key_value_weight": bell_draw(splits[3], (MODEL_WIDTH, 2 * KEY_VALUE_HEADS * HEAD_SIZE), MODEL_WIDTH ** -0.5, 0.0625, ((0, 8), (1, 16))),
        "o_weight": bell_draw(splits[4], (MODEL_WIDTH, QUERY_HEADS * HEAD_SIZE), (QUERY_HEADS * HEAD_SIZE) ** -0.5, 0.0625, ((0, 8), (1, 16))),
        "cotangent": bell_draw(splits[5], (TOKENS, MODEL_WIDTH), 1.0, 6.0, ((0, 8),)),
    }


THETA = 10000.0

def rope_tables(length, width):
    half_width = width // 2
    position = jnp.arange(length, dtype=jnp.float32)[:, None]
    channel = jnp.arange(half_width, dtype=jnp.float32)[None, :]
    angle = position * jnp.power(THETA, -2.0 * channel / width)
    return (jnp.cos(angle), jnp.sin(angle))

def rotate(vector, cosine, sine):
    front_half, back_half = jnp.split(vector, 2, axis=-1)
    return jnp.concatenate([front_half * cosine - back_half * sine, back_half * cosine + front_half * sine], axis=-1)

def rotate_back(vector, cosine, sine):
    front_half, back_half = jnp.split(vector, 2, axis=-1)
    return jnp.concatenate([front_half * cosine + back_half * sine, back_half * cosine - front_half * sine], axis=-1)

def rounded_down(array):
    return lax.optimization_barrier(array.astype(jnp.bfloat16)).astype(jnp.float32)

def allowed_mask(segment_row):
    length = segment_row.shape[0]
    places = jnp.arange(length)
    causal = places[None, :] <= places[:, None]
    return causal & (segment_row[:, None] == segment_row[None, :])

def reference(tokens, segment_ids, q_weight, key_value_weight, o_weight, cotangent):
    block_list = N_TP
    group_width = QUERY_HEADS // KEY_VALUE_HEADS
    each_head_width = block_list // KEY_VALUE_HEADS
    score_scale = 1.0 / math.sqrt(HEAD_SIZE)
    key_value_divide = key_value_weight.reshape(MODEL_WIDTH, block_list, 2, KVD)
    key_matrix = key_value_divide[:, :, 0, :].reshape(MODEL_WIDTH, KEY_VALUE_HEADS * HEAD_SIZE)
    value_matrix = key_value_divide[:, :, 1, :].reshape(MODEL_WIDTH, KEY_VALUE_HEADS * HEAD_SIZE)
    cosine, sine = rope_tables(BATCH_TOKENS, HEAD_SIZE)
    cos_heads = cosine[:, None, :]
    sin_heads = sine[:, None, :]
    q_blocks = q_weight.reshape(MODEL_WIDTH, block_list, QPD * HEAD_SIZE).astype(jnp.float32)
    o_blocks = o_weight.reshape(MODEL_WIDTH, block_list, QPD * HEAD_SIZE).astype(jnp.float32)
    key_blocks = key_matrix.reshape(MODEL_WIDTH, block_list, KVD).astype(jnp.float32)
    value_blocks = value_matrix.reshape(MODEL_WIDTH, block_list, KVD).astype(jnp.float32)

    def one_group(carry, inputs):
        token_matrix_rows, cot_rows, segment_row = inputs
        query = jnp.dot(token_matrix_rows, q_weight, preferred_element_type=jnp.float32).reshape(BATCH_TOKENS, QUERY_HEADS, HEAD_SIZE)
        key_matrix_rows = jnp.dot(token_matrix_rows, key_matrix, preferred_element_type=jnp.float32).astype(jnp.bfloat16).reshape(BATCH_TOKENS, KEY_VALUE_HEADS, HEAD_SIZE)
        value_matrix_rows = jnp.dot(token_matrix_rows, value_matrix, preferred_element_type=jnp.float32).astype(jnp.bfloat16).reshape(BATCH_TOKENS, KEY_VALUE_HEADS, HEAD_SIZE)
        query_rot = rotate(query, cos_heads, sin_heads).astype(jnp.bfloat16)
        key_rot = rotate(key_matrix_rows.astype(jnp.float32), cos_heads, sin_heads).astype(jnp.bfloat16)
        key_full = jnp.repeat(key_rot, group_width, axis=1).astype(jnp.float32)
        value_full = jnp.repeat(value_matrix_rows, group_width, axis=1).astype(jnp.float32)
        scores = jnp.einsum('qhd,khd->hqk', query_rot.astype(jnp.float32), key_full) * score_scale
        allowed = allowed_mask(segment_row)
        scores = jnp.where(allowed[None], scores, -jnp.inf)
        top = lax.optimization_barrier(jnp.max(scores, axis=-1, keepdims=True))
        raised = jnp.exp(scores - top)
        probs = raised / lax.optimization_barrier(jnp.sum(raised, axis=-1, keepdims=True))
        probs_low = probs.astype(jnp.bfloat16)
        attn = jnp.einsum('hqk,khd->qhd', probs_low.astype(jnp.float32), value_full).astype(jnp.bfloat16).reshape(BATCH_TOKENS, QUERY_HEADS * HEAD_SIZE)
        out_parts = jnp.einsum('tbc,dbc->btd', attn.reshape(BATCH_TOKENS, block_list, QPD * HEAD_SIZE).astype(jnp.float32), o_blocks)
        mixed = lax.optimization_barrier(jnp.sum(rounded_down(out_parts), axis=0)).astype(jnp.bfloat16)
        d_attn = jnp.dot(cot_rows, o_weight, preferred_element_type=jnp.float32).astype(jnp.bfloat16).reshape(BATCH_TOKENS, QUERY_HEADS, HEAD_SIZE)
        d_prob = jnp.einsum('qhd,khd->hqk', d_attn.astype(jnp.float32), value_full)
        row_delta = lax.optimization_barrier(jnp.sum(probs * d_prob, axis=-1, keepdims=True))
        d_score = (probs * (d_prob - row_delta) * score_scale).astype(jnp.bfloat16)
        d_query = rotate_back(jnp.einsum('hqk,khd->qhd', d_score.astype(jnp.float32), key_full), cos_heads, sin_heads)
        d_query = d_query.astype(jnp.bfloat16).reshape(BATCH_TOKENS, QUERY_HEADS * HEAD_SIZE)
        key_products = jnp.einsum('hqk,qhd->khd', d_score.astype(jnp.float32), query_rot.astype(jnp.float32))
        value_products = jnp.einsum('hqk,qhd->khd', probs_low.astype(jnp.float32), d_attn.astype(jnp.float32))
        key_products = rotate_back(key_products.reshape(BATCH_TOKENS, block_list, QPD, HEAD_SIZE).sum(axis=2), cos_heads, sin_heads)
        value_products = value_products.reshape(BATCH_TOKENS, block_list, QPD, HEAD_SIZE).sum(axis=2)
        key_gradient = rounded_down(key_products).reshape(BATCH_TOKENS, KEY_VALUE_HEADS, each_head_width, HEAD_SIZE).sum(axis=2).astype(jnp.bfloat16).reshape(BATCH_TOKENS, KEY_VALUE_HEADS * HEAD_SIZE)
        value_gradient = rounded_down(value_products).reshape(BATCH_TOKENS, KEY_VALUE_HEADS, each_head_width, HEAD_SIZE).sum(axis=2).astype(jnp.bfloat16).reshape(BATCH_TOKENS, KEY_VALUE_HEADS * HEAD_SIZE)
        terms = jnp.einsum('tbc,dbc->btd', d_query.reshape(BATCH_TOKENS, block_list, QPD * HEAD_SIZE).astype(jnp.float32), q_blocks)
        terms = terms + jnp.einsum('tbc,dbc->btd', key_gradient.reshape(BATCH_TOKENS, block_list, KVD).astype(jnp.float32), key_blocks)
        terms = terms + jnp.einsum('tbc,dbc->btd', value_gradient.reshape(BATCH_TOKENS, block_list, KVD).astype(jnp.float32), value_blocks)
        d_tokens = lax.optimization_barrier(jnp.sum(rounded_down(terms), axis=0)).astype(jnp.bfloat16)
        token_cols = token_matrix_rows.T
        grad_q = rounded_down(jnp.dot(token_cols, d_query, preferred_element_type=jnp.float32))
        grad_k = rounded_down(jnp.dot(token_cols, key_gradient, preferred_element_type=jnp.float32))
        grad_v = rounded_down(jnp.dot(token_cols, value_gradient, preferred_element_type=jnp.float32))
        grad_o = rounded_down(jnp.dot(cot_rows.T, attn, preferred_element_type=jnp.float32))
        carry = (carry[0] + grad_q, carry[1] + grad_k, carry[2] + grad_v, carry[3] + grad_o)
        return (carry, (mixed, d_tokens))
    start_index = (jnp.zeros((MODEL_WIDTH, QUERY_HEADS * HEAD_SIZE), jnp.float32), jnp.zeros((MODEL_WIDTH, KEY_VALUE_HEADS * HEAD_SIZE), jnp.float32), jnp.zeros((MODEL_WIDTH, KEY_VALUE_HEADS * HEAD_SIZE), jnp.float32), jnp.zeros((MODEL_WIDTH, QUERY_HEADS * HEAD_SIZE), jnp.float32))
    inputs = (tokens.reshape(N_BLK, BATCH_TOKENS, MODEL_WIDTH), cotangent.reshape(N_BLK, BATCH_TOKENS, MODEL_WIDTH), segment_ids)
    sums, results = lax.scan(one_group, start_index, inputs)
    mixed = results[0].reshape(TOKENS, MODEL_WIDTH)
    d_tokens = results[1].reshape(TOKENS, MODEL_WIDTH)
    q_grad = sums[0].astype(jnp.bfloat16)
    key_value_gradient = jnp.stack([sums[1].reshape(MODEL_WIDTH, block_list, KVD), sums[2].reshape(MODEL_WIDTH, block_list, KVD)], axis=2)
    key_value_gradient = key_value_gradient.reshape(MODEL_WIDTH, 2 * KEY_VALUE_HEADS * HEAD_SIZE).astype(jnp.bfloat16)
    o_grad = sums[3].astype(jnp.bfloat16)
    return (mixed, d_tokens, q_grad, key_value_gradient, o_grad)
```

```python
import math

import jax
import jax.numpy as jnp
from jax import lax
from jax.sharding import PartitionSpec as P

HEAD_SIZE = 128


THETA = 10000.0


def rope_tables(length, width):
    half_width = width // 2
    position = jnp.arange(length, dtype=jnp.float32)[:, None]
    channel = jnp.arange(half_width, dtype=jnp.float32)[None, :]
    angle = position * jnp.power(THETA, -2.0 * channel / width)
    return (jnp.cos(angle), jnp.sin(angle))


def rotate(vector, cosine, sine):
    front_half, back_half = jnp.split(vector, 2, axis=-1)
    return jnp.concatenate(
        [front_half * cosine - back_half * sine, back_half * cosine + front_half * sine], axis=-1
    )


def rotate_back(vector, cosine, sine):
    front_half, back_half = jnp.split(vector, 2, axis=-1)
    return jnp.concatenate(
        [front_half * cosine + back_half * sine, back_half * cosine - front_half * sine], axis=-1
    )


def allowed_mask(segment_row):
    length = segment_row.shape[0]
    places = jnp.arange(length)
    causal = places[None, :] <= places[:, None]
    return causal & (segment_row[:, None] == segment_row[None, :])


def places(device):
    blk, tp = divmod(device, 16)
    return (*divmod(blk, 4), tp // 4, tp // 2 % 2, tp % 2)


def device_at(h, x, z, low, core):
    return (h * 4 + x) * 16 + z * 4 + low * 2 + core


def move(block, dh=0, dx=0, dz=0, dl=0, dc=0):
    route = []
    for device in range(128):
        h, x, z, low, core = places(device)
        target = device_at(h ^ dh, (x + dx) % 4, (z + dz) % 4, low ^ dl, core ^ dc)
        route.append((device, target))
    return lax.ppermute(block, ("blk", "tp"), route)


def hand_over(block):
    route = []
    for device in range(128):
        h, x, z, low, core = places(device)
        dh, dx = divmod(z * 2 + low, 4)
        blk = (h ^ dh) * 4 + (x - dx) % 4
        route.append((device, blk * 16 + (h * 4 + x) * 2 + core))
    return lax.ppermute(block, ("blk", "tp"), route)


def low_bits(array):
    return array.astype(jnp.bfloat16)


def product(left, right):
    return jnp.dot(left, right, preferred_element_type=jnp.float32)


def product_t(left, right):
    return jnp.einsum("tc,dc->td", left, right, preferred_element_type=jnp.float32)


def column_block(rows, place):
    h, x, z, _, core = place
    height = rows.shape[0] // 8
    width = rows.shape[1] // 8
    mine = lax.dynamic_slice(rows, ((z * 2 + core) * height, 0), (height, rows.shape[1]))
    mine = mine.reshape(height, 8, width)
    pieces = []
    for dh in range(2):
        for dx in range(4):
            target = (h ^ dh) * 4 + (x + dx) % 4
            piece = lax.dynamic_index_in_dim(mine, target, 1, keepdims=False)
            pieces.append(move(piece, dh=dh, dx=dx) if dh or dx else piece)
    own = jnp.stack(pieces)
    below = move(own, dz=1)
    above = move(own, dz=-1)
    far = jnp.concatenate([move(below[:4], dz=1), move(above[4:], dz=-1)])
    buffer = jnp.zeros((8, 8, height, width), rows.dtype)
    for dz, part in ((0, own), (-1, below), (1, above), (2, far)):
        level = (z + dz) % 4
        for other in range(2):
            piece = move(part, dc=1) if other else part
            at = level * 2 + (core ^ other)
            buffer = lax.dynamic_update_slice(buffer, piece[:, None], (0, at, 0, 0))
    return buffer.reshape(8, 8 * height, width)


def reduce_blk(block, weight):
    def term(dh, dx):
        return product(block[dh * 4 + dx], weight)

    first = move(low_bits(term(0, 2)), dx=-1)
    second = move(low_bits(term(1, 2)), dx=1)
    near_right = move(low_bits(term(1, 1)), dx=-1)
    near_left = move(low_bits(term(0, 3)), dx=1)
    sum_left = move(low_bits(term(0, 1) + first), dx=-1)
    sum_right = move(low_bits(term(1, 3) + second), dx=1)
    other = move(low_bits(term(1, 0) + near_right + sum_right), dh=1)
    return term(0, 0) + near_left + sum_left + other


def spread_ring(block, side, ring):
    beside = move(block, **{side: 1})
    left = [move(part, **{ring: 1}) for part in (block, beside)]
    right = [move(part, **{ring: -1}) for part in (block, beside)]
    far = [move(left[0], **{ring: 1}), move(right[1], **{ring: -1})]
    return [block, left[0], far[0], right[0], beside, left[1], far[1], right[1]]


def reduce_tp(pairs, place):
    _, _, z, low, core = place

    def term(dz, half):
        total = 0.0
        for rows, weight in pairs:
            level = (z + dz) % 4
            part = lax.dynamic_index_in_dim(
                rows.reshape(4, rows.shape[0] // 4, -1), level, 0, keepdims=False
            )
            columns = lax.dynamic_index_in_dim(
                weight.reshape(2, weight.shape[0] // 2, -1), half, 0, keepdims=False
            )
            total = total + product_t(part, columns)
        return total

    def both(dz):
        other = move(low_bits(term(dz, 1 - core)), dc=1)
        total = term(dz, core) + other
        return total.reshape(2, total.shape[0] // 2, -1)

    distant = low_bits(both(2))
    first = move(distant[0], dz=-1)
    second = move(distant[1], dz=1)
    lower = both(-1)
    upper = both(1)
    from_above_one = move(low_bits(lower[1]), dz=-1)
    from_below_zero = move(low_bits(upper[0]), dz=1)
    from_above_zero = move(low_bits(lower[0] + first), dz=-1)
    from_below_one = move(low_bits(upper[1] + second), dz=1)
    own = both(0)
    zero = own[0] + from_above_zero + from_below_zero
    one = own[1] + from_above_one + from_below_one
    beside = move(low_bits(jnp.where(low == 0, one, zero)), dl=1)
    return hand_over(low_bits(jnp.where(low == 0, zero, one) + beside))


def spread_tp(block, place):
    _, _, z, low, core = place
    width = block.shape[1]
    result = jnp.zeros((block.shape[0], 16 * width), block.dtype)
    for index, part in enumerate(spread_ring(block, "dl", "dz")):
        dl, dz = divmod(index, 4)
        base = (z - dz) % 4 * 4 + (low ^ dl) * 2
        for other in range(2):
            piece = move(part, dc=1) if other else part
            at = (base + (core ^ other)) * width
            result = lax.dynamic_update_slice(result, piece, (0, at))
    return result


def shards(tokens, segment_ids, q_weight, key_value_weight, o_weight, cotangent):
    length = tokens.shape[0]
    kv_width = key_value_weight.shape[1] // 2
    q_width = q_weight.shape[1]
    local_heads = q_width // HEAD_SIZE
    score_scale = 1.0 / math.sqrt(HEAD_SIZE)
    blk, tp = lax.axis_index("blk"), lax.axis_index("tp")
    place = (blk // 4, blk % 4, tp // 4, tp // 2 % 2, tp % 2)
    core = place[4]
    token_block = column_block(tokens, place)
    cot_block = column_block(cotangent, place)
    in_weight = jnp.concatenate([q_weight, key_value_weight], axis=1)
    projected = reduce_blk(token_block, in_weight)
    d_attn = low_bits(reduce_blk(cot_block, o_weight))
    cosine, sine = rope_tables(length, HEAD_SIZE)
    cos_heads = cosine[:, None, :]
    sin_heads = sine[:, None, :]
    query = projected[:, :q_width].reshape(length, local_heads, HEAD_SIZE)
    kv_local = low_bits(projected[:, q_width:])
    kv_other = move(kv_local, dc=1)
    lower_part = jnp.where(core == 0, kv_local, kv_other)
    upper_part = jnp.where(core == 0, kv_other, kv_local)
    key_matrix_rows = jnp.concatenate([lower_part[:, :kv_width], upper_part[:, :kv_width]], axis=1)
    value_matrix_rows = jnp.concatenate(
        [lower_part[:, kv_width:], upper_part[:, kv_width:]], axis=1
    )
    query_rot = low_bits(rotate(query, cos_heads, sin_heads))
    key_rot = low_bits(rotate(key_matrix_rows.astype(jnp.float32), cosine, sine))
    scores = (
        jnp.einsum("qhd,kd->hqk", query_rot, key_rot, preferred_element_type=jnp.float32)
        * score_scale
    )
    allowed = allowed_mask(segment_ids[0])
    scores = jnp.where(allowed[None], scores, -jnp.inf)
    top = jnp.max(scores, axis=-1, keepdims=True)
    raised = jnp.exp(scores - top)
    probs = raised / jnp.sum(raised, axis=-1, keepdims=True)
    probs_low = low_bits(probs)
    attn = jnp.einsum(
        "hqk,kd->qhd", probs_low, value_matrix_rows, preferred_element_type=jnp.float32
    )
    attn = low_bits(attn).reshape(length, q_width)
    attn_all = jnp.concatenate(spread_ring(attn, "dh", "dx"))
    mixed = spread_tp(reduce_tp([(attn_all, o_weight)], place), place)
    d_attn = d_attn.reshape(length, local_heads, HEAD_SIZE)
    d_prob = jnp.einsum(
        "qhd,kd->hqk", d_attn, value_matrix_rows, preferred_element_type=jnp.float32
    )
    row_delta = jnp.sum(probs * d_prob, axis=-1, keepdims=True)
    d_score = low_bits(probs * (d_prob - row_delta) * score_scale)
    d_query = jnp.einsum("hqk,kd->qhd", d_score, key_rot, preferred_element_type=jnp.float32)
    d_query = low_bits(rotate_back(d_query, cos_heads, sin_heads)).reshape(length, q_width)
    key_part = jnp.einsum("hqk,qhd->kd", d_score, query_rot, preferred_element_type=jnp.float32)
    key_part = low_bits(rotate_back(key_part, cosine, sine))
    value_part = low_bits(
        jnp.einsum("hqk,qhd->kd", probs_low, d_attn, preferred_element_type=jnp.float32)
    )
    own_key = jnp.where(core == 0, key_part[:, :kv_width], key_part[:, kv_width:])
    other_key = jnp.where(core == 0, key_part[:, kv_width:], key_part[:, :kv_width])
    own_value = jnp.where(core == 0, value_part[:, :kv_width], value_part[:, kv_width:])
    other_value = jnp.where(core == 0, value_part[:, kv_width:], value_part[:, :kv_width])
    own_part = jnp.concatenate([own_key, own_value], axis=1)
    other_part = jnp.concatenate([other_key, other_value], axis=1)
    received = move(other_part, dc=1)
    kv_grad_rows = low_bits(own_part.astype(jnp.float32) + received.astype(jnp.float32))
    grad_cols = jnp.concatenate([d_query, kv_grad_rows], axis=1)
    grad_all = jnp.concatenate(spread_ring(grad_cols, "dh", "dx"))
    d_tokens = reduce_tp([(grad_all, in_weight)], place)
    token_rows = token_block.reshape(-1, token_block.shape[2])
    cot_rows = cot_block.reshape(-1, cot_block.shape[2])
    projection_grad = low_bits(
        jnp.einsum("tr,tc->rc", token_rows, grad_all, preferred_element_type=jnp.float32)
    )
    o_grad = low_bits(
        jnp.einsum("tr,tc->rc", cot_rows, attn_all, preferred_element_type=jnp.float32)
    )
    return (mixed, d_tokens, projection_grad[:, :q_width], projection_grad[:, q_width:], o_grad)


def solution(mesh):
    in_specs = (
        P("blk", None),
        P("blk", None),
        P("blk", "tp"),
        P("blk", "tp"),
        P("blk", "tp"),
        P("blk", None),
    )
    out_specs = (P("blk", None), P("blk", "tp"), P("blk", "tp"), P("blk", "tp"), P("blk", "tp"))
    return jax.shard_map(shards, mesh=mesh, in_specs=in_specs, out_specs=out_specs, check_vma=False)
```

```python
import math

import jax
import jax.numpy as jnp
from jax import lax
from jax.experimental import pallas as pl
from jax.experimental.pallas import tpu as pltpu
from jax.sharding import PartitionSpec as P

HEAD_SIZE = 128


THETA = 10000.0


def rope_tables(length, width):
    half_width = width // 2
    position = jnp.arange(length, dtype=jnp.float32)[:, None]
    channel = jnp.arange(half_width, dtype=jnp.float32)[None, :]
    angle = position * jnp.power(THETA, -2.0 * channel / width)
    return (jnp.cos(angle), jnp.sin(angle))


def rotate(vector, cosine, sine):
    front_half, back_half = jnp.split(vector, 2, axis=-1)
    return jnp.concatenate(
        [front_half * cosine - back_half * sine, back_half * cosine + front_half * sine], axis=-1
    )


def rotate_back(vector, cosine, sine):
    front_half, back_half = jnp.split(vector, 2, axis=-1)
    return jnp.concatenate(
        [front_half * cosine + back_half * sine, back_half * cosine - front_half * sine], axis=-1
    )


def allowed_mask(segment_row):
    length = segment_row.shape[0]
    places = jnp.arange(length)
    causal = places[None, :] <= places[:, None]
    return causal & (segment_row[:, None] == segment_row[None, :])


def places(device):
    blk, tp = divmod(device, 16)
    return (*divmod(blk, 4), tp // 4, tp // 2 % 2, tp % 2)


def device_at(h, x, z, low, core):
    return (h * 4 + x) * 16 + z * 4 + low * 2 + core


def move(block, dh=0, dx=0, dz=0, dl=0, dc=0):
    route = []
    for device in range(128):
        h, x, z, low, core = places(device)
        target = device_at(h ^ dh, (x + dx) % 4, (z + dz) % 4, low ^ dl, core ^ dc)
        route.append((device, target))
    return lax.ppermute(block, ("blk", "tp"), route)


def hand_over(block):
    route = []
    for device in range(128):
        h, x, z, low, core = places(device)
        dh, dx = divmod(z * 2 + low, 4)
        blk = (h ^ dh) * 4 + (x - dx) % 4
        route.append((device, blk * 16 + (h * 4 + x) * 2 + core))
    return lax.ppermute(block, ("blk", "tp"), route)


def low_bits(array):
    return array.astype(jnp.bfloat16)


def product(left, right):
    return jnp.dot(left, right, preferred_element_type=jnp.float32)


def product_t(left, right):
    return jnp.einsum("tc,dc->td", left, right, preferred_element_type=jnp.float32)


MESH = pl.DeviceIdType.MESH
BF16 = jnp.bfloat16
F32 = jnp.float32
MIB = 1 << 20


def here():
    blk, tp = lax.axis_index("blk"), lax.axis_index("tp")
    return blk // 4, blk % 4, tp // 4, tp // 2 % 2, tp % 2


def near(place, dh=0, dx=0, dz=0, dl=0, dc=0):
    h, x, z, low, core = place
    h, low, core = (h + dh) % 2, (low + dl) % 2, (core + dc) % 2
    x, z = (x + dx + 4) % 4, (z + dz + 4) % 4
    return h * 4 + x, z * 4 + low * 2 + core


def greet(devices):
    barrier = pltpu.get_barrier_semaphore()
    for device in devices:
        pl.semaphore_signal(barrier, inc=1, device_id=device, device_id_type=MESH)
    pl.semaphore_wait(barrier, len(devices))


def send(source, target, sems, device):
    copy = pltpu.make_async_remote_copy(
        src_ref=source,
        dst_ref=target,
        send_sem=sems[0],
        recv_sem=sems[1],
        device_id=device,
        device_id_type=MESH,
    )
    copy.start()
    return copy


def arrived(ref, sem):
    pltpu.make_async_copy(ref, ref, sem).wait()


CHUNKS = ((0, 2), (1, 2), (1, 1), (0, 3), (0, 1), (1, 3), (1, 0), (0, 0))


def project_kernel(
    tokens, cot, in_weight, o_weight, token_out, cot_out, proj_out, d_attn_out,
    blocks, proj_send, proj_recv, cot_send, cot_recv,
    a2a_s, a2a_r, up_s, up_r, down_s, down_r, far_s, far_r, core_s, core_r, sum_s, sum_r, keep,
):
    place = here()
    h, x, z, low, core = place
    seat = z * 2 + core
    height = blocks.shape[2] // 8
    width = blocks.shape[3]
    right, left = near(place, dx=1), near(place, dx=-1)
    above, below = near(place, dz=1), near(place, dz=-1)
    twin, across = near(place, dc=1), near(place, dh=1)
    shifts = [shift for shift in CHUNKS if shift != (0, 0)]
    greet([near(place, dh=dh, dx=dx) for dh, dx in shifts] + [above, below, twin])
    sent = []

    def rows(a, dh, dx, at):
        return blocks.at[a, dh * 4 + dx, pl.ds(pl.multiple_of(at * height, height), height)]

    def level(dz):
        return (z + dz + 4) % 4 * 2 + core

    def index(dh, dx):
        return dh * 4 + dx

    def start_blocks(a, source):
        for dh, dx in CHUNKS:
            target = near(place, dh=dh, dx=dx)
            piece = source.at[
                pl.ds(pl.multiple_of(seat * height, height), height),
                pl.ds(pl.multiple_of(target[0] * width, width), width),
            ]
            j = index(dh, dx)
            if j:
                sent.append(send(piece, rows(a, dh, dx, seat), (a2a_s.at[a, j], a2a_r.at[a, j]), target))
            else:
                pltpu.make_async_copy(piece, rows(a, 0, 0, seat), a2a_r.at[a, 0]).start()

    def to_twin(a, dh, dx, which, at):
        j = index(dh, dx)
        piece = rows(a, dh, dx, at)
        sent.append(send(piece, piece, (core_s.at[a, j, which], core_r.at[a, j, which]), twin))

    def first_stage(a, dh, dx):
        j = index(dh, dx)
        piece = rows(a, dh, dx, seat)
        arrived(piece, a2a_r.at[a, j])
        sent.append(send(piece, piece, (up_s.at[a, j], up_r.at[a, j]), above))
        sent.append(send(piece, piece, (down_s.at[a, j], down_r.at[a, j]), below))
        to_twin(a, dh, dx, 0, seat)

    def second_stage(a, dh, dx):
        j = index(dh, dx)
        sems = (far_s.at[a, j], far_r.at[a, j])
        lower, upper = rows(a, dh, dx, level(-1)), rows(a, dh, dx, level(1))
        arrived(lower, up_r.at[a, j])
        if dh == 0:
            sent.append(send(lower, lower, sems, above))
        to_twin(a, dh, dx, 1, level(-1))
        arrived(upper, down_r.at[a, j])
        if dh == 1:
            sent.append(send(upper, upper, sems, below))
        to_twin(a, dh, dx, 2, level(1))

    def third_stage(a, dh, dx):
        j = index(dh, dx)
        arrived(rows(a, dh, dx, level(2)), far_r.at[a, j])
        to_twin(a, dh, dx, 3, level(2))

    def complete(a, dh, dx):
        j = index(dh, dx)
        for which, dz in enumerate((0, -1, 1, 2)):
            seat_there = (z + dz + 4) % 4 * 2 + (1 - core)
            arrived(rows(a, dh, dx, seat_there), core_r.at[a, j, which])

    weights = (in_weight, o_weight)
    outgoing = (proj_send, cot_send)
    incoming = (proj_recv, cot_recv)
    results = (proj_out, d_attn_out)
    adds = {4: (0,), 5: (1,), 6: (2, 5), 7: (3, 4, 6)}
    ways = (left, right, left, right, left, right, across)

    def chunk(a, k):
        dh, dx = CHUNKS[k]
        j = index(dh, dx)
        third_stage(a, dh, dx)
        complete(a, dh, dx)
        terms = adds.get(k, ())
        for term in terms:
            arrived(incoming[a].at[term], sum_r.at[a, term])
        target = outgoing[a].at[k] if k < 7 else results[a]
        tile = blocks.shape[2] // 2

        @pl.loop(0, 2)
        def _(step):
            part = pl.ds(pl.multiple_of(step * tile, tile), tile)
            total = jnp.dot(blocks[a, j, part, :], weights[a][...], preferred_element_type=F32)
            for term in terms:
                total = total + incoming[a][term, part, :].astype(F32)
            target[part, :] = total.astype(target.dtype)

        if k < 7:
            sent.append(send(target, incoming[a].at[k], (sum_s.at[a, k], sum_r.at[a, k]), ways[k]))

    start_blocks(0, tokens)
    start_blocks(1, cot)
    for shift in CHUNKS:
        first_stage(0, *shift)
    for shift in CHUNKS:
        second_stage(0, *shift)
    for shift in CHUNKS:
        first_stage(1, *shift)
    for k in range(6):
        chunk(0, k)
        second_stage(1, *CHUNKS[k])
    for k in (6, 7):
        second_stage(1, *CHUNKS[k])
    for k in range(4):
        chunk(1, k)
    chunk(0, 6)
    for k in (4, 5):
        chunk(1, k)
    chunk(0, 7)
    chunk(1, 6)
    chunk(1, 7)
    keeps = [
        pltpu.make_async_copy(blocks.at[0], token_out, keep.at[0]),
        pltpu.make_async_copy(blocks.at[1], cot_out, keep.at[1]),
    ]
    for copy in keeps:
        copy.start()
    for copy in sent:
        copy.wait_send()
    for copy in keeps:
        copy.wait()


def project(tokens, cot, in_weight, o_weight):
    length = tokens.shape[0]
    width = tokens.shape[1] // 8
    in_width, o_width = in_weight.shape[1], o_weight.shape[1]
    dma = pltpu.SemaphoreType.DMA
    pair = [dma((2, 8)), dma((2, 8))]
    block = jax.ShapeDtypeStruct((8, length, width), BF16)
    return pl.pallas_call(
        project_kernel,
        out_shape=(
            block,
            block,
            jax.ShapeDtypeStruct((length, in_width), F32),
            jax.ShapeDtypeStruct((length, o_width), BF16),
        ),
        in_specs=[pl.BlockSpec(memory_space=pl.ANY)] * 2
        + [pl.BlockSpec(memory_space=pltpu.VMEM)] * 2,
        out_specs=(pl.BlockSpec(memory_space=pl.ANY),) * 2
        + (pl.BlockSpec(memory_space=pltpu.VMEM),) * 2,
        scratch_shapes=[
            pltpu.VMEM((2, 8, length, width), BF16),
            pltpu.VMEM((7, length, in_width), BF16),
            pltpu.VMEM((7, length, in_width), BF16),
            pltpu.VMEM((7, length, o_width), BF16),
            pltpu.VMEM((7, length, o_width), BF16),
            *pair,
            *pair,
            *pair,
            *pair,
            dma((2, 8, 4)),
            dma((2, 8, 4)),
            dma((2, 7)),
            dma((2, 7)),
            dma((2,)),
        ],
        compiler_params=pltpu.CompilerParams(
            collective_id=0, has_side_effects=True, vmem_limit_bytes=56 * MIB
        ),
        name="project",
    )(tokens, cot, in_weight, o_weight)


def spread_ring(block, side, ring):
    beside = move(block, **{side: 1})
    left = [move(part, **{ring: 1}) for part in (block, beside)]
    right = [move(part, **{ring: -1}) for part in (block, beside)]
    far = [move(left[0], **{ring: 1}), move(right[1], **{ring: -1})]
    return [block, left[0], far[0], right[0], beside, left[1], far[1], right[1]]


def reduce_tp(pairs, place):
    _, _, z, low, core = place

    def term(dz, half):
        total = 0.0
        for rows, weight in pairs:
            level = (z + dz) % 4
            part = lax.dynamic_index_in_dim(
                rows.reshape(4, rows.shape[0] // 4, -1), level, 0, keepdims=False
            )
            columns = lax.dynamic_index_in_dim(
                weight.reshape(2, weight.shape[0] // 2, -1), half, 0, keepdims=False
            )
            total = total + product_t(part, columns)
        return total

    def both(dz):
        other = move(low_bits(term(dz, 1 - core)), dc=1)
        total = term(dz, core) + other
        return total.reshape(2, total.shape[0] // 2, -1)

    distant = low_bits(both(2))
    first = move(distant[0], dz=-1)
    second = move(distant[1], dz=1)
    lower = both(-1)
    upper = both(1)
    from_above_one = move(low_bits(lower[1]), dz=-1)
    from_below_zero = move(low_bits(upper[0]), dz=1)
    from_above_zero = move(low_bits(lower[0] + first), dz=-1)
    from_below_one = move(low_bits(upper[1] + second), dz=1)
    own = both(0)
    zero = own[0] + from_above_zero + from_below_zero
    one = own[1] + from_above_one + from_below_one
    beside = move(low_bits(jnp.where(low == 0, one, zero)), dl=1)
    return hand_over(low_bits(jnp.where(low == 0, zero, one) + beside))


def spread_tp(block, place):
    _, _, z, low, core = place
    width = block.shape[1]
    result = jnp.zeros((block.shape[0], 16 * width), block.dtype)
    for index, part in enumerate(spread_ring(block, "dl", "dz")):
        dl, dz = divmod(index, 4)
        base = (z - dz) % 4 * 4 + (low ^ dl) * 2
        for other in range(2):
            piece = move(part, dc=1) if other else part
            at = (base + (core ^ other)) * width
            result = lax.dynamic_update_slice(result, piece, (0, at))
    return result


def shards(tokens, segment_ids, q_weight, key_value_weight, o_weight, cotangent):
    length = tokens.shape[0]
    kv_width = key_value_weight.shape[1] // 2
    q_width = q_weight.shape[1]
    local_heads = q_width // HEAD_SIZE
    score_scale = 1.0 / math.sqrt(HEAD_SIZE)
    blk, tp = lax.axis_index("blk"), lax.axis_index("tp")
    place = (blk // 4, blk % 4, tp // 4, tp // 2 % 2, tp % 2)
    core = place[4]
    in_weight = jnp.concatenate([q_weight, key_value_weight], axis=1)
    token_block, cot_block, projected, d_attn = project(tokens, cotangent, in_weight, o_weight)
    cosine, sine = rope_tables(length, HEAD_SIZE)
    cos_heads = cosine[:, None, :]
    sin_heads = sine[:, None, :]
    query = projected[:, :q_width].reshape(length, local_heads, HEAD_SIZE)
    kv_local = low_bits(projected[:, q_width:])
    kv_other = move(kv_local, dc=1)
    lower_part = jnp.where(core == 0, kv_local, kv_other)
    upper_part = jnp.where(core == 0, kv_other, kv_local)
    key_matrix_rows = jnp.concatenate([lower_part[:, :kv_width], upper_part[:, :kv_width]], axis=1)
    value_matrix_rows = jnp.concatenate(
        [lower_part[:, kv_width:], upper_part[:, kv_width:]], axis=1
    )
    query_rot = low_bits(rotate(query, cos_heads, sin_heads))
    key_rot = low_bits(rotate(key_matrix_rows.astype(jnp.float32), cosine, sine))
    scores = (
        jnp.einsum("qhd,kd->hqk", query_rot, key_rot, preferred_element_type=jnp.float32)
        * score_scale
    )
    allowed = allowed_mask(segment_ids[0])
    scores = jnp.where(allowed[None], scores, -jnp.inf)
    top = jnp.max(scores, axis=-1, keepdims=True)
    raised = jnp.exp(scores - top)
    probs = raised / jnp.sum(raised, axis=-1, keepdims=True)
    probs_low = low_bits(probs)
    attn = jnp.einsum(
        "hqk,kd->qhd", probs_low, value_matrix_rows, preferred_element_type=jnp.float32
    )
    attn = low_bits(attn).reshape(length, q_width)
    attn_all = jnp.concatenate(spread_ring(attn, "dh", "dx"))
    mixed = spread_tp(reduce_tp([(attn_all, o_weight)], place), place)
    d_attn = d_attn.reshape(length, local_heads, HEAD_SIZE)
    d_prob = jnp.einsum(
        "qhd,kd->hqk", d_attn, value_matrix_rows, preferred_element_type=jnp.float32
    )
    row_delta = jnp.sum(probs * d_prob, axis=-1, keepdims=True)
    d_score = low_bits(probs * (d_prob - row_delta) * score_scale)
    d_query = jnp.einsum("hqk,kd->qhd", d_score, key_rot, preferred_element_type=jnp.float32)
    d_query = low_bits(rotate_back(d_query, cos_heads, sin_heads)).reshape(length, q_width)
    key_part = jnp.einsum("hqk,qhd->kd", d_score, query_rot, preferred_element_type=jnp.float32)
    key_part = low_bits(rotate_back(key_part, cosine, sine))
    value_part = low_bits(
        jnp.einsum("hqk,qhd->kd", probs_low, d_attn, preferred_element_type=jnp.float32)
    )
    own_key = jnp.where(core == 0, key_part[:, :kv_width], key_part[:, kv_width:])
    other_key = jnp.where(core == 0, key_part[:, kv_width:], key_part[:, :kv_width])
    own_value = jnp.where(core == 0, value_part[:, :kv_width], value_part[:, kv_width:])
    other_value = jnp.where(core == 0, value_part[:, kv_width:], value_part[:, :kv_width])
    own_part = jnp.concatenate([own_key, own_value], axis=1)
    other_part = jnp.concatenate([other_key, other_value], axis=1)
    received = move(other_part, dc=1)
    kv_grad_rows = low_bits(own_part.astype(jnp.float32) + received.astype(jnp.float32))
    grad_cols = jnp.concatenate([d_query, kv_grad_rows], axis=1)
    grad_all = jnp.concatenate(spread_ring(grad_cols, "dh", "dx"))
    d_tokens = reduce_tp([(grad_all, in_weight)], place)
    token_rows = token_block.reshape(-1, token_block.shape[2])
    cot_rows = cot_block.reshape(-1, cot_block.shape[2])
    projection_grad = low_bits(
        jnp.einsum("tr,tc->rc", token_rows, grad_all, preferred_element_type=jnp.float32)
    )
    o_grad = low_bits(
        jnp.einsum("tr,tc->rc", cot_rows, attn_all, preferred_element_type=jnp.float32)
    )
    return (mixed, d_tokens, projection_grad[:, :q_width], projection_grad[:, q_width:], o_grad)


def solution(mesh):
    in_specs = (
        P("blk", None),
        P("blk", None),
        P("blk", "tp"),
        P("blk", "tp"),
        P("blk", "tp"),
        P("blk", None),
    )
    out_specs = (P("blk", None), P("blk", "tp"), P("blk", "tp"), P("blk", "tp"), P("blk", "tp"))
    return jax.shard_map(shards, mesh=mesh, in_specs=in_specs, out_specs=out_specs, check_vma=False)
```

```python
import math

import jax
import jax.numpy as jnp
from jax import lax
from jax.experimental import pallas as pl
from jax.experimental.pallas import tpu as pltpu
from jax.sharding import PartitionSpec as P

HEAD_SIZE = 128


THETA = 10000.0


def rope_tables(length, width):
    half_width = width // 2
    position = jnp.arange(length, dtype=jnp.float32)[:, None]
    channel = jnp.arange(half_width, dtype=jnp.float32)[None, :]
    angle = position * jnp.power(THETA, -2.0 * channel / width)
    return (jnp.cos(angle), jnp.sin(angle))


MESH = pl.DeviceIdType.MESH
BF16 = jnp.bfloat16
F32 = jnp.float32
MIB = 1 << 20


def here():
    blk, tp = lax.axis_index("blk"), lax.axis_index("tp")
    return blk // 4, blk % 4, tp // 4, tp // 2 % 2, tp % 2


def near(place, dh=0, dx=0, dz=0, dl=0, dc=0):
    h, x, z, low, core = place
    h, low, core = (h + dh) % 2, (low + dl) % 2, (core + dc) % 2
    x, z = (x + dx + 4) % 4, (z + dz + 4) % 4
    return h * 4 + x, z * 4 + low * 2 + core


def greet(devices):
    barrier = pltpu.get_barrier_semaphore()
    for device in devices:
        pl.semaphore_signal(barrier, inc=1, device_id=device, device_id_type=MESH)
    pl.semaphore_wait(barrier, len(devices))


def send(source, target, sems, device):
    copy = pltpu.make_async_remote_copy(
        src_ref=source,
        dst_ref=target,
        send_sem=sems[0],
        recv_sem=sems[1],
        device_id=device,
        device_id_type=MESH,
    )
    copy.start()
    return copy


def arrived(ref, sem):
    pltpu.make_async_copy(ref, ref, sem).wait()


CHUNKS = ((0, 2), (1, 2), (1, 1), (0, 3), (0, 1), (1, 3), (1, 0), (0, 0))


def project_kernel(
    tokens, cot, in_weight, o_weight, token_out, cot_out, proj_out, d_attn_out,
    blocks, proj_send, proj_recv, cot_send, cot_recv,
    a2a_s, a2a_r, up_s, up_r, down_s, down_r, far_s, far_r, core_s, core_r, sum_s, sum_r, keep,
):
    place = here()
    h, x, z, low, core = place
    seat = z * 2 + core
    height = blocks.shape[2] // 8
    width = blocks.shape[3]
    right, left = near(place, dx=1), near(place, dx=-1)
    above, below = near(place, dz=1), near(place, dz=-1)
    twin, across = near(place, dc=1), near(place, dh=1)
    shifts = [shift for shift in CHUNKS if shift != (0, 0)]
    greet([near(place, dh=dh, dx=dx) for dh, dx in shifts] + [above, below, twin])
    sent = []

    def rows(a, dh, dx, at):
        return blocks.at[a, dh * 4 + dx, pl.ds(pl.multiple_of(at * height, height), height)]

    def level(dz):
        return (z + dz + 4) % 4 * 2 + core

    def index(dh, dx):
        return dh * 4 + dx

    def start_blocks(a, source):
        for dh, dx in CHUNKS:
            target = near(place, dh=dh, dx=dx)
            piece = source.at[
                pl.ds(pl.multiple_of(seat * height, height), height),
                pl.ds(pl.multiple_of(target[0] * width, width), width),
            ]
            j = index(dh, dx)
            if j:
                sent.append(send(piece, rows(a, dh, dx, seat), (a2a_s.at[a, j], a2a_r.at[a, j]), target))
            else:
                pltpu.make_async_copy(piece, rows(a, 0, 0, seat), a2a_r.at[a, 0]).start()

    def to_twin(a, dh, dx, which, at):
        j = index(dh, dx)
        piece = rows(a, dh, dx, at)
        sent.append(send(piece, piece, (core_s.at[a, j, which], core_r.at[a, j, which]), twin))

    def first_stage(a, dh, dx):
        j = index(dh, dx)
        piece = rows(a, dh, dx, seat)
        arrived(piece, a2a_r.at[a, j])
        sent.append(send(piece, piece, (up_s.at[a, j], up_r.at[a, j]), above))
        sent.append(send(piece, piece, (down_s.at[a, j], down_r.at[a, j]), below))
        to_twin(a, dh, dx, 0, seat)

    def second_stage(a, dh, dx):
        j = index(dh, dx)
        sems = (far_s.at[a, j], far_r.at[a, j])
        lower, upper = rows(a, dh, dx, level(-1)), rows(a, dh, dx, level(1))
        arrived(lower, up_r.at[a, j])
        if dh == 0:
            sent.append(send(lower, lower, sems, above))
        to_twin(a, dh, dx, 1, level(-1))
        arrived(upper, down_r.at[a, j])
        if dh == 1:
            sent.append(send(upper, upper, sems, below))
        to_twin(a, dh, dx, 2, level(1))

    def third_stage(a, dh, dx):
        j = index(dh, dx)
        arrived(rows(a, dh, dx, level(2)), far_r.at[a, j])
        to_twin(a, dh, dx, 3, level(2))

    def complete(a, dh, dx):
        j = index(dh, dx)
        for which, dz in enumerate((0, -1, 1, 2)):
            seat_there = (z + dz + 4) % 4 * 2 + (1 - core)
            arrived(rows(a, dh, dx, seat_there), core_r.at[a, j, which])

    weights = (in_weight, o_weight)
    outgoing = (proj_send, cot_send)
    incoming = (proj_recv, cot_recv)
    results = (proj_out, d_attn_out)
    adds = {4: (0,), 5: (1,), 6: (2, 5), 7: (3, 4, 6)}
    ways = (left, right, left, right, left, right, across)

    def chunk(a, k):
        dh, dx = CHUNKS[k]
        j = index(dh, dx)
        third_stage(a, dh, dx)
        complete(a, dh, dx)
        terms = adds.get(k, ())
        for term in terms:
            arrived(incoming[a].at[term], sum_r.at[a, term])
        target = outgoing[a].at[k] if k < 7 else results[a]
        tile = blocks.shape[2] // 2

        @pl.loop(0, 2)
        def _(step):
            part = pl.ds(pl.multiple_of(step * tile, tile), tile)
            total = jnp.dot(blocks[a, j, part, :], weights[a][...], preferred_element_type=F32)
            for term in terms:
                total = total + incoming[a][term, part, :].astype(F32)
            target[part, :] = total.astype(target.dtype)

        if k < 7:
            sent.append(send(target, incoming[a].at[k], (sum_s.at[a, k], sum_r.at[a, k]), ways[k]))

    start_blocks(0, tokens)
    start_blocks(1, cot)
    for shift in CHUNKS:
        first_stage(0, *shift)
    for shift in CHUNKS:
        second_stage(0, *shift)
    for shift in CHUNKS:
        first_stage(1, *shift)
    for k in range(6):
        chunk(0, k)
        second_stage(1, *CHUNKS[k])
    for k in (6, 7):
        second_stage(1, *CHUNKS[k])
    for k in range(4):
        chunk(1, k)
    chunk(0, 6)
    for k in (4, 5):
        chunk(1, k)
    chunk(0, 7)
    chunk(1, 6)
    chunk(1, 7)
    keeps = [
        pltpu.make_async_copy(blocks.at[0], token_out, keep.at[0]),
        pltpu.make_async_copy(blocks.at[1], cot_out, keep.at[1]),
    ]
    for copy in keeps:
        copy.start()
    for copy in sent:
        copy.wait_send()
    for copy in keeps:
        copy.wait()


def project(tokens, cot, in_weight, o_weight):
    length = tokens.shape[0]
    width = tokens.shape[1] // 8
    in_width, o_width = in_weight.shape[1], o_weight.shape[1]
    dma = pltpu.SemaphoreType.DMA
    pair = [dma((2, 8)), dma((2, 8))]
    block = jax.ShapeDtypeStruct((8, length, width), BF16)
    return pl.pallas_call(
        project_kernel,
        out_shape=(
            block,
            block,
            jax.ShapeDtypeStruct((length, in_width), F32),
            jax.ShapeDtypeStruct((length, o_width), BF16),
        ),
        in_specs=[pl.BlockSpec(memory_space=pl.ANY)] * 2
        + [pl.BlockSpec(memory_space=pltpu.VMEM)] * 2,
        out_specs=(pl.BlockSpec(memory_space=pl.ANY),) * 2
        + (pl.BlockSpec(memory_space=pltpu.VMEM),) * 2,
        scratch_shapes=[
            pltpu.VMEM((2, 8, length, width), BF16),
            pltpu.VMEM((7, length, in_width), BF16),
            pltpu.VMEM((7, length, in_width), BF16),
            pltpu.VMEM((7, length, o_width), BF16),
            pltpu.VMEM((7, length, o_width), BF16),
            *pair,
            *pair,
            *pair,
            *pair,
            dma((2, 8, 4)),
            dma((2, 8, 4)),
            dma((2, 7)),
            dma((2, 7)),
            dma((2,)),
        ],
        compiler_params=pltpu.CompilerParams(
            collective_id=0, has_side_effects=True, vmem_limit_bytes=56 * MIB
        ),
        name="project",
    )(tokens, cot, in_weight, o_weight)


def nt(left, right):
    return lax.dot_general(left, right, (((1,), (1,)), ((), ())), preferred_element_type=F32)


def tn(left, right):
    return lax.dot_general(left, right, (((0,), (0,)), ((), ())), preferred_element_type=F32)


def swap_halves(array):
    return pltpu.roll(array, array.shape[1] // 2, 1)


LEVELS = (2, -1, 1, 0)


def finish_kernel(
    proj, d_attn, cosine, sine, seg_col, seg_row, in_weight, o_weight, token_blocks, cot_blocks,
    mixed, d_tokens, q_grad, kv_grad, o_grad,
    attn_all, grad_all, q_rot, probs, bias, keys, values, kv_send, kv_recv, key_sum, value_sum,
    kv_grad_send, kv_grad_recv,
    half_send, half_recv, level_send, level_recv, side_send, side_recv, last_send, last_recv,
    column, grad_sum,
    kv_sems, ring_s, ring_r, half_s, half_r, level_s, level_r, side_sems, hand_s, hand_r,
    mixed_s, mixed_r, twin_s, twin_r, column_sem, out_sem,
):
    place = here()
    h, x, z, low, core = place
    blk, tp = h * 4 + x, z * 4 + low * 2 + core
    length, q_width = d_attn.shape
    tile = length // 2
    score_scale = 1.0 / math.sqrt(HEAD_SIZE)
    right, left = near(place, dx=1), near(place, dx=-1)
    above, below = near(place, dz=1), near(place, dz=-1)
    twin, across, beside = near(place, dc=1), near(place, dh=1), near(place, dl=1)
    halves = []
    group = z * 2 + low
    home = (group, blk * 2 + core)
    away = group != blk
    sent = []

    barrier = pltpu.get_barrier_semaphore()
    for device in (right, left, above, below, twin, across, beside):
        pl.semaphore_signal(barrier, inc=1, device_id=device, device_id_type=MESH)

    @pl.when(away)
    def _():
        pl.semaphore_signal(barrier, inc=1, device_id=home, device_id_type=MESH)

    pl.semaphore_wait(barrier, 7 + jnp.where(away, 1, 0))

    def post(source, target, sems, device):
        sent.append(send(source, target, sems, device))

    lane = lax.broadcasted_iota(jnp.int32, (length, HEAD_SIZE), 1)
    in_front = lane < HEAD_SIZE // 2
    is_lower = jnp.full((length, HEAD_SIZE), core) == 0
    kv_send[...] = proj[:, q_width:].astype(BF16)
    post(kv_send, kv_recv, (kv_sems.at[0], kv_sems.at[1]), twin)

    @pl.loop(0, 2)
    def _(step):
        start = pl.multiple_of(step * tile, tile)
        part = pl.ds(start, tile)
        row = lax.broadcasted_iota(jnp.int32, (tile, length), 0) + start
        key = lax.broadcasted_iota(jnp.int32, (tile, length), 1)
        allowed = (key <= row) & (seg_col[part, :] == seg_row[...])
        bias[part, :] = jnp.where(allowed, 0.0, -jnp.inf)

    @pl.loop(0, q_width // HEAD_SIZE)
    def _(head):
        cols = pl.ds(pl.multiple_of(head * HEAD_SIZE, HEAD_SIZE), HEAD_SIZE)
        query = proj[:, cols]
        q_rot[:, cols] = (query * cosine[...] + swap_halves(query) * sine[...]).astype(BF16)

    arrived(kv_recv, kv_sems.at[1])
    own, other = kv_send[...].astype(F32), kv_recv[...].astype(F32)
    lower, upper = jnp.where(is_lower, own, other), jnp.where(is_lower, other, own)
    key = jnp.where(in_front, lower, swap_halves(upper))
    keys[...] = (key * cosine[...] + swap_halves(key) * sine[...]).astype(BF16)
    values[...] = jnp.where(in_front, swap_halves(lower), upper).astype(BF16)

    @pl.loop(0, q_width // HEAD_SIZE)
    def _(head):
        cols = pl.ds(pl.multiple_of(head * HEAD_SIZE, HEAD_SIZE), HEAD_SIZE)

        @pl.loop(0, 2)
        def _(step):
            part = pl.ds(pl.multiple_of(step * tile, tile), tile)
            scores = nt(q_rot[part, cols], keys[...]) * score_scale + bias[part, :]
            raised = jnp.exp(scores - jnp.max(scores, axis=1, keepdims=True))
            prob = raised / jnp.sum(raised, axis=1, keepdims=True)
            probs[head, part, :] = prob
            mixed_values = jnp.dot(prob.astype(BF16), values[...], preferred_element_type=F32)
            attn_all[0, part, cols] = mixed_values.astype(BF16)

    rings = (attn_all, grad_all)

    def hop(i, k, source, target, device):
        ring = rings[i]
        post(ring.at[source], ring.at[target], (ring_s.at[i, k], ring_r.at[i, k]), device)

    def ring_wait(i, k, target):
        arrived(rings[i].at[target], ring_r.at[i, k])

    def ring_start(i):
        hop(i, 0, 0, 4, across)
        hop(i, 1, 0, 1, right)
        hop(i, 2, 0, 3, left)

    def ring_side(i):
        ring_wait(i, 0, 4)
        hop(i, 3, 4, 5, right)
        hop(i, 4, 4, 7, left)

    def ring_forward(i):
        ring_wait(i, 1, 1)
        hop(i, 5, 1, 2, right)
        ring_wait(i, 4, 7)
        hop(i, 6, 7, 6, left)

    def ring_end(i):
        for k, target in ((2, 3), (3, 5), (5, 2), (6, 6)):
            ring_wait(i, k, target)

    ring_start(0)

    key_sum[...] = jnp.zeros_like(key_sum)
    value_sum[...] = jnp.zeros_like(value_sum)

    @pl.loop(0, q_width // HEAD_SIZE)
    def _(head):
        cols = pl.ds(pl.multiple_of(head * HEAD_SIZE, HEAD_SIZE), HEAD_SIZE)

        @pl.loop(0, 2)
        def _(step):
            part = pl.ds(pl.multiple_of(step * tile, tile), tile)
            d_out = d_attn[part, cols]
            prob = probs[head, part, :]
            d_prob = nt(d_out, values[...])
            row_delta = jnp.sum(prob * d_prob, axis=1, keepdims=True)
            d_score = (prob * (d_prob - row_delta) * score_scale).astype(BF16)
            d_query = jnp.dot(d_score, keys[...], preferred_element_type=F32)
            d_query = d_query * cosine[part, :] - swap_halves(d_query) * sine[part, :]
            grad_all[0, part, cols] = d_query.astype(BF16)
            key_sum[...] += tn(d_score, q_rot[part, cols])
            value_sum[...] += tn(prob.astype(BF16), d_out)

    d_key = key_sum[...] * cosine[...] - swap_halves(key_sum[...]) * sine[...]
    d_key, d_value = d_key.astype(BF16).astype(F32), value_sum[...].astype(BF16).astype(F32)
    lower = jnp.where(in_front, d_key, swap_halves(d_value))
    upper = jnp.where(in_front, swap_halves(d_key), d_value)
    kv_grad_send[...] = jnp.where(is_lower, upper, lower).astype(BF16)
    post(kv_grad_send, kv_grad_recv, (kv_sems.at[2], kv_sems.at[3]), twin)
    own = jnp.where(is_lower, lower, upper)
    arrived(kv_grad_recv, kv_sems.at[3])
    grad_all[0, :, q_width:] = (own + kv_grad_recv[...].astype(F32)).astype(BF16)

    weights = (o_weight, in_weight)
    half = o_weight.shape[0] // 2

    def spot(dz, side):
        there = (z + dz + 4) % 4 * 2 + side
        return (h + there // 4) % 2 * 4 + (x - there % 4 + 4) % 4

    def term(i, dz, side, which, part):
        rows = pl.ds(pl.multiple_of(which * half, half), half)
        return nt(rings[i][spot(dz, side), part, :], weights[i][rows, :])

    def give_half(i):
        for q, dz in enumerate(LEVELS):
            if i:
                halves[q].wait_send()
            for side in range(2):

                @pl.loop(0, 2)
                def _(step):
                    part = pl.ds(pl.multiple_of(step * tile, tile), tile)
                    half_send[q, side, part, :] = term(i, dz, side, 1 - core, part).astype(BF16)

            sems = (half_s.at[i, q], half_r.at[i, q])
            halves.append(send(half_send.at[q], half_recv.at[i, q], sems, twin))

    def half_wait(i, q):
        arrived(half_recv.at[i, q], half_r.at[i, q])

    def add_up(i, q, side, target, terms):
        @pl.loop(0, 2)
        def _(step):
            part = pl.ds(pl.multiple_of(step * tile, tile), tile)
            total = term(i, LEVELS[q], side, core, part)
            total = total + half_recv[i, q, side, part, :].astype(F32)
            for ref in terms:
                total = total + ref[part, :].astype(F32)
            target[part, :] = total.astype(target.dtype)

    def level_hop(i, k, slot, device):
        sems = (level_s.at[i, k], level_r.at[i, slot])
        post(level_send.at[i, k], level_recv.at[i, slot], sems, device)

    def level_wait(i, slot):
        arrived(level_recv.at[i, slot], level_r.at[i, slot])

    def far_level(i):
        half_wait(i, 0)
        add_up(i, 0, 0, level_send.at[i, 0], ())
        level_hop(i, 0, 0, below)
        add_up(i, 0, 1, level_send.at[i, 1], ())
        level_hop(i, 1, 1, above)

    def near_level(i):
        half_wait(i, 1)
        add_up(i, 1, 1, level_send.at[i, 2], ())
        level_hop(i, 2, 3, below)
        half_wait(i, 2)
        add_up(i, 2, 0, level_send.at[i, 3], ())
        level_hop(i, 3, 4, above)

    def pass_level(i):
        level_wait(i, 0)
        add_up(i, 1, 0, level_send.at[i, 4], (level_recv.at[i, 0],))
        level_hop(i, 4, 2, below)
        level_wait(i, 1)
        add_up(i, 2, 1, level_send.at[i, 5], (level_recv.at[i, 1],))
        level_hop(i, 5, 5, above)

    def own_level(i):
        half_wait(i, 3)
        for slot in range(2, 6):
            level_wait(i, slot)
        terms = (level_recv.at[i, 2 + 1 - low], level_recv.at[i, 4 + 1 - low])
        add_up(i, 3, 1 - low, side_send.at[i], terms)
        post(side_send.at[i], side_recv.at[i], (side_sems.at[i, 0], side_sems.at[i, 1]), beside)

    tp_width = half

    def columns(t):
        return mixed.at[:, pl.ds(pl.multiple_of(t * tp_width, tp_width), tp_width)]

    def last_target(i):
        return columns(tp) if i == 0 else last_recv

    def last_level(i):
        arrived(side_recv.at[i], side_sems.at[i, 1])
        terms = (level_recv.at[i, 2 + low], level_recv.at[i, 4 + low], side_recv.at[i])
        add_up(i, 3, low, last_send.at[i], terms)
        there = columns(home[1]) if i == 0 else last_recv

        @pl.when(away)
        def _():
            send(last_send.at[i], there, (hand_s.at[i], hand_r.at[i]), home)

        @pl.when(group == blk)
        def _():
            pltpu.make_async_copy(last_send.at[i], last_target(i), hand_r.at[i]).start()

    def hand_end(i):
        arrived(last_target(i), hand_r.at[i])

    def hand_sent(i):
        @pl.when(away)
        def _():
            arrived(last_send.at[i], hand_s.at[i])

    def tp_at(dz, dl, dc=0):
        return (z + dz + 4) % 4 * 4 + (low + dl) % 2 * 2 + (core + dc) % 2

    def mixed_hop(k, t, device):
        post(columns(t), columns(t), (mixed_s.at[k], mixed_r.at[k]), device)

    def mixed_wait(k, t):
        arrived(columns(t), mixed_r.at[k])

    def mixed_twin(k, t):
        post(columns(t), columns(t), (twin_s.at[k], twin_r.at[k]), twin)

    def mixed_start():
        hand_end(0)
        mixed_hop(0, tp, beside)
        mixed_hop(1, tp, above)
        mixed_hop(2, tp, below)
        mixed_twin(0, tp)

    def mixed_side():
        mixed_wait(0, tp_at(0, 1))
        mixed_hop(3, tp_at(0, 1), above)
        mixed_hop(4, tp_at(0, 1), below)
        mixed_twin(1, tp_at(0, 1))

    def mixed_forward():
        mixed_wait(1, tp_at(-1, 0))
        mixed_hop(5, tp_at(-1, 0), above)
        mixed_twin(2, tp_at(-1, 0))
        mixed_wait(2, tp_at(1, 0))
        mixed_twin(3, tp_at(1, 0))
        mixed_wait(4, tp_at(1, 1))
        mixed_hop(6, tp_at(1, 1), below)
        mixed_twin(4, tp_at(1, 1))

    def mixed_end():
        mixed_wait(3, tp_at(-1, 1))
        mixed_twin(5, tp_at(-1, 1))
        mixed_wait(5, tp_at(2, 0))
        mixed_twin(6, tp_at(2, 0))
        mixed_wait(6, tp_at(2, 1))
        mixed_twin(7, tp_at(2, 1))
        sources = ((0, 0), (0, 1), (-1, 0), (1, 0), (1, 1), (-1, 1), (2, 0), (2, 1))
        for k, (dz, dl) in enumerate(sources):
            arrived(columns(tp_at(dz, dl, 1)), twin_r.at[k])

    sources = (cot_blocks, token_blocks)
    order = (0, 4, 1, 3, 5, 7, 2, 6)
    steps = [(i, j) for i in range(2) for j in order]

    def load(n):
        i, j = steps[n]
        pltpu.make_async_copy(sources[i].at[j], column.at[n % 2], column_sem.at[n % 2]).start()

    def grad_step(n):
        i, j = steps[n]
        slot = n % 2
        arrived(column.at[slot], column_sem.at[slot])
        width = rings[i].shape[2]
        strip = 256

        @pl.loop(0, column.shape[2] // strip)
        def _(step):
            part = pl.ds(pl.multiple_of(step * strip, strip), strip)
            value = tn(column[slot, :, part], rings[i][j])
            if n % 8:
                value = value + grad_sum[part, :width]
            if n % 8 < 7:
                grad_sum[part, :width] = value
            elif i == 0:
                o_grad[part, :] = value.astype(BF16)
            else:
                q_grad[part, :] = value[:, :q_width].astype(BF16)
                kv_grad[part, :] = value[:, q_width:].astype(BF16)

        if n + 2 < len(steps):
            load(n + 2)

    load(0)
    load(1)
    ring_side(0)
    ring_start(1)
    grad_step(0)
    ring_forward(0)
    ring_side(1)
    grad_step(1)
    ring_end(0)
    give_half(0)
    ring_forward(1)
    far_level(0)
    near_level(0)
    for n in range(2, 5):
        grad_step(n)
    pass_level(0)
    for n in range(5, 8):
        grad_step(n)
    ring_end(1)
    give_half(1)
    far_level(1)
    near_level(1)
    own_level(0)
    grad_step(8)
    grad_step(9)
    last_level(0)
    pass_level(1)
    grad_step(10)
    grad_step(11)
    mixed_start()
    grad_step(12)
    grad_step(13)
    mixed_side()
    own_level(1)
    grad_step(14)
    grad_step(15)
    mixed_forward()
    last_level(1)
    mixed_end()
    hand_end(1)
    out = pltpu.make_async_copy(last_recv, d_tokens, out_sem)
    out.start()
    for copy in sent + halves[4:]:
        copy.wait_send()
    hand_sent(0)
    hand_sent(1)
    out.wait()


def finish(proj, d_attn, cosine, sine, segments, in_weight, o_weight, token_blocks, cot_blocks):
    length, q_width = d_attn.shape
    in_width = in_weight.shape[1]
    depth = in_weight.shape[0]
    half = depth // 2
    heads = q_width // HEAD_SIZE
    dma = pltpu.SemaphoreType.DMA
    vmem = pl.BlockSpec(memory_space=pltpu.VMEM)
    hbm = pl.BlockSpec(memory_space=pl.ANY)
    part = pltpu.VMEM((length, HEAD_SIZE), BF16)
    part_sum = pltpu.VMEM((length, HEAD_SIZE), F32)
    return pl.pallas_call(
        finish_kernel,
        out_shape=(
            jax.ShapeDtypeStruct((length, 16 * half), BF16),
            jax.ShapeDtypeStruct((length, half), BF16),
            jax.ShapeDtypeStruct((depth, q_width), BF16),
            jax.ShapeDtypeStruct((depth, in_width - q_width), BF16),
            jax.ShapeDtypeStruct((depth, q_width), BF16),
        ),
        in_specs=[vmem] * 8 + [hbm] * 2,
        out_specs=(hbm, hbm, vmem, vmem, vmem),
        scratch_shapes=[
            pltpu.VMEM((8, length, q_width), BF16),
            pltpu.VMEM((8, length, in_width), BF16),
            pltpu.VMEM((length, q_width), BF16),
            pltpu.VMEM((heads, length, length), F32),
            pltpu.VMEM((length, length), F32),
            part,
            part,
            part,
            part,
            part_sum,
            part_sum,
            part,
            part,
            pltpu.VMEM((4, 2, length, half), BF16),
            pltpu.VMEM((2, 4, 2, length, half), BF16),
            pltpu.VMEM((2, 6, length, half), BF16),
            pltpu.VMEM((2, 6, length, half), BF16),
            pltpu.VMEM((2, length, half), BF16),
            pltpu.VMEM((2, length, half), BF16),
            pltpu.VMEM((2, length, half), BF16),
            pltpu.VMEM((length, half), BF16),
            pltpu.VMEM((2, length, depth), BF16),
            pltpu.VMEM((depth, in_width), F32),
            dma((4,)),
            dma((2, 7)),
            dma((2, 7)),
            dma((2, 4)),
            dma((2, 4)),
            dma((2, 6)),
            dma((2, 6)),
            dma((2, 2)),
            dma((2,)),
            dma((2,)),
            dma((7,)),
            dma((7,)),
            dma((8,)),
            dma((8,)),
            dma((2,)),
            dma,
        ],
        compiler_params=pltpu.CompilerParams(
            collective_id=1, has_side_effects=True, vmem_limit_bytes=63 * MIB
        ),
        name="finish",
    )(
        proj, d_attn, cosine, sine, segments.reshape(length, 1), segments.reshape(1, length),
        in_weight, o_weight, token_blocks, cot_blocks,
    )


def shards(tokens, segment_ids, q_weight, key_value_weight, o_weight, cotangent):
    in_weight = jnp.concatenate([q_weight, key_value_weight], axis=1)
    token_blocks, cot_blocks, proj, d_attn = project(tokens, cotangent, in_weight, o_weight)
    cosine, sine = rope_tables(tokens.shape[0], HEAD_SIZE)
    cosine = jnp.concatenate([cosine, cosine], axis=1)
    sine = jnp.concatenate([-sine, sine], axis=1)
    return finish(
        proj, d_attn, cosine, sine, segment_ids[0], in_weight, o_weight, token_blocks, cot_blocks
    )


def solution(mesh):
    in_specs = (
        P("blk", None),
        P("blk", None),
        P("blk", "tp"),
        P("blk", "tp"),
        P("blk", "tp"),
        P("blk", None),
    )
    out_specs = (P("blk", None), P("blk", "tp"), P("blk", "tp"), P("blk", "tp"), P("blk", "tp"))
    return jax.shard_map(shards, mesh=mesh, in_specs=in_specs, out_specs=out_specs, check_vma=False)
```

```python
import math

import jax
import jax.numpy as jnp
from jax import lax
from jax.experimental import pallas as pl
from jax.experimental.pallas import tpu as pltpu
from jax.sharding import PartitionSpec as P

HEAD_SIZE = 128


THETA = 10000.0


def rope_tables(length, width):
    half_width = width // 2
    position = jnp.arange(length, dtype=jnp.float32)[:, None]
    channel = jnp.arange(half_width, dtype=jnp.float32)[None, :]
    angle = position * jnp.power(THETA, -2.0 * channel / width)
    return (jnp.cos(angle), jnp.sin(angle))


MESH = pl.DeviceIdType.MESH
BF16 = jnp.bfloat16
F32 = jnp.float32
MIB = 1 << 20


def here():
    blk, tp = lax.axis_index("blk"), lax.axis_index("tp")
    return blk // 4, blk % 4, tp // 4, tp // 2 % 2, tp % 2


def near(place, dh=0, dx=0, dz=0, dl=0, dc=0):
    h, x, z, low, core = place
    h, low, core = (h + dh) % 2, (low + dl) % 2, (core + dc) % 2
    x, z = (x + dx + 4) % 4, (z + dz + 4) % 4
    return h * 4 + x, z * 4 + low * 2 + core


def greet(devices):
    barrier = pltpu.get_barrier_semaphore()
    for device in devices:
        pl.semaphore_signal(barrier, inc=1, device_id=device, device_id_type=MESH)
    pl.semaphore_wait(barrier, len(devices))


def send(source, target, sems, device):
    copy = pltpu.make_async_remote_copy(
        src_ref=source,
        dst_ref=target,
        send_sem=sems[0],
        recv_sem=sems[1],
        device_id=device,
        device_id_type=MESH,
    )
    copy.start()
    return copy


def arrived(ref, sem):
    pltpu.make_async_copy(ref, ref, sem).wait()


CHUNKS = ((0, 2), (1, 2), (1, 1), (0, 3), (0, 1), (1, 3), (1, 0), (0, 0))


def project_kernel(
    tokens, cot, in_weight, o_weight, token_out, cot_out, proj_out, d_attn_out,
    blocks, proj_send, proj_recv, cot_send, cot_recv,
    a2a_s, a2a_r, up_s, up_r, down_s, down_r, far_s, far_r, core_s, core_r, sum_s, sum_r, keep,
):
    place = here()
    h, x, z, low, core = place
    seat = z * 2 + core
    height = blocks.shape[2] // 8
    width = blocks.shape[3]
    right, left = near(place, dx=1), near(place, dx=-1)
    above, below = near(place, dz=1), near(place, dz=-1)
    twin, across = near(place, dc=1), near(place, dh=1)
    shifts = [shift for shift in CHUNKS if shift != (0, 0)]
    greet([near(place, dh=dh, dx=dx) for dh, dx in shifts] + [above, below, twin])
    sent = []

    def rows(a, dh, dx, at):
        return blocks.at[a, dh * 4 + dx, pl.ds(pl.multiple_of(at * height, height), height)]

    def level(dz):
        return (z + dz + 4) % 4 * 2 + core

    def index(dh, dx):
        return dh * 4 + dx

    def start_blocks(a, source):
        for dh, dx in CHUNKS:
            target = near(place, dh=dh, dx=dx)
            piece = source.at[
                pl.ds(pl.multiple_of(seat * height, height), height),
                pl.ds(pl.multiple_of(target[0] * width, width), width),
            ]
            j = index(dh, dx)
            if j:
                sent.append(send(piece, rows(a, dh, dx, seat), (a2a_s.at[a, j], a2a_r.at[a, j]), target))
            else:
                pltpu.make_async_copy(piece, rows(a, 0, 0, seat), a2a_r.at[a, 0]).start()

    def to_twin(a, dh, dx, which, at):
        j = index(dh, dx)
        piece = rows(a, dh, dx, at)
        sent.append(send(piece, piece, (core_s.at[a, j, which], core_r.at[a, j, which]), twin))

    def first_stage(a, dh, dx):
        j = index(dh, dx)
        piece = rows(a, dh, dx, seat)
        arrived(piece, a2a_r.at[a, j])
        sent.append(send(piece, piece, (up_s.at[a, j], up_r.at[a, j]), above))
        sent.append(send(piece, piece, (down_s.at[a, j], down_r.at[a, j]), below))
        to_twin(a, dh, dx, 0, seat)

    def second_stage(a, dh, dx):
        j = index(dh, dx)
        sems = (far_s.at[a, j], far_r.at[a, j])
        lower, upper = rows(a, dh, dx, level(-1)), rows(a, dh, dx, level(1))
        arrived(lower, up_r.at[a, j])
        if dh == 0:
            sent.append(send(lower, lower, sems, above))
        to_twin(a, dh, dx, 1, level(-1))
        arrived(upper, down_r.at[a, j])
        if dh == 1:
            sent.append(send(upper, upper, sems, below))
        to_twin(a, dh, dx, 2, level(1))

    def third_stage(a, dh, dx):
        j = index(dh, dx)
        arrived(rows(a, dh, dx, level(2)), far_r.at[a, j])
        to_twin(a, dh, dx, 3, level(2))

    def complete(a, dh, dx):
        j = index(dh, dx)
        for which, dz in enumerate((0, -1, 1, 2)):
            seat_there = (z + dz + 4) % 4 * 2 + (1 - core)
            arrived(rows(a, dh, dx, seat_there), core_r.at[a, j, which])

    weights = (in_weight, o_weight)
    outgoing = (proj_send, cot_send)
    incoming = (proj_recv, cot_recv)
    results = (proj_out, d_attn_out)
    adds = {4: (0,), 5: (1,), 6: (2, 5), 7: (3, 4, 6)}
    ways = (left, right, left, right, left, right, across)

    def chunk(a, k):
        dh, dx = CHUNKS[k]
        j = index(dh, dx)
        complete(a, dh, dx)
        terms = adds.get(k, ())
        for term in terms:
            arrived(incoming[a].at[term], sum_r.at[a, term])
        target = outgoing[a].at[k] if k < 7 else results[a]
        tile = blocks.shape[2] // 2

        @pl.loop(0, 2)
        def _(step):
            part = pl.ds(pl.multiple_of(step * tile, tile), tile)
            total = jnp.dot(blocks[a, j, part, :], weights[a][...], preferred_element_type=F32)
            for term in terms:
                total = total + incoming[a][term, part, :].astype(F32)
            target[part, :] = total.astype(target.dtype)

        if k < 7:
            sent.append(send(target, incoming[a].at[k], (sum_s.at[a, k], sum_r.at[a, k]), ways[k]))

    start_blocks(0, tokens)
    start_blocks(1, cot)
    pieces = [(a, k) for a in range(2) for k in range(8)]
    waiting = [(0, 0), (0, 1), (0, 2), (0, 3), (0, 4), (0, 5), (0, 6), (1, 0), (1, 1), (1, 2), (1, 3)]
    waiting += [(0, 7), (1, 4), (1, 5), (1, 6), (1, 7)]
    late = {(0, 6): 7, (0, 7): 9}
    for step in range(len(pieces) + 5):
        for stage, lag in ((first_stage, 0), (second_stage, 2), (third_stage, 4)):
            if 0 <= step - lag < len(pieces):
                a, k = pieces[step - lag]
                stage(a, *CHUNKS[k])
        while waiting and pieces.index(waiting[0]) + late.get(waiting[0], 5) <= step:
            chunk(*waiting.pop(0))
    assert not waiting
    keeps = [
        pltpu.make_async_copy(blocks.at[0], token_out, keep.at[0]),
        pltpu.make_async_copy(blocks.at[1], cot_out, keep.at[1]),
    ]
    for copy in keeps:
        copy.start()
    for copy in sent:
        copy.wait_send()
    for copy in keeps:
        copy.wait()


def project(tokens, cot, in_weight, o_weight):
    length = tokens.shape[0]
    width = tokens.shape[1] // 8
    in_width, o_width = in_weight.shape[1], o_weight.shape[1]
    dma = pltpu.SemaphoreType.DMA
    pair = [dma((2, 8)), dma((2, 8))]
    block = jax.ShapeDtypeStruct((8, length, width), BF16)
    return pl.pallas_call(
        project_kernel,
        out_shape=(
            block,
            block,
            jax.ShapeDtypeStruct((length, in_width), F32),
            jax.ShapeDtypeStruct((length, o_width), BF16),
        ),
        in_specs=[pl.BlockSpec(memory_space=pl.ANY)] * 2
        + [pl.BlockSpec(memory_space=pltpu.VMEM)] * 2,
        out_specs=(pl.BlockSpec(memory_space=pl.ANY),) * 2
        + (pl.BlockSpec(memory_space=pltpu.VMEM),) * 2,
        scratch_shapes=[
            pltpu.VMEM((2, 8, length, width), BF16),
            pltpu.VMEM((7, length, in_width), BF16),
            pltpu.VMEM((7, length, in_width), BF16),
            pltpu.VMEM((7, length, o_width), BF16),
            pltpu.VMEM((7, length, o_width), BF16),
            *pair,
            *pair,
            *pair,
            *pair,
            dma((2, 8, 4)),
            dma((2, 8, 4)),
            dma((2, 7)),
            dma((2, 7)),
            dma((2,)),
        ],
        compiler_params=pltpu.CompilerParams(
            collective_id=0, has_side_effects=True, vmem_limit_bytes=56 * MIB
        ),
        name="project",
    )(tokens, cot, in_weight, o_weight)


def nt(left, right):
    return lax.dot_general(left, right, (((1,), (1,)), ((), ())), preferred_element_type=F32)


def tn(left, right):
    return lax.dot_general(left, right, (((0,), (0,)), ((), ())), preferred_element_type=F32)


def swap_halves(array):
    return pltpu.roll(array, array.shape[1] // 2, 1)


LEVELS = (2, -1, 1, 0)


def finish_kernel(
    proj, d_attn, cosine, sine, seg_col, seg_row, in_weight, o_weight, token_blocks, cot_blocks,
    mixed, d_tokens, q_grad, kv_grad, o_grad,
    attn_all, grad_all, q_rot, probs, bias, keys, values, kv_send, kv_recv, key_sum, value_sum,
    kv_grad_send, kv_grad_recv,
    half_send, half_recv, level_send, level_recv, side_send, side_recv, last_send, last_recv,
    column, grad_sum,
    kv_sems, ring_s, ring_r, half_s, half_r, level_s, level_r, side_sems, hand_s, hand_r,
    mixed_s, mixed_r, twin_s, twin_r, column_sem, out_sem,
):
    place = here()
    h, x, z, low, core = place
    blk, tp = h * 4 + x, z * 4 + low * 2 + core
    length, q_width = d_attn.shape
    tile = length // 2
    score_scale = 1.0 / math.sqrt(HEAD_SIZE)
    right, left = near(place, dx=1), near(place, dx=-1)
    above, below = near(place, dz=1), near(place, dz=-1)
    twin, across, beside = near(place, dc=1), near(place, dh=1), near(place, dl=1)
    halves = []
    group = z * 2 + low
    home = (group, blk * 2 + core)
    away = group != blk
    sent = []

    barrier = pltpu.get_barrier_semaphore()
    for device in (right, left, above, below, twin, across, beside):
        pl.semaphore_signal(barrier, inc=1, device_id=device, device_id_type=MESH)

    @pl.when(away)
    def _():
        pl.semaphore_signal(barrier, inc=1, device_id=home, device_id_type=MESH)

    pl.semaphore_wait(barrier, 7 + jnp.where(away, 1, 0))

    def post(source, target, sems, device):
        sent.append(send(source, target, sems, device))

    lane = lax.broadcasted_iota(jnp.int32, (length, HEAD_SIZE), 1)
    in_front = lane < HEAD_SIZE // 2
    is_lower = jnp.full((length, HEAD_SIZE), core) == 0
    kv_send[...] = proj[:, q_width:].astype(BF16)
    post(kv_send, kv_recv, (kv_sems.at[0], kv_sems.at[1]), twin)

    @pl.loop(0, 2)
    def _(step):
        start = pl.multiple_of(step * tile, tile)
        part = pl.ds(start, tile)
        row = lax.broadcasted_iota(jnp.int32, (tile, length), 0) + start
        key = lax.broadcasted_iota(jnp.int32, (tile, length), 1)
        allowed = (key <= row) & (seg_col[part, :] == seg_row[...])
        bias[part, :] = jnp.where(allowed, 0.0, -jnp.inf)

    @pl.loop(0, q_width // HEAD_SIZE)
    def _(head):
        cols = pl.ds(pl.multiple_of(head * HEAD_SIZE, HEAD_SIZE), HEAD_SIZE)
        query = proj[:, cols]
        q_rot[:, cols] = (query * cosine[...] + swap_halves(query) * sine[...]).astype(BF16)

    arrived(kv_recv, kv_sems.at[1])
    own, other = kv_send[...].astype(F32), kv_recv[...].astype(F32)
    lower, upper = jnp.where(is_lower, own, other), jnp.where(is_lower, other, own)
    key = jnp.where(in_front, lower, swap_halves(upper))
    keys[...] = (key * cosine[...] + swap_halves(key) * sine[...]).astype(BF16)
    values[...] = jnp.where(in_front, swap_halves(lower), upper).astype(BF16)

    @pl.loop(0, q_width // HEAD_SIZE)
    def _(head):
        cols = pl.ds(pl.multiple_of(head * HEAD_SIZE, HEAD_SIZE), HEAD_SIZE)

        @pl.loop(0, 2)
        def _(step):
            part = pl.ds(pl.multiple_of(step * tile, tile), tile)
            scores = nt(q_rot[part, cols], keys[...]) * score_scale + bias[part, :]
            raised = jnp.exp(scores - jnp.max(scores, axis=1, keepdims=True))
            prob = raised / jnp.sum(raised, axis=1, keepdims=True)
            probs[head, part, :] = prob
            mixed_values = jnp.dot(prob.astype(BF16), values[...], preferred_element_type=F32)
            attn_all[0, part, cols] = mixed_values.astype(BF16)

    rings = (attn_all, grad_all)

    def hop(i, k, source, target, device):
        ring = rings[i]
        post(ring.at[source], ring.at[target], (ring_s.at[i, k], ring_r.at[i, k]), device)

    def ring_wait(i, k, target):
        arrived(rings[i].at[target], ring_r.at[i, k])

    def ring_across(i):
        hop(i, 0, 0, 4, across)

    def ring_start(i):
        hop(i, 1, 0, 1, right)
        hop(i, 2, 0, 3, left)

    def ring_side(i):
        ring_wait(i, 0, 4)
        hop(i, 3, 4, 5, right)
        hop(i, 4, 4, 7, left)

    def ring_forward(i):
        ring_wait(i, 1, 1)
        hop(i, 5, 1, 2, right)
        ring_wait(i, 4, 7)
        hop(i, 6, 7, 6, left)

    def ring_end(i):
        for k, target in ((2, 3), (3, 5), (5, 2), (6, 6)):
            ring_wait(i, k, target)

    ring_across(0)
    ring_start(0)

    key_sum[...] = jnp.zeros_like(key_sum)
    value_sum[...] = jnp.zeros_like(value_sum)

    @pl.loop(0, q_width // HEAD_SIZE)
    def _(head):
        cols = pl.ds(pl.multiple_of(head * HEAD_SIZE, HEAD_SIZE), HEAD_SIZE)

        @pl.loop(0, 2)
        def _(step):
            part = pl.ds(pl.multiple_of(step * tile, tile), tile)
            d_out = d_attn[part, cols]
            prob = probs[head, part, :]
            d_prob = nt(d_out, values[...])
            row_delta = jnp.sum(prob * d_prob, axis=1, keepdims=True)
            d_score = (prob * (d_prob - row_delta) * score_scale).astype(BF16)
            d_query = jnp.dot(d_score, keys[...], preferred_element_type=F32)
            d_query = d_query * cosine[part, :] - swap_halves(d_query) * sine[part, :]
            grad_all[0, part, cols] = d_query.astype(BF16)
            key_sum[...] += tn(d_score, q_rot[part, cols])
            value_sum[...] += tn(prob.astype(BF16), d_out)

    d_key = key_sum[...] * cosine[...] - swap_halves(key_sum[...]) * sine[...]
    d_key, d_value = d_key.astype(BF16).astype(F32), value_sum[...].astype(BF16).astype(F32)
    lower = jnp.where(in_front, d_key, swap_halves(d_value))
    upper = jnp.where(in_front, swap_halves(d_key), d_value)
    kv_grad_send[...] = jnp.where(is_lower, upper, lower).astype(BF16)
    post(kv_grad_send, kv_grad_recv, (kv_sems.at[2], kv_sems.at[3]), twin)
    own = jnp.where(is_lower, lower, upper)
    arrived(kv_grad_recv, kv_sems.at[3])
    grad_all[0, :, q_width:] = (own + kv_grad_recv[...].astype(F32)).astype(BF16)

    weights = (o_weight, in_weight)
    half = o_weight.shape[0] // 2

    def spot(dz, side):
        there = (z + dz + 4) % 4 * 2 + side
        return (h + there // 4) % 2 * 4 + (x - there % 4 + 4) % 4

    def term(i, dz, side, which, part):
        rows = pl.ds(pl.multiple_of(which * half, half), half)
        return nt(rings[i][spot(dz, side), part, :], weights[i][rows, :])

    def give_half(i):
        for q, dz in enumerate(LEVELS):
            if i:
                halves[q].wait_send()
            for side in range(2):

                @pl.loop(0, 2)
                def _(step):
                    part = pl.ds(pl.multiple_of(step * tile, tile), tile)
                    half_send[q, side, part, :] = term(i, dz, side, 1 - core, part).astype(BF16)

            sems = (half_s.at[i, q], half_r.at[i, q])
            halves.append(send(half_send.at[q], half_recv.at[i, q], sems, twin))

    def half_wait(i, q):
        arrived(half_recv.at[i, q], half_r.at[i, q])

    def add_up(i, q, side, target, terms):
        @pl.loop(0, 2)
        def _(step):
            part = pl.ds(pl.multiple_of(step * tile, tile), tile)
            total = term(i, LEVELS[q], side, core, part)
            total = total + half_recv[i, q, side, part, :].astype(F32)
            for ref in terms:
                total = total + ref[part, :].astype(F32)
            target[part, :] = total.astype(target.dtype)

    def level_hop(i, k, slot, device):
        sems = (level_s.at[i, k], level_r.at[i, slot])
        post(level_send.at[i, k], level_recv.at[i, slot], sems, device)

    def level_wait(i, slot):
        arrived(level_recv.at[i, slot], level_r.at[i, slot])

    def far_level(i):
        half_wait(i, 0)
        add_up(i, 0, 0, level_send.at[i, 0], ())
        level_hop(i, 0, 0, below)
        add_up(i, 0, 1, level_send.at[i, 1], ())
        level_hop(i, 1, 1, above)

    def near_level(i):
        half_wait(i, 1)
        add_up(i, 1, 1, level_send.at[i, 2], ())
        level_hop(i, 2, 3, below)
        half_wait(i, 2)
        add_up(i, 2, 0, level_send.at[i, 3], ())
        level_hop(i, 3, 4, above)

    def pass_level(i):
        level_wait(i, 0)
        add_up(i, 1, 0, level_send.at[i, 4], (level_recv.at[i, 0],))
        level_hop(i, 4, 2, below)
        level_wait(i, 1)
        add_up(i, 2, 1, level_send.at[i, 5], (level_recv.at[i, 1],))
        level_hop(i, 5, 5, above)

    def own_level(i):
        half_wait(i, 3)
        for slot in range(2, 6):
            level_wait(i, slot)
        terms = (level_recv.at[i, 2 + 1 - low], level_recv.at[i, 4 + 1 - low])
        add_up(i, 3, 1 - low, side_send.at[i], terms)
        post(side_send.at[i], side_recv.at[i], (side_sems.at[i, 0], side_sems.at[i, 1]), beside)

    tp_width = half

    def columns(t):
        return mixed.at[:, pl.ds(pl.multiple_of(t * tp_width, tp_width), tp_width)]

    def last_target(i):
        return columns(tp) if i == 0 else last_recv

    def last_level(i):
        arrived(side_recv.at[i], side_sems.at[i, 1])
        terms = (level_recv.at[i, 2 + low], level_recv.at[i, 4 + low], side_recv.at[i])
        add_up(i, 3, low, last_send.at[i], terms)
        there = columns(home[1]) if i == 0 else last_recv

        @pl.when(away)
        def _():
            send(last_send.at[i], there, (hand_s.at[i], hand_r.at[i]), home)

        @pl.when(group == blk)
        def _():
            pltpu.make_async_copy(last_send.at[i], last_target(i), hand_r.at[i]).start()

    def hand_end(i):
        arrived(last_target(i), hand_r.at[i])

    def hand_sent(i):
        @pl.when(away)
        def _():
            arrived(last_send.at[i], hand_s.at[i])

    def tp_at(dz, dl, dc=0):
        return (z + dz + 4) % 4 * 4 + (low + dl) % 2 * 2 + (core + dc) % 2

    def mixed_hop(k, t, device):
        post(columns(t), columns(t), (mixed_s.at[k], mixed_r.at[k]), device)

    def mixed_wait(k, t):
        arrived(columns(t), mixed_r.at[k])

    def mixed_twin(k, t):
        post(columns(t), columns(t), (twin_s.at[k], twin_r.at[k]), twin)

    def mixed_start():
        hand_end(0)
        mixed_hop(0, tp, beside)
        mixed_hop(1, tp, above)
        mixed_hop(2, tp, below)
        mixed_twin(0, tp)

    def mixed_side():
        mixed_wait(0, tp_at(0, 1))
        mixed_hop(3, tp_at(0, 1), above)
        mixed_hop(4, tp_at(0, 1), below)
        mixed_twin(1, tp_at(0, 1))

    def mixed_forward():
        mixed_wait(1, tp_at(-1, 0))
        mixed_hop(5, tp_at(-1, 0), above)
        mixed_twin(2, tp_at(-1, 0))
        mixed_wait(2, tp_at(1, 0))
        mixed_twin(3, tp_at(1, 0))
        mixed_wait(4, tp_at(1, 1))
        mixed_hop(6, tp_at(1, 1), below)
        mixed_twin(4, tp_at(1, 1))

    def mixed_end():
        mixed_wait(3, tp_at(-1, 1))
        mixed_twin(5, tp_at(-1, 1))
        mixed_wait(5, tp_at(2, 0))
        mixed_twin(6, tp_at(2, 0))
        mixed_wait(6, tp_at(2, 1))
        mixed_twin(7, tp_at(2, 1))
        sources = ((0, 0), (0, 1), (-1, 0), (1, 0), (1, 1), (-1, 1), (2, 0), (2, 1))
        for k, (dz, dl) in enumerate(sources):
            arrived(columns(tp_at(dz, dl, 1)), twin_r.at[k])

    sources = (cot_blocks, token_blocks)
    order = (0, 4, 1, 3, 5, 7, 2, 6)
    steps = [(i, j) for i in range(2) for j in order]

    def load(n):
        i, j = steps[n]
        pltpu.make_async_copy(sources[i].at[j], column.at[n % 2], column_sem.at[n % 2]).start()

    def grad_step(n):
        i, j = steps[n]
        slot = n % 2
        arrived(column.at[slot], column_sem.at[slot])
        width = rings[i].shape[2]
        strip = 256

        @pl.loop(0, column.shape[2] // strip)
        def _(step):
            part = pl.ds(pl.multiple_of(step * strip, strip), strip)
            value = tn(column[slot, :, part], rings[i][j])
            if n % 8:
                value = value + grad_sum[part, :width]
            if n % 8 < 7:
                grad_sum[part, :width] = value
            elif i == 0:
                o_grad[part, :] = value.astype(BF16)
            else:
                q_grad[part, :] = value[:, :q_width].astype(BF16)
                kv_grad[part, :] = value[:, q_width:].astype(BF16)

        if n + 2 < len(steps):
            load(n + 2)

    load(0)
    load(1)
    ring_across(1)
    ring_side(0)
    grad_step(0)
    ring_forward(0)
    ring_start(1)
    ring_side(1)
    grad_step(1)
    ring_end(0)
    give_half(0)
    far_level(0)
    near_level(0)
    grad_step(2)
    ring_forward(1)
    pass_level(0)
    for n in range(3, 8):
        grad_step(n)
    own_level(0)
    ring_end(1)
    give_half(1)
    far_level(1)
    last_level(0)
    near_level(1)
    grad_step(8)
    grad_step(9)
    mixed_start()
    pass_level(1)
    grad_step(10)
    grad_step(11)
    mixed_side()
    grad_step(12)
    grad_step(13)
    mixed_forward()
    own_level(1)
    grad_step(14)
    grad_step(15)
    last_level(1)
    mixed_end()
    hand_end(1)
    out = pltpu.make_async_copy(last_recv, d_tokens, out_sem)
    out.start()
    for copy in sent + halves[4:]:
        copy.wait_send()
    hand_sent(0)
    hand_sent(1)
    out.wait()


def finish(proj, d_attn, cosine, sine, segments, in_weight, o_weight, token_blocks, cot_blocks):
    length, q_width = d_attn.shape
    in_width = in_weight.shape[1]
    depth = in_weight.shape[0]
    half = depth // 2
    heads = q_width // HEAD_SIZE
    dma = pltpu.SemaphoreType.DMA
    vmem = pl.BlockSpec(memory_space=pltpu.VMEM)
    hbm = pl.BlockSpec(memory_space=pl.ANY)
    part = pltpu.VMEM((length, HEAD_SIZE), BF16)
    part_sum = pltpu.VMEM((length, HEAD_SIZE), F32)
    return pl.pallas_call(
        finish_kernel,
        out_shape=(
            jax.ShapeDtypeStruct((length, 16 * half), BF16),
            jax.ShapeDtypeStruct((length, half), BF16),
            jax.ShapeDtypeStruct((depth, q_width), BF16),
            jax.ShapeDtypeStruct((depth, in_width - q_width), BF16),
            jax.ShapeDtypeStruct((depth, q_width), BF16),
        ),
        in_specs=[vmem] * 8 + [hbm] * 2,
        out_specs=(hbm, hbm, vmem, vmem, vmem),
        scratch_shapes=[
            pltpu.VMEM((8, length, q_width), BF16),
            pltpu.VMEM((8, length, in_width), BF16),
            pltpu.VMEM((length, q_width), BF16),
            pltpu.VMEM((heads, length, length), F32),
            pltpu.VMEM((length, length), F32),
            part,
            part,
            part,
            part,
            part_sum,
            part_sum,
            part,
            part,
            pltpu.VMEM((4, 2, length, half), BF16),
            pltpu.VMEM((2, 4, 2, length, half), BF16),
            pltpu.VMEM((2, 6, length, half), BF16),
            pltpu.VMEM((2, 6, length, half), BF16),
            pltpu.VMEM((2, length, half), BF16),
            pltpu.VMEM((2, length, half), BF16),
            pltpu.VMEM((2, length, half), BF16),
            pltpu.VMEM((length, half), BF16),
            pltpu.VMEM((2, length, depth), BF16),
            pltpu.VMEM((depth, in_width), F32),
            dma((4,)),
            dma((2, 7)),
            dma((2, 7)),
            dma((2, 4)),
            dma((2, 4)),
            dma((2, 6)),
            dma((2, 6)),
            dma((2, 2)),
            dma((2,)),
            dma((2,)),
            dma((7,)),
            dma((7,)),
            dma((8,)),
            dma((8,)),
            dma((2,)),
            dma,
        ],
        compiler_params=pltpu.CompilerParams(
            collective_id=1, has_side_effects=True, vmem_limit_bytes=63 * MIB
        ),
        name="finish",
    )(
        proj, d_attn, cosine, sine, segments.reshape(length, 1), segments.reshape(1, length),
        in_weight, o_weight, token_blocks, cot_blocks,
    )


def shards(tokens, segment_ids, q_weight, key_value_weight, o_weight, cotangent):
    in_weight = jnp.concatenate([q_weight, key_value_weight], axis=1)
    token_blocks, cot_blocks, proj, d_attn = project(tokens, cotangent, in_weight, o_weight)
    cosine, sine = rope_tables(tokens.shape[0], HEAD_SIZE)
    cosine = jnp.concatenate([cosine, cosine], axis=1)
    sine = jnp.concatenate([-sine, sine], axis=1)
    return finish(
        proj, d_attn, cosine, sine, segment_ids[0], in_weight, o_weight, token_blocks, cot_blocks
    )


def solution(mesh):
    in_specs = (
        P("blk", None),
        P("blk", None),
        P("blk", "tp"),
        P("blk", "tp"),
        P("blk", "tp"),
        P("blk", None),
    )
    out_specs = (P("blk", None), P("blk", "tp"), P("blk", "tp"), P("blk", "tp"), P("blk", "tp"))
    return jax.shard_map(shards, mesh=mesh, in_specs=in_specs, out_specs=out_specs, check_vma=False)
```

```python
import math

import jax
import jax.numpy as jnp
from jax import lax
from jax.experimental import pallas as pl
from jax.experimental.pallas import tpu as pltpu
from jax.sharding import PartitionSpec as P

HEAD_SIZE = 128


THETA = 10000.0


def rope_tables(length, width):
    half_width = width // 2
    position = jnp.arange(length, dtype=jnp.float32)[:, None]
    channel = jnp.arange(half_width, dtype=jnp.float32)[None, :]
    angle = position * jnp.power(THETA, -2.0 * channel / width)
    return (jnp.cos(angle), jnp.sin(angle))


MESH = pl.DeviceIdType.MESH
BF16 = jnp.bfloat16
F32 = jnp.float32
MIB = 1 << 20


def here():
    blk, tp = lax.axis_index("blk"), lax.axis_index("tp")
    return blk // 4, blk % 4, tp // 4, tp // 2 % 2, tp % 2


def near(place, dh=0, dx=0, dz=0, dl=0, dc=0):
    h, x, z, low, core = place
    h, low, core = (h + dh) % 2, (low + dl) % 2, (core + dc) % 2
    x, z = (x + dx + 4) % 4, (z + dz + 4) % 4
    return h * 4 + x, z * 4 + low * 2 + core


def greet(devices):
    barrier = pltpu.get_barrier_semaphore()
    for device in devices:
        pl.semaphore_signal(barrier, inc=1, device_id=device, device_id_type=MESH)
    pl.semaphore_wait(barrier, len(devices))


def send(source, target, sems, device):
    copy = pltpu.make_async_remote_copy(
        src_ref=source,
        dst_ref=target,
        send_sem=sems[0],
        recv_sem=sems[1],
        device_id=device,
        device_id_type=MESH,
    )
    copy.start()
    return copy


def arrived(ref, sem):
    pltpu.make_async_copy(ref, ref, sem).wait()


CHUNKS = ((0, 2), (1, 2), (1, 1), (0, 3), (0, 1), (1, 3), (1, 0), (0, 0))


def project_kernel(
    tokens, cot, in_weight, o_weight, token_out, cot_out, proj_out, d_attn_out,
    blocks, proj_send, proj_recv, cot_send, cot_recv,
    a2a_s, a2a_r, up_s, up_r, down_s, down_r, far_s, far_r, core_s, core_r, sum_s, sum_r, keep,
):
    place = here()
    h, x, z, low, core = place
    seat = z * 2 + core
    height = blocks.shape[2] // 8
    width = blocks.shape[3]
    right, left = near(place, dx=1), near(place, dx=-1)
    above, below = near(place, dz=1), near(place, dz=-1)
    twin, across = near(place, dc=1), near(place, dh=1)
    shifts = [shift for shift in CHUNKS if shift != (0, 0)]
    greet([near(place, dh=dh, dx=dx) for dh, dx in shifts] + [above, below, twin])
    sent = []

    def rows(a, dh, dx, at):
        return blocks.at[a, dh * 4 + dx, pl.ds(pl.multiple_of(at * height, height), height)]

    def level(dz):
        return (z + dz + 4) % 4 * 2 + core

    def index(dh, dx):
        return dh * 4 + dx

    def start_blocks(a, source):
        for dh, dx in CHUNKS:
            target = near(place, dh=dh, dx=dx)
            piece = source.at[
                pl.ds(pl.multiple_of(seat * height, height), height),
                pl.ds(pl.multiple_of(target[0] * width, width), width),
            ]
            j = index(dh, dx)
            if j:
                sent.append(send(piece, rows(a, dh, dx, seat), (a2a_s.at[a, j], a2a_r.at[a, j]), target))
            else:
                pltpu.make_async_copy(piece, rows(a, 0, 0, seat), a2a_r.at[a, 0]).start()

    def to_twin(a, dh, dx, which, at):
        j = index(dh, dx)
        piece = rows(a, dh, dx, at)
        sent.append(send(piece, piece, (core_s.at[a, j, which], core_r.at[a, j, which]), twin))

    def first_stage(a, dh, dx):
        j = index(dh, dx)
        piece = rows(a, dh, dx, seat)
        arrived(piece, a2a_r.at[a, j])
        sent.append(send(piece, piece, (up_s.at[a, j], up_r.at[a, j]), above))
        sent.append(send(piece, piece, (down_s.at[a, j], down_r.at[a, j]), below))
        to_twin(a, dh, dx, 0, seat)

    def second_stage(a, dh, dx):
        j = index(dh, dx)
        sems = (far_s.at[a, j], far_r.at[a, j])
        lower, upper = rows(a, dh, dx, level(-1)), rows(a, dh, dx, level(1))
        arrived(lower, up_r.at[a, j])
        if dh == 0:
            sent.append(send(lower, lower, sems, above))
        to_twin(a, dh, dx, 1, level(-1))
        arrived(upper, down_r.at[a, j])
        if dh == 1:
            sent.append(send(upper, upper, sems, below))
        to_twin(a, dh, dx, 2, level(1))

    def third_stage(a, dh, dx):
        j = index(dh, dx)
        arrived(rows(a, dh, dx, level(2)), far_r.at[a, j])
        to_twin(a, dh, dx, 3, level(2))

    def complete(a, dh, dx):
        j = index(dh, dx)
        for which, dz in enumerate((0, -1, 1, 2)):
            seat_there = (z + dz + 4) % 4 * 2 + (1 - core)
            arrived(rows(a, dh, dx, seat_there), core_r.at[a, j, which])

    weights = (in_weight, o_weight)
    outgoing = (proj_send, cot_send)
    incoming = (proj_recv, cot_recv)
    results = (proj_out, d_attn_out)
    adds = {4: (0,), 5: (1,), 6: (2, 5), 7: (3, 4, 6)}
    ways = (left, right, left, right, left, right, across)

    def chunk(a, k):
        dh, dx = CHUNKS[k]
        j = index(dh, dx)
        complete(a, dh, dx)
        terms = adds.get(k, ())
        for term in terms:
            arrived(incoming[a].at[term], sum_r.at[a, term])
        target = outgoing[a].at[k] if k < 7 else results[a]
        tile = blocks.shape[2] // 2

        @pl.loop(0, 2)
        def _(step):
            part = pl.ds(pl.multiple_of(step * tile, tile), tile)
            total = jnp.dot(blocks[a, j, part, :], weights[a][...], preferred_element_type=F32)
            for term in terms:
                total = total + incoming[a][term, part, :].astype(F32)
            target[part, :] = total.astype(target.dtype)

        if k < 7:
            sent.append(send(target, incoming[a].at[k], (sum_s.at[a, k], sum_r.at[a, k]), ways[k]))

    start_blocks(0, tokens)
    start_blocks(1, cot)
    pieces = [(a, k) for a in range(2) for k in range(8)]
    waiting = [(0, 0), (0, 1), (0, 2), (0, 3), (0, 4), (0, 5), (0, 6), (1, 0), (1, 1), (1, 2), (1, 3)]
    waiting += [(0, 7), (1, 4), (1, 5), (1, 6), (1, 7)]
    late = {(0, 6): 7, (0, 7): 9}
    for step in range(len(pieces) + 5):
        for stage, lag in ((first_stage, 0), (second_stage, 2), (third_stage, 4)):
            if 0 <= step - lag < len(pieces):
                a, k = pieces[step - lag]
                stage(a, *CHUNKS[k])
        while waiting and pieces.index(waiting[0]) + late.get(waiting[0], 5) <= step:
            chunk(*waiting.pop(0))
    assert not waiting
    keeps = [
        pltpu.make_async_copy(blocks.at[0], token_out, keep.at[0]),
        pltpu.make_async_copy(blocks.at[1], cot_out, keep.at[1]),
    ]
    for copy in keeps:
        copy.start()
    for copy in sent:
        copy.wait_send()
    for copy in keeps:
        copy.wait()


def project(tokens, cot, in_weight, o_weight):
    length = tokens.shape[0]
    width = tokens.shape[1] // 8
    in_width, o_width = in_weight.shape[1], o_weight.shape[1]
    dma = pltpu.SemaphoreType.DMA
    pair = [dma((2, 8)), dma((2, 8))]
    block = jax.ShapeDtypeStruct((8, length, width), BF16)
    return pl.pallas_call(
        project_kernel,
        out_shape=(
            block,
            block,
            jax.ShapeDtypeStruct((length, in_width), F32),
            jax.ShapeDtypeStruct((length, o_width), BF16),
        ),
        in_specs=[pl.BlockSpec(memory_space=pl.ANY)] * 2
        + [pl.BlockSpec(memory_space=pltpu.VMEM)] * 2,
        out_specs=(pl.BlockSpec(memory_space=pl.ANY),) * 2
        + (pl.BlockSpec(memory_space=pltpu.VMEM),) * 2,
        scratch_shapes=[
            pltpu.VMEM((2, 8, length, width), BF16),
            pltpu.VMEM((7, length, in_width), BF16),
            pltpu.VMEM((7, length, in_width), BF16),
            pltpu.VMEM((7, length, o_width), BF16),
            pltpu.VMEM((7, length, o_width), BF16),
            *pair,
            *pair,
            *pair,
            *pair,
            dma((2, 8, 4)),
            dma((2, 8, 4)),
            dma((2, 7)),
            dma((2, 7)),
            dma((2,)),
        ],
        compiler_params=pltpu.CompilerParams(
            collective_id=0, has_side_effects=True, vmem_limit_bytes=56 * MIB
        ),
        name="project",
    )(tokens, cot, in_weight, o_weight)


def nt(left, right):
    return lax.dot_general(left, right, (((1,), (1,)), ((), ())), preferred_element_type=F32)


def tn(left, right):
    return lax.dot_general(left, right, (((0,), (0,)), ((), ())), preferred_element_type=F32)


def swap_halves(array):
    return pltpu.roll(array, array.shape[1] // 2, 1)


LEVELS = (2, -1, 1, 0)


def finish_kernel(
    proj, d_attn, cosine, sine, seg_col, seg_row, in_weight, o_weight, token_blocks, cot_blocks,
    mixed, d_tokens, q_grad, kv_grad, o_grad,
    attn_all, grad_all, q_rot, probs, bias, keys, values, kv_send, kv_recv, key_sum, value_sum,
    kv_grad_send, kv_grad_recv,
    half_send, half_recv, level_send, level_recv, side_send, side_recv, last_send, last_recv,
    column, grad_sum,
    kv_sems, ring_s, ring_r, half_s, half_r, level_s, level_r, side_sems, hand_s, hand_r,
    mixed_s, mixed_r, twin_s, twin_r, column_sem, out_sem,
):
    place = here()
    h, x, z, low, core = place
    blk = h * 4 + x
    length, q_width = d_attn.shape
    tile = length // 2
    score_scale = 1.0 / math.sqrt(HEAD_SIZE)
    right, left = near(place, dx=1), near(place, dx=-1)
    above, below = near(place, dz=1), near(place, dz=-1)
    twin, across, beside = near(place, dc=1), near(place, dh=1), near(place, dl=1)
    halves = []
    far_h, far_x = z // 2, z % 2 * 2 + low
    origin = z * 2 + low
    origin_h, origin_x = (origin // 4 + h) % 2, (origin % 4 - x + 4) % 4
    homes = (
        near(place, dh=far_h, dx=-far_x),
        (near(place, dh=far_h, dx=-far_x)[0], blk * 2 + core),
    )
    givers = (
        near(place, dh=far_h, dx=far_x),
        (origin, (origin_h * 2 + origin_x // 2) * 4 + origin_x % 2 * 2 + core),
    )
    stays = (z * 2 + low == 0, z * 2 + low + blk == 0)
    sent, halves = [], []

    barrier = pltpu.get_barrier_semaphore()
    for device in (right, left, above, below, twin, across, beside):
        pl.semaphore_signal(barrier, inc=1, device_id=device, device_id_type=MESH)
    for i in range(2):

        @pl.when(jnp.logical_not(stays[i]))
        def _():
            pl.semaphore_signal(barrier, inc=1, device_id=givers[i], device_id_type=MESH)

    pl.semaphore_wait(barrier, 9 - jnp.where(stays[0], 1, 0) - jnp.where(stays[1], 1, 0))

    def post(source, target, sems, device):
        sent.append(send(source, target, sems, device))

    lane = lax.broadcasted_iota(jnp.int32, (length, HEAD_SIZE), 1)
    in_front = lane < HEAD_SIZE // 2
    is_lower = jnp.full((length, HEAD_SIZE), core) == 0
    kv_send[...] = proj[:, q_width:].astype(BF16)
    post(kv_send, kv_recv, (kv_sems.at[0], kv_sems.at[1]), twin)

    @pl.loop(0, 2)
    def _(step):
        start = pl.multiple_of(step * tile, tile)
        part = pl.ds(start, tile)
        row = lax.broadcasted_iota(jnp.int32, (tile, length), 0) + start
        key = lax.broadcasted_iota(jnp.int32, (tile, length), 1)
        allowed = (key <= row) & (seg_col[part, :] == seg_row[...])
        bias[part, :] = jnp.where(allowed, 0.0, -jnp.inf)

    @pl.loop(0, q_width // HEAD_SIZE)
    def _(head):
        cols = pl.ds(pl.multiple_of(head * HEAD_SIZE, HEAD_SIZE), HEAD_SIZE)
        query = proj[:, cols]
        q_rot[:, cols] = (query * cosine[...] + swap_halves(query) * sine[...]).astype(BF16)

    arrived(kv_recv, kv_sems.at[1])
    own, other = kv_send[...].astype(F32), kv_recv[...].astype(F32)
    lower, upper = jnp.where(is_lower, own, other), jnp.where(is_lower, other, own)
    key = jnp.where(in_front, lower, swap_halves(upper))
    keys[...] = (key * cosine[...] + swap_halves(key) * sine[...]).astype(BF16)
    values[...] = jnp.where(in_front, swap_halves(lower), upper).astype(BF16)

    @pl.loop(0, q_width // HEAD_SIZE)
    def _(head):
        cols = pl.ds(pl.multiple_of(head * HEAD_SIZE, HEAD_SIZE), HEAD_SIZE)

        @pl.loop(0, 2)
        def _(step):
            part = pl.ds(pl.multiple_of(step * tile, tile), tile)
            scores = nt(q_rot[part, cols], keys[...]) * score_scale + bias[part, :]
            raised = jnp.exp(scores - jnp.max(scores, axis=1, keepdims=True))
            prob = raised / jnp.sum(raised, axis=1, keepdims=True)
            probs[head, part, :] = prob
            mixed_values = jnp.dot(prob.astype(BF16), values[...], preferred_element_type=F32)
            attn_all[0, part, cols] = mixed_values.astype(BF16)

    rings = (attn_all, grad_all)

    def hop(i, k, source, target, device):
        ring = rings[i]
        post(ring.at[source], ring.at[target], (ring_s.at[i, k], ring_r.at[i, k]), device)

    def ring_wait(i, k, target):
        arrived(rings[i].at[target], ring_r.at[i, k])

    def ring_across(i):
        hop(i, 0, 0, 4, across)

    def ring_start(i):
        hop(i, 1, 0, 1, right)
        hop(i, 2, 0, 3, left)

    def ring_side(i):
        ring_wait(i, 0, 4)
        hop(i, 3, 4, 5, right)
        hop(i, 4, 4, 7, left)

    def ring_pass(i):
        ring_wait(i, 1, 1)
        hop(i, 5, 1, 2, right)

    def ring_back(i):
        ring_wait(i, 4, 7)
        hop(i, 6, 7, 6, left)

    def ring_end(i):
        for k, target in ((2, 3), (3, 5), (5, 2), (6, 6)):
            ring_wait(i, k, target)

    ring_across(0)
    ring_start(0)

    key_sum[...] = jnp.zeros_like(key_sum)
    value_sum[...] = jnp.zeros_like(value_sum)

    @pl.loop(0, q_width // HEAD_SIZE)
    def _(head):
        cols = pl.ds(pl.multiple_of(head * HEAD_SIZE, HEAD_SIZE), HEAD_SIZE)

        @pl.loop(0, 2)
        def _(step):
            part = pl.ds(pl.multiple_of(step * tile, tile), tile)
            d_out = d_attn[part, cols]
            prob = probs[head, part, :]
            d_prob = nt(d_out, values[...])
            row_delta = jnp.sum(prob * d_prob, axis=1, keepdims=True)
            d_score = (prob * (d_prob - row_delta) * score_scale).astype(BF16)
            d_query = jnp.dot(d_score, keys[...], preferred_element_type=F32)
            d_query = d_query * cosine[part, :] - swap_halves(d_query) * sine[part, :]
            grad_all[0, part, cols] = d_query.astype(BF16)
            key_sum[...] += tn(d_score, q_rot[part, cols])
            value_sum[...] += tn(prob.astype(BF16), d_out)

    d_key = key_sum[...] * cosine[...] - swap_halves(key_sum[...]) * sine[...]
    d_key, d_value = d_key.astype(BF16).astype(F32), value_sum[...].astype(BF16).astype(F32)
    lower = jnp.where(in_front, d_key, swap_halves(d_value))
    upper = jnp.where(in_front, swap_halves(d_key), d_value)
    kv_grad_send[...] = jnp.where(is_lower, upper, lower).astype(BF16)
    post(kv_grad_send, kv_grad_recv, (kv_sems.at[2], kv_sems.at[3]), twin)
    own = jnp.where(is_lower, lower, upper)
    arrived(kv_grad_recv, kv_sems.at[3])
    grad_all[0, :, q_width:] = (own + kv_grad_recv[...].astype(F32)).astype(BF16)

    weights = (o_weight, in_weight)
    half = o_weight.shape[0] // 2

    def spot(dz, side):
        return (z + dz + 4) % 4 * 2 + side

    def term(i, dz, side, which, part):
        rows = pl.ds(pl.multiple_of(which * half, half), half)
        return nt(rings[i][spot(dz, side), part, :], weights[i][rows, :])

    def give_half(i):
        for q, dz in enumerate(LEVELS):
            if i:
                halves[q].wait_send()
            for side in range(2):

                @pl.loop(0, 2)
                def _(step):
                    part = pl.ds(pl.multiple_of(step * tile, tile), tile)
                    half_send[q, side, part, :] = term(i, dz, side, 1 - core, part).astype(BF16)

            sems = (half_s.at[i, q], half_r.at[i, q])
            halves.append(send(half_send.at[q], half_recv.at[i, q], sems, twin))

    def half_wait(i, q):
        arrived(half_recv.at[i, q], half_r.at[i, q])

    def add_up(i, q, side, target, terms):
        @pl.loop(0, 2)
        def _(step):
            part = pl.ds(pl.multiple_of(step * tile, tile), tile)
            total = term(i, LEVELS[q], side, core, part)
            total = total + half_recv[i, q, side, part, :].astype(F32)
            for ref in terms:
                total = total + ref[part, :].astype(F32)
            target[part, :] = total.astype(target.dtype)

    def level_hop(i, k, slot, device):
        sems = (level_s.at[i, k], level_r.at[i, slot])
        post(level_send.at[i, k], level_recv.at[i, slot], sems, device)

    def level_wait(i, slot):
        arrived(level_recv.at[i, slot], level_r.at[i, slot])

    def far_level(i):
        half_wait(i, 0)
        add_up(i, 0, 0, level_send.at[i, 0], ())
        level_hop(i, 0, 0, below)
        add_up(i, 0, 1, level_send.at[i, 1], ())
        level_hop(i, 1, 1, above)

    def near_level(i):
        half_wait(i, 1)
        add_up(i, 1, 1, level_send.at[i, 2], ())
        level_hop(i, 2, 3, below)
        half_wait(i, 2)
        add_up(i, 2, 0, level_send.at[i, 3], ())
        level_hop(i, 3, 4, above)

    def pass_level(i):
        level_wait(i, 0)
        add_up(i, 1, 0, level_send.at[i, 4], (level_recv.at[i, 0],))
        level_hop(i, 4, 2, below)
        level_wait(i, 1)
        add_up(i, 2, 1, level_send.at[i, 5], (level_recv.at[i, 1],))
        level_hop(i, 5, 5, above)

    def own_level(i):
        half_wait(i, 3)
        for slot in range(2, 6):
            level_wait(i, slot)
        terms = (level_recv.at[i, 2 + 1 - low], level_recv.at[i, 4 + 1 - low])
        add_up(i, 3, 1 - low, side_send.at[i], terms)
        post(side_send.at[i], side_recv.at[i], (side_sems.at[i, 0], side_sems.at[i, 1]), beside)

    tp_width = half

    def columns(t):
        return mixed.at[:, pl.ds(pl.multiple_of(t * tp_width, tp_width), tp_width)]

    def tp_at(dz, dl, dc=0):
        level, side = (z + dz + 4) % 4, (low + dl) % 2
        owner = (h + level // 2) % 2 * 4 + (x + level % 2 * 2 + side) % 4
        return owner * 2 + (core + dc) % 2

    def last_target(i):
        return columns(tp_at(0, 0)) if i == 0 else last_recv

    def last_level(i):
        arrived(side_recv.at[i], side_sems.at[i, 1])
        terms = (level_recv.at[i, 2 + low], level_recv.at[i, 4 + low], side_recv.at[i])
        add_up(i, 3, low, last_send.at[i], terms)
        there = columns(blk * 2 + core) if i == 0 else last_recv

        @pl.when(jnp.logical_not(stays[i]))
        def _():
            send(last_send.at[i], there, (hand_s.at[i], hand_r.at[i]), homes[i])

        @pl.when(stays[i])
        def _():
            pltpu.make_async_copy(last_send.at[i], last_target(i), hand_r.at[i]).start()

    def hand_end(i):
        arrived(last_target(i), hand_r.at[i])

    def hand_sent(i):
        @pl.when(jnp.logical_not(stays[i]))
        def _():
            arrived(last_send.at[i], hand_s.at[i])

    whole, top, bottom = (0, length), (0, tile), (tile, tile)
    quarters = ((tile, tile // 2), (tile + tile // 2, tile // 2))

    def cell(t, rows):
        return columns(t).at[pl.ds(*rows)]

    def mixed_hop(k, t, rows, device):
        post(cell(t, rows), cell(t, rows), (mixed_s.at[k], mixed_r.at[k]), device)

    def mixed_wait(k, t, rows):
        arrived(cell(t, rows), mixed_r.at[k])

    given = []

    def mixed_twin(dz, dl, rows):
        k, t = len(given), tp_at(dz, dl)
        given.append((tp_at(dz, dl, 1), rows))
        post(cell(t, rows), cell(t, rows), (twin_s.at[k], twin_r.at[k]), twin)

    def mixed_start():
        hand_end(0)
        mixed_hop(0, tp_at(0, 0), top, beside)
        mixed_hop(7, tp_at(0, 0), bottom, above)
        mixed_hop(8, tp_at(0, 0), bottom, below)
        mixed_hop(1, tp_at(0, 0), top, above)
        mixed_hop(2, tp_at(0, 0), top, below)
        mixed_hop(11, tp_at(0, 0), bottom, beside)
        mixed_twin(0, 0, whole)

    def mixed_side():
        mixed_wait(0, tp_at(0, 1), top)
        mixed_hop(3, tp_at(0, 1), top, above)
        mixed_hop(4, tp_at(0, 1), top, below)
        mixed_twin(0, 1, top)

    def mixed_bottom():
        mixed_wait(7, tp_at(-1, 0), bottom)
        mixed_hop(9, tp_at(-1, 0), quarters[0], above)
        mixed_hop(12, tp_at(-1, 0), bottom, beside)
        mixed_twin(-1, 0, bottom)
        mixed_wait(8, tp_at(1, 0), bottom)
        mixed_hop(10, tp_at(1, 0), quarters[1], below)
        mixed_hop(13, tp_at(1, 0), bottom, beside)
        mixed_twin(1, 0, bottom)

    def mixed_pass():
        mixed_wait(1, tp_at(-1, 0), top)
        mixed_hop(5, tp_at(-1, 0), top, above)
        mixed_twin(-1, 0, top)
        mixed_wait(2, tp_at(1, 0), top)
        mixed_twin(1, 0, top)

    def mixed_back():
        mixed_wait(4, tp_at(1, 1), top)
        mixed_hop(6, tp_at(1, 1), top, below)
        mixed_twin(1, 1, top)

    def mixed_far():
        mixed_wait(9, tp_at(2, 0), quarters[0])
        mixed_wait(10, tp_at(2, 0), quarters[1])
        mixed_hop(14, tp_at(2, 0), bottom, beside)
        mixed_twin(2, 0, bottom)
        mixed_wait(11, tp_at(0, 1), bottom)
        mixed_twin(0, 1, bottom)
        mixed_wait(12, tp_at(-1, 1), bottom)
        mixed_twin(-1, 1, bottom)
        mixed_wait(13, tp_at(1, 1), bottom)
        mixed_twin(1, 1, bottom)

    def mixed_end():
        for k, dz, dl, rows in ((3, -1, 1, top), (5, 2, 0, top), (6, 2, 1, top), (14, 2, 1, bottom)):
            mixed_wait(k, tp_at(dz, dl), rows)
            mixed_twin(dz, dl, rows)
        for k, (t, rows) in enumerate(given):
            arrived(cell(t, rows), twin_r.at[k])

    sources = (cot_blocks, token_blocks)
    order = (0, 4, 1, 3, 5, 7, 2, 6)
    steps = [(i, j) for i in range(2) for j in order]

    def load(n):
        i, j = steps[n]
        pltpu.make_async_copy(sources[i].at[j], column.at[n % 2], column_sem.at[n % 2]).start()

    def grad_step(n):
        i, j = steps[n]
        slot = n % 2
        arrived(column.at[slot], column_sem.at[slot])
        width = rings[i].shape[2]
        strip = 256

        @pl.loop(0, column.shape[2] // strip)
        def _(step):
            part = pl.ds(pl.multiple_of(step * strip, strip), strip)
            value = tn(column[slot, :, part], rings[i][j])
            if n % 8:
                value = value + grad_sum[part, :width]
            if n % 8 < 7:
                grad_sum[part, :width] = value
            elif i == 0:
                o_grad[part, :] = value.astype(BF16)
            else:
                q_grad[part, :] = value[:, :q_width].astype(BF16)
                kv_grad[part, :] = value[:, q_width:].astype(BF16)

        if n + 2 < len(steps):
            load(n + 2)

    load(0)
    load(1)
    ring_across(1)
    grad_step(0)
    ring_side(0)
    grad_step(1)
    ring_pass(0)
    grad_step(2)
    ring_back(0)
    ring_start(1)
    ring_side(1)
    ring_end(0)
    give_half(0)
    far_level(0)
    near_level(0)
    ring_pass(1)
    grad_step(3)
    pass_level(0)
    grad_step(4)
    grad_step(5)
    ring_back(1)
    grad_step(6)
    grad_step(7)
    own_level(0)
    ring_end(1)
    give_half(1)
    far_level(1)
    last_level(0)
    near_level(1)
    grad_step(8)
    pass_level(1)
    mixed_start()
    grad_step(9)
    grad_step(10)
    grad_step(11)
    mixed_side()
    grad_step(12)
    own_level(1)
    mixed_bottom()
    grad_step(13)
    mixed_pass()
    grad_step(14)
    grad_step(15)
    last_level(1)
    mixed_far()
    mixed_back()
    mixed_end()
    hand_end(1)
    out = pltpu.make_async_copy(last_recv, d_tokens, out_sem)
    out.start()
    for copy in sent + halves[4:]:
        copy.wait_send()
    hand_sent(0)
    hand_sent(1)
    out.wait()


def finish(proj, d_attn, cosine, sine, segments, in_weight, o_weight, token_blocks, cot_blocks):
    length, q_width = d_attn.shape
    in_width = in_weight.shape[1]
    depth = in_weight.shape[0]
    half = depth // 2
    heads = q_width // HEAD_SIZE
    dma = pltpu.SemaphoreType.DMA
    vmem = pl.BlockSpec(memory_space=pltpu.VMEM)
    hbm = pl.BlockSpec(memory_space=pl.ANY)
    part = pltpu.VMEM((length, HEAD_SIZE), BF16)
    part_sum = pltpu.VMEM((length, HEAD_SIZE), F32)
    return pl.pallas_call(
        finish_kernel,
        out_shape=(
            jax.ShapeDtypeStruct((length, 16 * half), BF16),
            jax.ShapeDtypeStruct((length, half), BF16),
            jax.ShapeDtypeStruct((depth, q_width), BF16),
            jax.ShapeDtypeStruct((depth, in_width - q_width), BF16),
            jax.ShapeDtypeStruct((depth, q_width), BF16),
        ),
        in_specs=[vmem] * 8 + [hbm] * 2,
        out_specs=(hbm, hbm, vmem, vmem, vmem),
        scratch_shapes=[
            pltpu.VMEM((8, length, q_width), BF16),
            pltpu.VMEM((8, length, in_width), BF16),
            pltpu.VMEM((length, q_width), BF16),
            pltpu.VMEM((heads, length, length), F32),
            pltpu.VMEM((length, length), F32),
            part,
            part,
            part,
            part,
            part_sum,
            part_sum,
            part,
            part,
            pltpu.VMEM((4, 2, length, half), BF16),
            pltpu.VMEM((2, 4, 2, length, half), BF16),
            pltpu.VMEM((2, 6, length, half), BF16),
            pltpu.VMEM((2, 6, length, half), BF16),
            pltpu.VMEM((2, length, half), BF16),
            pltpu.VMEM((2, length, half), BF16),
            pltpu.VMEM((2, length, half), BF16),
            pltpu.VMEM((length, half), BF16),
            pltpu.VMEM((2, length, depth), BF16),
            pltpu.VMEM((depth, in_width), F32),
            dma((4,)),
            dma((2, 7)),
            dma((2, 7)),
            dma((2, 4)),
            dma((2, 4)),
            dma((2, 6)),
            dma((2, 6)),
            dma((2, 2)),
            dma((2,)),
            dma((2,)),
            dma((15,)),
            dma((15,)),
            dma((15,)),
            dma((15,)),
            dma((2,)),
            dma,
        ],
        compiler_params=pltpu.CompilerParams(
            collective_id=1, has_side_effects=True, vmem_limit_bytes=63 * MIB
        ),
        name="finish",
    )(
        proj, d_attn, cosine, sine, segments.reshape(length, 1), segments.reshape(1, length),
        in_weight, o_weight, token_blocks, cot_blocks,
    )


def shards(tokens, segment_ids, q_weight, key_value_weight, o_weight, cotangent):
    in_weight = jnp.concatenate([q_weight, key_value_weight], axis=1)
    token_blocks, cot_blocks, proj, d_attn = project(tokens, cotangent, in_weight, o_weight)
    cosine, sine = rope_tables(tokens.shape[0], HEAD_SIZE)
    cosine = jnp.concatenate([cosine, cosine], axis=1)
    sine = jnp.concatenate([-sine, sine], axis=1)
    return finish(
        proj, d_attn, cosine, sine, segment_ids[0], in_weight, o_weight, token_blocks, cot_blocks
    )


def solution(mesh):
    in_specs = (
        P("blk", None),
        P("blk", None),
        P("blk", "tp"),
        P("blk", "tp"),
        P("blk", "tp"),
        P("blk", None),
    )
    out_specs = (P("blk", None), P("blk", "tp"), P("blk", "tp"), P("blk", "tp"), P("blk", "tp"))
    return jax.shard_map(shards, mesh=mesh, in_specs=in_specs, out_specs=out_specs, check_vma=False)
```

```python
import math

import jax
import jax.numpy as jnp
from jax import lax
from jax.experimental import pallas as pl
from jax.experimental.pallas import tpu as pltpu
from jax.sharding import PartitionSpec as P

HEAD_SIZE = 128


THETA = 10000.0


def rope_tables(length, width):
    half_width = width // 2
    position = jnp.arange(length, dtype=jnp.float32)[:, None]
    channel = jnp.arange(half_width, dtype=jnp.float32)[None, :]
    angle = position * jnp.power(THETA, -2.0 * channel / width)
    return (jnp.cos(angle), jnp.sin(angle))


MESH = pl.DeviceIdType.MESH
BF16 = jnp.bfloat16
F32 = jnp.float32
MIB = 1 << 20


def here():
    blk, tp = lax.axis_index("blk"), lax.axis_index("tp")
    return blk // 4, blk % 4, tp // 4, tp // 2 % 2, tp % 2


def near(place, dh=0, dx=0, dz=0, dl=0, dc=0):
    h, x, z, low, core = place
    h, low, core = (h + dh) % 2, (low + dl) % 2, (core + dc) % 2
    x, z = (x + dx + 4) % 4, (z + dz + 4) % 4
    return h * 4 + x, z * 4 + low * 2 + core


def greet(devices):
    barrier = pltpu.get_barrier_semaphore()
    for device in devices:
        pl.semaphore_signal(barrier, inc=1, device_id=device, device_id_type=MESH)
    pl.semaphore_wait(barrier, len(devices))


def send(source, target, sems, device):
    copy = pltpu.make_async_remote_copy(
        src_ref=source,
        dst_ref=target,
        send_sem=sems[0],
        recv_sem=sems[1],
        device_id=device,
        device_id_type=MESH,
    )
    copy.start()
    return copy


def arrived(ref, sem):
    pltpu.make_async_copy(ref, ref, sem).wait()


def load_weights(q_weight, kv_weight, o_source, in_weight, o_weight, sems):
    width = q_weight.shape[1]
    kv_part = pl.ds(width, kv_weight.shape[1])
    loads = [
        pltpu.make_async_copy(q_weight, in_weight.at[:, pl.ds(0, width)], sems.at[0]),
        pltpu.make_async_copy(kv_weight, in_weight.at[:, kv_part], sems.at[1]),
        pltpu.make_async_copy(o_source, o_weight, sems.at[2]),
    ]
    for held in loads:
        held.start()
    return loads


CHUNKS = ((0, 2), (1, 2), (1, 1), (0, 3), (0, 1), (1, 3), (1, 0), (0, 0))


def project_kernel(
    tokens, cot, q_weight, kv_weight, o_source, token_out, cot_out, proj_out, d_attn_out,
    in_weight, o_weight, weight_sem, blocks, proj_send, proj_recv, cot_send, cot_recv,
    a2a_s, a2a_r, up_s, up_r, down_s, down_r, far_s, far_r, core_s, core_r, sum_s, sum_r, keep,
):
    place = here()
    h, x, z, low, core = place
    seat = z * 2 + core
    height = blocks.shape[2] // 8
    width = blocks.shape[3]
    right, left = near(place, dx=1), near(place, dx=-1)
    above, below = near(place, dz=1), near(place, dz=-1)
    twin, across = near(place, dc=1), near(place, dh=1)
    shifts = [shift for shift in CHUNKS if shift != (0, 0)]
    loads = load_weights(q_weight, kv_weight, o_source, in_weight, o_weight, weight_sem)
    greet([near(place, dh=dh, dx=dx) for dh, dx in shifts] + [above, below, twin])
    sent = []

    def rows(a, dh, dx, at):
        return blocks.at[a, dh * 4 + dx, pl.ds(pl.multiple_of(at * height, height), height)]

    def level(dz):
        return (z + dz + 4) % 4 * 2 + core

    def index(dh, dx):
        return dh * 4 + dx

    def start_blocks(a, source):
        for dh, dx in CHUNKS:
            target = near(place, dh=dh, dx=dx)
            piece = source.at[
                pl.ds(pl.multiple_of(seat * height, height), height),
                pl.ds(pl.multiple_of(target[0] * width, width), width),
            ]
            j = index(dh, dx)
            if j:
                sent.append(send(piece, rows(a, dh, dx, seat), (a2a_s.at[a, j], a2a_r.at[a, j]), target))
            else:
                pltpu.make_async_copy(piece, rows(a, 0, 0, seat), a2a_r.at[a, 0]).start()

    def to_twin(a, dh, dx, which, at):
        j = index(dh, dx)
        piece = rows(a, dh, dx, at)
        sent.append(send(piece, piece, (core_s.at[a, j, which], core_r.at[a, j, which]), twin))

    def first_stage(a, dh, dx):
        j = index(dh, dx)
        piece = rows(a, dh, dx, seat)
        arrived(piece, a2a_r.at[a, j])
        sent.append(send(piece, piece, (up_s.at[a, j], up_r.at[a, j]), above))
        sent.append(send(piece, piece, (down_s.at[a, j], down_r.at[a, j]), below))
        to_twin(a, dh, dx, 0, seat)

    def second_stage(a, dh, dx):
        j = index(dh, dx)
        sems = (far_s.at[a, j], far_r.at[a, j])
        lower, upper = rows(a, dh, dx, level(-1)), rows(a, dh, dx, level(1))
        arrived(lower, up_r.at[a, j])
        if dh == 0:
            sent.append(send(lower, lower, sems, above))
        to_twin(a, dh, dx, 1, level(-1))
        arrived(upper, down_r.at[a, j])
        if dh == 1:
            sent.append(send(upper, upper, sems, below))
        to_twin(a, dh, dx, 2, level(1))

    def third_stage(a, dh, dx):
        j = index(dh, dx)
        arrived(rows(a, dh, dx, level(2)), far_r.at[a, j])
        to_twin(a, dh, dx, 3, level(2))

    def complete(a, dh, dx):
        j = index(dh, dx)
        for which, dz in enumerate((0, -1, 1, 2)):
            seat_there = (z + dz + 4) % 4 * 2 + (1 - core)
            arrived(rows(a, dh, dx, seat_there), core_r.at[a, j, which])

    weights = (in_weight, o_weight)
    outgoing = (proj_send, cot_send)
    incoming = (proj_recv, cot_recv)
    results = (proj_out, d_attn_out)
    adds = {4: (0,), 5: (1,), 6: (2, 5), 7: (3, 4, 6)}
    ways = (left, right, left, right, left, right, across)

    def chunk(a, k):
        dh, dx = CHUNKS[k]
        j = index(dh, dx)
        complete(a, dh, dx)
        terms = adds.get(k, ())
        for term in terms:
            arrived(incoming[a].at[term], sum_r.at[a, term])
        target = outgoing[a].at[k] if k < 7 else results[a]
        tile = blocks.shape[2] // 2

        @pl.loop(0, 2)
        def _(step):
            part = pl.ds(pl.multiple_of(step * tile, tile), tile)
            total = jnp.dot(blocks[a, j, part, :], weights[a][...], preferred_element_type=F32)
            for term in terms:
                total = total + incoming[a][term, part, :].astype(F32)
            target[part, :] = total.astype(target.dtype)

        if k < 7:
            sent.append(send(target, incoming[a].at[k], (sum_s.at[a, k], sum_r.at[a, k]), ways[k]))

    start_blocks(0, tokens)
    start_blocks(1, cot)
    pieces = [(a, k) for a in range(2) for k in range(8)]
    waiting = [(0, 0), (0, 1), (0, 2), (0, 3), (0, 4), (0, 5), (0, 6), (1, 0), (1, 1), (1, 2), (1, 3)]
    waiting += [(0, 7), (1, 4), (1, 5), (1, 6), (1, 7)]
    late = {(0, 6): 7, (0, 7): 9}
    for step in range(len(pieces) + 5):
        for stage, lag in ((first_stage, 0), (second_stage, 2), (third_stage, 4)):
            if 0 <= step - lag < len(pieces):
                a, k = pieces[step - lag]
                stage(a, *CHUNKS[k])
        if step == 4:
            for held in loads:
                held.wait()
        while waiting and pieces.index(waiting[0]) + late.get(waiting[0], 5) <= step:
            chunk(*waiting.pop(0))
    assert not waiting
    keeps = [
        pltpu.make_async_copy(blocks.at[0], token_out, keep.at[0]),
        pltpu.make_async_copy(blocks.at[1], cot_out, keep.at[1]),
    ]
    for copy in keeps:
        copy.start()
    for copy in sent:
        copy.wait_send()
    for copy in keeps:
        copy.wait()


def project(tokens, cot, q_weight, kv_weight, o_weight):
    length = tokens.shape[0]
    width = tokens.shape[1] // 8
    in_width, o_width = q_weight.shape[1] + kv_weight.shape[1], o_weight.shape[1]
    depth = q_weight.shape[0]
    dma = pltpu.SemaphoreType.DMA
    pair = [dma((2, 8)), dma((2, 8))]
    block = jax.ShapeDtypeStruct((8, length, width), BF16)
    return pl.pallas_call(
        project_kernel,
        out_shape=(
            block,
            block,
            jax.ShapeDtypeStruct((length, in_width), F32),
            jax.ShapeDtypeStruct((length, o_width), BF16),
        ),
        in_specs=[pl.BlockSpec(memory_space=pl.ANY)] * 5,
        out_specs=(pl.BlockSpec(memory_space=pl.ANY),) * 2
        + (pl.BlockSpec(memory_space=pltpu.VMEM),) * 2,
        scratch_shapes=[
            pltpu.VMEM((depth, in_width), BF16),
            pltpu.VMEM((depth, o_width), BF16),
            dma((3,)),
            pltpu.VMEM((2, 8, length, width), BF16),
            pltpu.VMEM((7, length, in_width), BF16),
            pltpu.VMEM((7, length, in_width), BF16),
            pltpu.VMEM((7, length, o_width), BF16),
            pltpu.VMEM((7, length, o_width), BF16),
            *pair,
            *pair,
            *pair,
            *pair,
            dma((2, 8, 4)),
            dma((2, 8, 4)),
            dma((2, 7)),
            dma((2, 7)),
            dma((2,)),
        ],
        compiler_params=pltpu.CompilerParams(
            collective_id=0, has_side_effects=True, vmem_limit_bytes=56 * MIB
        ),
        name="project",
    )(tokens, cot, q_weight, kv_weight, o_weight)


def nt(left, right):
    return lax.dot_general(left, right, (((1,), (1,)), ((), ())), preferred_element_type=F32)


def tn(left, right):
    return lax.dot_general(left, right, (((0,), (0,)), ((), ())), preferred_element_type=F32)


def swap_halves(array):
    return pltpu.roll(array, array.shape[1] // 2, 1)


LEVELS = (2, -1, 1, 0)


def finish_kernel(
    proj, d_attn, cosine, sine, seg_row, q_weight, kv_weight, o_source, token_blocks, cot_blocks,
    mixed, d_tokens, q_grad, kv_grad, o_grad, in_weight, o_weight, weight_sem,
    attn_all, grad_all, q_rot, probs, bias, seg_cols, keys, values, kv_send, kv_recv, key_sum, value_sum,
    kv_grad_send, kv_grad_recv,
    half_send, half_recv, level_send, level_recv, side_send, side_recv, cross_send, cross_recv,
    plane_send, plane_recv, last_send, last_recv,
    column, grad_sum,
    kv_sems, ring_s, ring_r, half_s, half_r, level_s, level_r, side_sems, cross_s, cross_r,
    plane_s, plane_r, hand_s, hand_r,
    mixed_s, mixed_r, twin_s, twin_r, column_sem, out_sem,
):
    place = here()
    h, x, z, low, core = place
    blk = h * 4 + x
    length, q_width = d_attn.shape
    tile = length // 2
    score_scale = 1.0 / math.sqrt(HEAD_SIZE)
    right, left = near(place, dx=1), near(place, dx=-1)
    above, below = near(place, dz=1), near(place, dz=-1)
    twin, across, beside = near(place, dc=1), near(place, dh=1), near(place, dl=1)
    halves = []
    far_h, far_x = z // 2, z % 2 * 2 + low
    origin = z * 2 + low
    origin_h, origin_x = (origin // 4 + h) % 2, (origin % 4 - x + 4) % 4
    homes = (
        near(place, dh=far_h, dx=-far_x),
        (near(place, dh=far_h, dx=-far_x)[0], blk * 2 + core),
    )
    givers = (
        near(place, dh=far_h, dx=far_x),
        (origin, (origin_h * 2 + origin_x // 2) * 4 + origin_x % 2 * 2 + core),
    )
    stays = (z * 2 + low == 0, z * 2 + low + blk == 0)
    sent, halves = [], []
    loads = load_weights(q_weight, kv_weight, o_source, in_weight, o_weight, weight_sem)

    barrier = pltpu.get_barrier_semaphore()
    for device in (right, left, above, below, twin, across, beside):
        pl.semaphore_signal(barrier, inc=1, device_id=device, device_id_type=MESH)
    for i in range(2):

        @pl.when(jnp.logical_not(stays[i]))
        def _():
            pl.semaphore_signal(barrier, inc=1, device_id=givers[i], device_id_type=MESH)

    pl.semaphore_wait(barrier, 9 - jnp.where(stays[0], 1, 0) - jnp.where(stays[1], 1, 0))

    def post(source, target, sems, device):
        sent.append(send(source, target, sems, device))

    lane = lax.broadcasted_iota(jnp.int32, (length, HEAD_SIZE), 1)
    in_front = lane < HEAD_SIZE // 2
    is_lower = jnp.full((length, HEAD_SIZE), core) == 0
    kv_send[...] = proj[:, q_width:].astype(BF16)
    post(kv_send, kv_recv, (kv_sems.at[0], kv_sems.at[1]), twin)
    seg_col = jnp.transpose(jnp.broadcast_to(seg_row[...].astype(F32), (HEAD_SIZE, length)))[:, :1]
    seg_cols[...] = jnp.broadcast_to(seg_col, seg_cols.shape)

    @pl.loop(0, 2)
    def _(step):
        start = pl.multiple_of(step * tile, tile)
        part = pl.ds(start, tile)
        row = lax.broadcasted_iota(jnp.int32, (tile, length), 0) + start
        key = lax.broadcasted_iota(jnp.int32, (tile, length), 1)
        allowed = (key <= row) & (seg_cols[part, :1] == seg_row[...].astype(F32))
        bias[part, :] = jnp.where(allowed, 0.0, -jnp.inf)

    @pl.loop(0, q_width // HEAD_SIZE)
    def _(head):
        cols = pl.ds(pl.multiple_of(head * HEAD_SIZE, HEAD_SIZE), HEAD_SIZE)
        query = proj[:, cols]
        q_rot[:, cols] = (query * cosine[...] + swap_halves(query) * sine[...]).astype(BF16)

    arrived(kv_recv, kv_sems.at[1])
    own, other = kv_send[...].astype(F32), kv_recv[...].astype(F32)
    lower, upper = jnp.where(is_lower, own, other), jnp.where(is_lower, other, own)
    key = jnp.where(in_front, lower, swap_halves(upper))
    keys[...] = (key * cosine[...] + swap_halves(key) * sine[...]).astype(BF16)
    values[...] = jnp.where(in_front, swap_halves(lower), upper).astype(BF16)

    @pl.loop(0, q_width // HEAD_SIZE)
    def _(head):
        cols = pl.ds(pl.multiple_of(head * HEAD_SIZE, HEAD_SIZE), HEAD_SIZE)

        @pl.loop(0, 2)
        def _(step):
            part = pl.ds(pl.multiple_of(step * tile, tile), tile)
            scores = nt(q_rot[part, cols], keys[...]) * score_scale + bias[part, :]
            raised = jnp.exp(scores - jnp.max(scores, axis=1, keepdims=True))
            prob = raised / jnp.sum(raised, axis=1, keepdims=True)
            probs[head, part, :] = prob
            mixed_values = jnp.dot(prob.astype(BF16), values[...], preferred_element_type=F32)
            attn_all[0, part, cols] = mixed_values.astype(BF16)

    rings = (attn_all, grad_all)

    def hop(i, k, source, target, device):
        ring = rings[i]
        post(ring.at[source], ring.at[target], (ring_s.at[i, k], ring_r.at[i, k]), device)

    def ring_wait(i, k, target):
        arrived(rings[i].at[target], ring_r.at[i, k])

    def ring_across(i):
        hop(i, 0, 0, 4, across)

    def ring_start(i):
        hop(i, 1, 0, 1, right)
        hop(i, 2, 0, 3, left)

    def ring_side(i):
        ring_wait(i, 0, 4)
        hop(i, 3, 4, 5, right)
        hop(i, 4, 4, 7, left)

    def ring_pass(i):
        ring_wait(i, 1, 1)
        hop(i, 5, 1, 2, right)

    def ring_back(i):
        ring_wait(i, 4, 7)
        hop(i, 6, 7, 6, left)

    def ring_end(i):
        for k, target in ((2, 3), (3, 5), (5, 2), (6, 6)):
            ring_wait(i, k, target)

    ring_across(0)
    ring_start(0)

    key_sum[...] = jnp.zeros_like(key_sum)
    value_sum[...] = jnp.zeros_like(value_sum)

    @pl.loop(0, q_width // HEAD_SIZE)
    def _(head):
        cols = pl.ds(pl.multiple_of(head * HEAD_SIZE, HEAD_SIZE), HEAD_SIZE)

        @pl.loop(0, 2)
        def _(step):
            part = pl.ds(pl.multiple_of(step * tile, tile), tile)
            d_out = d_attn[part, cols]
            prob = probs[head, part, :]
            d_prob = nt(d_out, values[...])
            row_delta = jnp.sum(prob * d_prob, axis=1, keepdims=True)
            d_score = (prob * (d_prob - row_delta) * score_scale).astype(BF16)
            d_query = jnp.dot(d_score, keys[...], preferred_element_type=F32)
            d_query = d_query * cosine[part, :] - swap_halves(d_query) * sine[part, :]
            grad_all[0, part, cols] = d_query.astype(BF16)
            key_sum[...] += tn(d_score, q_rot[part, cols])
            value_sum[...] += tn(prob.astype(BF16), d_out)

    d_key = key_sum[...] * cosine[...] - swap_halves(key_sum[...]) * sine[...]
    d_key, d_value = d_key.astype(BF16).astype(F32), value_sum[...].astype(BF16).astype(F32)
    lower = jnp.where(in_front, d_key, swap_halves(d_value))
    upper = jnp.where(in_front, swap_halves(d_key), d_value)
    kv_grad_send[...] = jnp.where(is_lower, upper, lower).astype(BF16)
    post(kv_grad_send, kv_grad_recv, (kv_sems.at[2], kv_sems.at[3]), twin)
    own = jnp.where(is_lower, lower, upper)
    arrived(kv_grad_recv, kv_sems.at[3])
    grad_all[0, :, q_width:] = (own + kv_grad_recv[...].astype(F32)).astype(BF16)

    weights = (o_weight, in_weight)
    half = o_weight.shape[0] // 2

    def spot(dz, side):
        return (z + dz + 4) % 4 * 2 + side

    def term(i, dz, side, which, part):
        rows = pl.ds(pl.multiple_of(which * half, half), half)
        return nt(rings[i][spot(dz, side), part, :], weights[i][rows, :])

    def give_half(i):
        for q, dz in enumerate(LEVELS):
            if i:
                halves[q].wait_send()
            for side in range(2):

                @pl.loop(0, 2)
                def _(step):
                    part = pl.ds(pl.multiple_of(step * tile, tile), tile)
                    half_send[q, side, part, :] = term(i, dz, side, 1 - core, part).astype(BF16)

            sems = (half_s.at[i, q], half_r.at[i, q])
            halves.append(send(half_send.at[q], half_recv.at[i, q], sems, twin))

    def half_wait(i, q):
        arrived(half_recv.at[i, q], half_r.at[i, q])

    def add_up(i, q, side, target, first, count, terms):
        part = pl.ds(first, count)
        total = term(i, LEVELS[q], side, core, part)
        total = total + half_recv[i, q, side, part, :].astype(F32)
        for ref in terms:
            total = total + ref[...].astype(F32)
        target[...] = total.astype(target.dtype)

    few = tile // 2

    def level_hop(i, k, slot, device):
        sems = (level_s.at[i, k], level_r.at[i, slot])
        post(level_send.at[i, k], level_recv.at[i, slot], sems, device)

    def level_wait(i, slot):
        arrived(level_recv.at[i, slot], level_r.at[i, slot])

    def cross(i, q):
        add_up(i, q, 1 - low, cross_send.at[i, q], tile, tile, ())
        post(cross_send.at[i, q], cross_recv.at[i, q], (cross_s.at[i, q], cross_r.at[i, q]), beside)

    def cross_wait(i, q):
        arrived(cross_recv.at[i, q], cross_r.at[i, q])

    def slab(ref, which):
        return ref.at[pl.ds(which * few, few)]

    def far_level(i):
        half_wait(i, 0)
        cross(i, 0)
        add_up(i, 0, 0, level_send.at[i, 0], 0, tile, ())
        level_hop(i, 0, 0, below)
        add_up(i, 0, 1, level_send.at[i, 1], 0, tile, ())
        level_hop(i, 1, 1, above)

    def near_level(i):
        half_wait(i, 1)
        cross(i, 1)
        add_up(i, 1, 1, level_send.at[i, 2], 0, tile, ())
        level_hop(i, 2, 3, below)
        half_wait(i, 2)
        cross(i, 2)
        add_up(i, 2, 0, level_send.at[i, 3], 0, tile, ())
        level_hop(i, 3, 4, above)
        half_wait(i, 3)
        cross(i, 3)

    def far_plane(i):
        cross_wait(i, 0)
        add_up(i, 0, low, plane_send.at[i, 0], tile, tile, (cross_recv.at[i, 0],))
        for which, k, device in ((0, 0, below), (1, 3, above)):
            sems = (plane_s.at[i, k], plane_r.at[i, k])
            post(slab(plane_send.at[i, 0], which), slab(plane_recv.at[i, 0], which), sems, device)

    def pass_level(i):
        level_wait(i, 0)
        add_up(i, 1, 0, level_send.at[i, 4], 0, tile, (level_recv.at[i, 0],))
        level_hop(i, 4, 2, below)
        level_wait(i, 1)
        add_up(i, 2, 1, level_send.at[i, 5], 0, tile, (level_recv.at[i, 1],))
        level_hop(i, 5, 5, above)

    def pass_plane(i):
        for q, joins, k, device in ((1, 0, 0, below), (2, 1, 3, above)):
            cross_wait(i, q)
            arrived(slab(plane_recv.at[i, 0], joins), plane_r.at[i, k])
            for which in range(2):
                terms = [slab(cross_recv.at[i, q], which)]
                if which == joins:
                    terms.append(slab(plane_recv.at[i, 0], which))
                add_up(i, q, low, slab(plane_send.at[i, q], which), tile + which * few, few, terms)
            sems = (plane_s.at[i, q], plane_r.at[i, q])
            post(plane_send.at[i, q], plane_recv.at[i, q], sems, device)

    def own_level(i):
        for slot in range(2, 6):
            level_wait(i, slot)
        terms = (level_recv.at[i, 2 + 1 - low], level_recv.at[i, 4 + 1 - low])
        add_up(i, 3, 1 - low, side_send.at[i], 0, tile, terms)
        post(side_send.at[i], side_recv.at[i], (side_sems.at[i, 0], side_sems.at[i, 1]), beside)

    tp_width = half

    def columns(t):
        return mixed.at[:, pl.ds(pl.multiple_of(t * tp_width, tp_width), tp_width)]

    def tp_at(dz, dl, dc=0):
        level, side = (z + dz + 4) % 4, (low + dl) % 2
        owner = (h + level // 2) % 2 * 4 + (x + level % 2 * 2 + side) % 4
        return owner * 2 + (core + dc) % 2

    def last_target(i):
        return columns(tp_at(0, 0)) if i == 0 else last_recv

    def last_level(i):
        cross_wait(i, 3)
        for q in (1, 2):
            arrived(plane_recv.at[i, q], plane_r.at[i, q])
        terms = (cross_recv.at[i, 3], plane_recv.at[i, 1], plane_recv.at[i, 2])
        add_up(i, 3, low, last_send.at[i, pl.ds(tile, tile)], tile, tile, terms)
        arrived(side_recv.at[i], side_sems.at[i, 1])
        terms = (level_recv.at[i, 2 + low], level_recv.at[i, 4 + low], side_recv.at[i])
        add_up(i, 3, low, last_send.at[i, pl.ds(0, tile)], 0, tile, terms)
        there = columns(blk * 2 + core) if i == 0 else last_recv

        @pl.when(jnp.logical_not(stays[i]))
        def _():
            send(last_send.at[i], there, (hand_s.at[i], hand_r.at[i]), homes[i])

        @pl.when(stays[i])
        def _():
            pltpu.make_async_copy(last_send.at[i], last_target(i), hand_r.at[i]).start()

    def hand_end(i):
        arrived(last_target(i), hand_r.at[i])

    def hand_sent(i):
        @pl.when(jnp.logical_not(stays[i]))
        def _():
            arrived(last_send.at[i], hand_s.at[i])

    whole, top, bottom = (0, length), (0, tile), (tile, tile)
    quarters = ((tile, tile // 2), (tile + tile // 2, tile // 2))

    def cell(t, rows):
        return columns(t).at[pl.ds(*rows)]

    def mixed_hop(k, t, rows, device):
        post(cell(t, rows), cell(t, rows), (mixed_s.at[k], mixed_r.at[k]), device)

    def mixed_wait(k, t, rows):
        arrived(cell(t, rows), mixed_r.at[k])

    given = []

    def mixed_twin(dz, dl, rows):
        k, t = len(given), tp_at(dz, dl)
        given.append((tp_at(dz, dl, 1), rows))
        post(cell(t, rows), cell(t, rows), (twin_s.at[k], twin_r.at[k]), twin)

    def mixed_start():
        hand_end(0)
        mixed_hop(0, tp_at(0, 0), top, beside)
        mixed_hop(7, tp_at(0, 0), bottom, above)
        mixed_hop(8, tp_at(0, 0), bottom, below)
        mixed_hop(1, tp_at(0, 0), top, above)
        mixed_hop(2, tp_at(0, 0), top, below)
        mixed_hop(11, tp_at(0, 0), bottom, beside)
        mixed_twin(0, 0, whole)

    def mixed_side():
        mixed_wait(0, tp_at(0, 1), top)
        mixed_hop(3, tp_at(0, 1), top, above)
        mixed_hop(4, tp_at(0, 1), top, below)
        mixed_twin(0, 1, top)

    def mixed_bottom():
        mixed_wait(7, tp_at(-1, 0), bottom)
        mixed_hop(9, tp_at(-1, 0), quarters[0], above)
        mixed_hop(12, tp_at(-1, 0), bottom, beside)
        mixed_twin(-1, 0, bottom)
        mixed_wait(8, tp_at(1, 0), bottom)
        mixed_hop(10, tp_at(1, 0), quarters[1], below)
        mixed_hop(13, tp_at(1, 0), bottom, beside)
        mixed_twin(1, 0, bottom)

    def mixed_pass():
        mixed_wait(1, tp_at(-1, 0), top)
        mixed_hop(5, tp_at(-1, 0), top, above)
        mixed_twin(-1, 0, top)
        mixed_wait(2, tp_at(1, 0), top)
        mixed_twin(1, 0, top)

    def mixed_back():
        mixed_wait(4, tp_at(1, 1), top)
        mixed_hop(6, tp_at(1, 1), top, below)
        mixed_twin(1, 1, top)

    def mixed_far():
        mixed_wait(9, tp_at(2, 0), quarters[0])
        mixed_wait(10, tp_at(2, 0), quarters[1])
        mixed_hop(14, tp_at(2, 0), bottom, beside)
        mixed_twin(2, 0, bottom)
        mixed_wait(11, tp_at(0, 1), bottom)
        mixed_twin(0, 1, bottom)
        mixed_wait(12, tp_at(-1, 1), bottom)
        mixed_twin(-1, 1, bottom)
        mixed_wait(13, tp_at(1, 1), bottom)
        mixed_twin(1, 1, bottom)

    def mixed_end():
        for k, dz, dl, rows in ((3, -1, 1, top), (5, 2, 0, top), (6, 2, 1, top), (14, 2, 1, bottom)):
            mixed_wait(k, tp_at(dz, dl), rows)
            mixed_twin(dz, dl, rows)
        for k, (t, rows) in enumerate(given):
            arrived(cell(t, rows), twin_r.at[k])

    sources = (cot_blocks, token_blocks)
    order = (0, 4, 1, 3, 5, 7, 2, 6)
    steps = [(i, j) for i in range(2) for j in order]

    def load(n):
        i, j = steps[n]
        pltpu.make_async_copy(sources[i].at[j], column.at[n % 2], column_sem.at[n % 2]).start()

    def grad_step(n):
        i, j = steps[n]
        slot = n % 2
        arrived(column.at[slot], column_sem.at[slot])
        width = rings[i].shape[2]
        strip = 256

        @pl.loop(0, column.shape[2] // strip)
        def _(step):
            part = pl.ds(pl.multiple_of(step * strip, strip), strip)
            value = tn(column[slot, :, part], rings[i][j])
            if n % 8:
                value = value + grad_sum[part, :width]
            if n % 8 < 7:
                grad_sum[part, :width] = value
            elif i == 0:
                o_grad[part, :] = value.astype(BF16)
            else:
                q_grad[part, :] = value[:, :q_width].astype(BF16)
                kv_grad[part, :] = value[:, q_width:].astype(BF16)

        if n + 2 < len(steps):
            load(n + 2)

    load(0)
    load(1)
    ring_across(1)
    grad_step(0)
    ring_side(0)
    grad_step(1)
    ring_pass(0)
    grad_step(2)
    ring_back(0)
    ring_start(1)
    ring_side(1)
    ring_end(0)
    for held in loads:
        held.wait()
    give_half(0)
    far_level(0)
    near_level(0)
    ring_pass(1)
    far_plane(0)
    pass_level(0)
    grad_step(3)
    grad_step(4)
    pass_plane(0)
    grad_step(5)
    ring_back(1)
    own_level(0)
    grad_step(6)
    grad_step(7)
    last_level(0)
    ring_end(1)
    give_half(1)
    far_level(1)
    near_level(1)
    far_plane(1)
    pass_level(1)
    mixed_start()
    grad_step(8)
    grad_step(9)
    pass_plane(1)
    grad_step(10)
    mixed_side()
    grad_step(11)
    own_level(1)
    mixed_bottom()
    grad_step(12)
    mixed_pass()
    grad_step(13)
    grad_step(14)
    grad_step(15)
    last_level(1)
    mixed_far()
    mixed_back()
    mixed_end()
    hand_end(1)
    out = pltpu.make_async_copy(last_recv, d_tokens, out_sem)
    out.start()
    for copy in sent + halves[4:]:
        copy.wait_send()
    hand_sent(0)
    hand_sent(1)
    out.wait()


def finish(proj, d_attn, cosine, sine, segments, weights, blocks):
    length, q_width = d_attn.shape
    in_width = proj.shape[1]
    depth = weights[0].shape[0]
    half = depth // 2
    heads = q_width // HEAD_SIZE
    dma = pltpu.SemaphoreType.DMA
    vmem = pl.BlockSpec(memory_space=pltpu.VMEM)
    hbm = pl.BlockSpec(memory_space=pl.ANY)
    part = pltpu.VMEM((length, HEAD_SIZE), BF16)
    part_sum = pltpu.VMEM((length, HEAD_SIZE), F32)
    return pl.pallas_call(
        finish_kernel,
        out_shape=(
            jax.ShapeDtypeStruct((length, 16 * half), BF16),
            jax.ShapeDtypeStruct((length, half), BF16),
            jax.ShapeDtypeStruct((depth, q_width), BF16),
            jax.ShapeDtypeStruct((depth, in_width - q_width), BF16),
            jax.ShapeDtypeStruct((depth, q_width), BF16),
        ),
        in_specs=[vmem] * 5 + [hbm] * 5,
        out_specs=(hbm, hbm, vmem, vmem, vmem),
        scratch_shapes=[
            pltpu.VMEM((depth, in_width), BF16),
            pltpu.VMEM((depth, q_width), BF16),
            dma((3,)),
            pltpu.VMEM((8, length, q_width), BF16),
            pltpu.VMEM((8, length, in_width), BF16),
            pltpu.VMEM((length, q_width), BF16),
            pltpu.VMEM((heads, length, length), F32),
            pltpu.VMEM((length, length), F32),
            pltpu.VMEM((length, HEAD_SIZE), F32),
            part,
            part,
            part,
            part,
            part_sum,
            part_sum,
            part,
            part,
            pltpu.VMEM((4, 2, length, half), BF16),
            pltpu.VMEM((2, 4, 2, length, half), BF16),
            pltpu.VMEM((2, 6, length // 2, half), BF16),
            pltpu.VMEM((2, 6, length // 2, half), BF16),
            pltpu.VMEM((2, length // 2, half), BF16),
            pltpu.VMEM((2, length // 2, half), BF16),
            pltpu.VMEM((2, 4, length // 2, half), BF16),
            pltpu.VMEM((2, 4, length // 2, half), BF16),
            pltpu.VMEM((2, 3, length // 2, half), BF16),
            pltpu.VMEM((2, 3, length // 2, half), BF16),
            pltpu.VMEM((2, length, half), BF16),
            pltpu.VMEM((length, half), BF16),
            pltpu.VMEM((2, length, depth), BF16),
            pltpu.VMEM((depth, in_width), F32),
            dma((4,)),
            dma((2, 7)),
            dma((2, 7)),
            dma((2, 4)),
            dma((2, 4)),
            dma((2, 6)),
            dma((2, 6)),
            dma((2, 2)),
            dma((2, 4)),
            dma((2, 4)),
            dma((2, 4)),
            dma((2, 4)),
            dma((2,)),
            dma((2,)),
            dma((15,)),
            dma((15,)),
            dma((15,)),
            dma((15,)),
            dma((2,)),
            dma,
        ],
        compiler_params=pltpu.CompilerParams(
            collective_id=1, has_side_effects=True, vmem_limit_bytes=63 * MIB
        ),
        name="finish",
    )(
        proj, d_attn, cosine, sine, segments, *weights, *blocks
    )


def shards(tokens, segment_ids, q_weight, key_value_weight, o_weight, cotangent):
    weights = (q_weight, key_value_weight, o_weight)
    token_blocks, cot_blocks, proj, d_attn = project(tokens, cotangent, *weights)
    cosine, sine = rope_tables(tokens.shape[0], HEAD_SIZE)
    cosine = jnp.concatenate([cosine, cosine], axis=1)
    sine = jnp.concatenate([-sine, sine], axis=1)
    blocks = (token_blocks, cot_blocks)
    return finish(proj, d_attn, cosine, sine, segment_ids, weights, blocks)


def solution(mesh):
    in_specs = (
        P("blk", None),
        P("blk", None),
        P("blk", "tp"),
        P("blk", "tp"),
        P("blk", "tp"),
        P("blk", None),
    )
    out_specs = (P("blk", None), P("blk", "tp"), P("blk", "tp"), P("blk", "tp"), P("blk", "tp"))
    return jax.shard_map(shards, mesh=mesh, in_specs=in_specs, out_specs=out_specs, check_vma=False)
```

```python
import math

import jax
import jax.numpy as jnp
from jax import lax
from jax.experimental import pallas as pl
from jax.experimental.pallas import tpu as pltpu
from jax.sharding import PartitionSpec as P

HEAD_SIZE = 128


THETA = 10000.0


def rope_tables(length, width):
    half_width = width // 2
    position = jnp.arange(length, dtype=jnp.float32)[:, None]
    channel = jnp.arange(half_width, dtype=jnp.float32)[None, :]
    angle = position * jnp.power(THETA, -2.0 * channel / width)
    return (jnp.cos(angle), jnp.sin(angle))


MESH = pl.DeviceIdType.MESH
BF16 = jnp.bfloat16
F32 = jnp.float32
MIB = 1 << 20


def here():
    blk, tp = lax.axis_index("blk"), lax.axis_index("tp")
    return blk // 4, blk % 4, tp // 4, tp // 2 % 2, tp % 2


def near(place, dh=0, dx=0, dz=0, dl=0, dc=0):
    h, x, z, low, core = place
    h, low, core = (h + dh) % 2, (low + dl) % 2, (core + dc) % 2
    x, z = (x + dx + 4) % 4, (z + dz + 4) % 4
    return h * 4 + x, z * 4 + low * 2 + core


def greet(devices):
    barrier = pltpu.get_barrier_semaphore()
    for device in devices:
        pl.semaphore_signal(barrier, inc=1, device_id=device, device_id_type=MESH)
    pl.semaphore_wait(barrier, len(devices))


def send(source, target, sems, device):
    copy = pltpu.make_async_remote_copy(
        src_ref=source,
        dst_ref=target,
        send_sem=sems[0],
        recv_sem=sems[1],
        device_id=device,
        device_id_type=MESH,
    )
    copy.start()
    return copy


def arrived(ref, sem):
    pltpu.make_async_copy(ref, ref, sem).wait()


def load_weights(q_weight, kv_weight, o_source, in_weight, o_weight, sems):
    width = q_weight.shape[1]
    kv_part = pl.ds(width, kv_weight.shape[1])
    loads = [
        pltpu.make_async_copy(q_weight, in_weight.at[:, pl.ds(0, width)], sems.at[0]),
        pltpu.make_async_copy(kv_weight, in_weight.at[:, kv_part], sems.at[1]),
        pltpu.make_async_copy(o_source, o_weight, sems.at[2]),
    ]
    for held in loads:
        held.start()
    return loads


CHUNKS = ((0, 2), (1, 2), (1, 1), (0, 3), (0, 1), (1, 3), (1, 0), (0, 0))


def project_kernel(
    tokens, cot, q_weight, kv_weight, o_source, token_out, cot_out, proj_out, d_attn_out,
    in_weight, o_weight, weight_sem, blocks, proj_send, proj_recv, cot_send, cot_recv,
    a2a_s, a2a_r, up_s, up_r, down_s, down_r, far_s, far_r, core_s, core_r, sum_s, sum_r, keep,
):
    place = here()
    h, x, z, low, core = place
    seat = z * 2 + core
    height = blocks.shape[2] // 8
    width = blocks.shape[3]
    right, left = near(place, dx=1), near(place, dx=-1)
    above, below = near(place, dz=1), near(place, dz=-1)
    twin, across = near(place, dc=1), near(place, dh=1)
    shifts = [shift for shift in CHUNKS if shift != (0, 0)]
    loads = load_weights(q_weight, kv_weight, o_source, in_weight, o_weight, weight_sem)
    greet([near(place, dh=dh, dx=dx) for dh, dx in shifts] + [above, below, twin])
    sent = []

    def rows(a, dh, dx, at):
        return blocks.at[a, dh * 4 + dx, pl.ds(pl.multiple_of(at * height, height), height)]

    def level(dz):
        return (z + dz + 4) % 4 * 2 + core

    def index(dh, dx):
        return dh * 4 + dx

    def start_blocks(a, source):
        for dh, dx in CHUNKS:
            target = near(place, dh=dh, dx=dx)
            piece = source.at[
                pl.ds(pl.multiple_of(seat * height, height), height),
                pl.ds(pl.multiple_of(target[0] * width, width), width),
            ]
            j = index(dh, dx)
            if j:
                sent.append(send(piece, rows(a, dh, dx, seat), (a2a_s.at[a, j], a2a_r.at[a, j]), target))
            else:
                pltpu.make_async_copy(piece, rows(a, 0, 0, seat), a2a_r.at[a, 0]).start()

    def to_twin(a, dh, dx, which, at):
        j = index(dh, dx)
        piece = rows(a, dh, dx, at)
        sent.append(send(piece, piece, (core_s.at[a, j, which], core_r.at[a, j, which]), twin))

    def first_stage(a, dh, dx):
        j = index(dh, dx)
        piece = rows(a, dh, dx, seat)
        arrived(piece, a2a_r.at[a, j])
        sent.append(send(piece, piece, (up_s.at[a, j], up_r.at[a, j]), above))
        sent.append(send(piece, piece, (down_s.at[a, j], down_r.at[a, j]), below))
        to_twin(a, dh, dx, 0, seat)

    def second_stage(a, dh, dx):
        j = index(dh, dx)
        sems = (far_s.at[a, j], far_r.at[a, j])
        lower, upper = rows(a, dh, dx, level(-1)), rows(a, dh, dx, level(1))
        arrived(lower, up_r.at[a, j])
        if dh == 0:
            sent.append(send(lower, lower, sems, above))
        to_twin(a, dh, dx, 1, level(-1))
        arrived(upper, down_r.at[a, j])
        if dh == 1:
            sent.append(send(upper, upper, sems, below))
        to_twin(a, dh, dx, 2, level(1))

    def third_stage(a, dh, dx):
        j = index(dh, dx)
        arrived(rows(a, dh, dx, level(2)), far_r.at[a, j])
        to_twin(a, dh, dx, 3, level(2))

    def complete(a, dh, dx):
        j = index(dh, dx)
        for which, dz in enumerate((0, -1, 1, 2)):
            seat_there = (z + dz + 4) % 4 * 2 + (1 - core)
            arrived(rows(a, dh, dx, seat_there), core_r.at[a, j, which])

    weights = (in_weight, o_weight)
    outgoing = (proj_send, cot_send)
    incoming = (proj_recv, cot_recv)
    results = (proj_out, d_attn_out)
    adds = {4: (0,), 5: (1,), 6: (2, 5), 7: (3, 4, 6)}
    ways = (left, right, left, right, left, right, across)

    def chunk(a, k):
        dh, dx = CHUNKS[k]
        j = index(dh, dx)
        complete(a, dh, dx)
        terms = adds.get(k, ())
        for term in terms:
            arrived(incoming[a].at[term], sum_r.at[a, term])
        target = outgoing[a].at[k] if k < 7 else results[a]
        tile = blocks.shape[2] // 2

        @pl.loop(0, 2)
        def _(step):
            part = pl.ds(pl.multiple_of(step * tile, tile), tile)
            total = jnp.dot(blocks[a, j, part, :], weights[a][...], preferred_element_type=F32)
            for term in terms:
                total = total + incoming[a][term, part, :].astype(F32)
            target[part, :] = total.astype(target.dtype)

        if k < 7:
            sent.append(send(target, incoming[a].at[k], (sum_s.at[a, k], sum_r.at[a, k]), ways[k]))

    start_blocks(0, tokens)
    start_blocks(1, cot)
    pieces = [(a, k) for a in range(2) for k in range(8)]
    waiting = [(0, 0), (0, 1), (0, 2), (0, 3), (0, 4), (0, 5), (0, 6), (1, 0), (1, 1), (1, 2), (1, 3)]
    waiting += [(0, 7), (1, 4), (1, 5), (1, 6), (1, 7)]
    late = {(0, 6): 7, (0, 7): 9}
    for step in range(len(pieces) + 5):
        for stage, lag in ((first_stage, 0), (second_stage, 2), (third_stage, 4)):
            if 0 <= step - lag < len(pieces):
                a, k = pieces[step - lag]
                stage(a, *CHUNKS[k])
        if step == 4:
            for held in loads:
                held.wait()
        while waiting and pieces.index(waiting[0]) + late.get(waiting[0], 5) <= step:
            chunk(*waiting.pop(0))
    assert not waiting
    keeps = [
        pltpu.make_async_copy(blocks.at[0], token_out, keep.at[0]),
        pltpu.make_async_copy(blocks.at[1], cot_out, keep.at[1]),
    ]
    for copy in keeps:
        copy.start()
    for copy in sent:
        copy.wait_send()
    for copy in keeps:
        copy.wait()


def project(tokens, cot, q_weight, kv_weight, o_weight):
    length = tokens.shape[0]
    width = tokens.shape[1] // 8
    in_width, o_width = q_weight.shape[1] + kv_weight.shape[1], o_weight.shape[1]
    depth = q_weight.shape[0]
    dma = pltpu.SemaphoreType.DMA
    pair = [dma((2, 8)), dma((2, 8))]
    block = jax.ShapeDtypeStruct((8, length, width), BF16)
    return pl.pallas_call(
        project_kernel,
        out_shape=(
            block,
            block,
            jax.ShapeDtypeStruct((length, in_width), F32),
            jax.ShapeDtypeStruct((length, o_width), BF16),
        ),
        in_specs=[pl.BlockSpec(memory_space=pl.ANY)] * 5,
        out_specs=(pl.BlockSpec(memory_space=pl.ANY),) * 2
        + (pl.BlockSpec(memory_space=pltpu.VMEM),) * 2,
        scratch_shapes=[
            pltpu.VMEM((depth, in_width), BF16),
            pltpu.VMEM((depth, o_width), BF16),
            dma((3,)),
            pltpu.VMEM((2, 8, length, width), BF16),
            pltpu.VMEM((7, length, in_width), BF16),
            pltpu.VMEM((7, length, in_width), BF16),
            pltpu.VMEM((7, length, o_width), BF16),
            pltpu.VMEM((7, length, o_width), BF16),
            *pair,
            *pair,
            *pair,
            *pair,
            dma((2, 8, 4)),
            dma((2, 8, 4)),
            dma((2, 7)),
            dma((2, 7)),
            dma((2,)),
        ],
        compiler_params=pltpu.CompilerParams(
            collective_id=0, has_side_effects=True, vmem_limit_bytes=56 * MIB
        ),
        name="project",
    )(tokens, cot, q_weight, kv_weight, o_weight)


def nt(left, right):
    return lax.dot_general(left, right, (((1,), (1,)), ((), ())), preferred_element_type=F32)


def tn(left, right):
    return lax.dot_general(left, right, (((0,), (0,)), ((), ())), preferred_element_type=F32)


def swap_halves(array):
    return pltpu.roll(array, array.shape[1] // 2, 1)


LEVELS = (2, -1, 1, 0)


def finish_kernel(
    proj, d_attn, cosine, sine, seg_row, q_weight, kv_weight, o_source, token_blocks, cot_blocks,
    mixed, d_tokens, q_grad, kv_grad, o_grad, in_weight, o_weight, weight_sem,
    attn_all, grad_all, q_rot, probs, bias, seg_cols, keys, values, kv_send, kv_recv, key_sum, value_sum,
    kv_grad_send, kv_grad_recv,
    half_send, half_recv, level_send, level_recv, side_send, side_recv, cross_send, cross_recv,
    plane_send, plane_recv, last_send, last_recv,
    column, grad_sum,
    kv_sems, ring_s, ring_r, half_s, half_r, level_s, level_r, side_sems, cross_s, cross_r,
    plane_s, plane_r, hand_s, hand_r,
    mixed_s, mixed_r, twin_s, twin_r, column_sem, out_sem,
):
    place = here()
    h, x, z, low, core = place
    blk = h * 4 + x
    length, q_width = d_attn.shape
    tile = length // 2
    score_scale = 1.0 / math.sqrt(HEAD_SIZE)
    right, left = near(place, dx=1), near(place, dx=-1)
    above, below = near(place, dz=1), near(place, dz=-1)
    twin, across, beside = near(place, dc=1), near(place, dh=1), near(place, dl=1)
    halves = []
    far_h, far_x = z // 2, z % 2 * 2 + low
    origin = z * 2 + low
    origin_h, origin_x = (origin // 4 + h) % 2, (origin % 4 - x + 4) % 4
    homes = (
        near(place, dh=far_h, dx=-far_x),
        (near(place, dh=far_h, dx=-far_x)[0], blk * 2 + core),
    )
    givers = (
        near(place, dh=far_h, dx=far_x),
        (origin, (origin_h * 2 + origin_x // 2) * 4 + origin_x % 2 * 2 + core),
    )
    stays = (z * 2 + low == 0, z * 2 + low + blk == 0)
    sent, halves = [], []
    loads = load_weights(q_weight, kv_weight, o_source, in_weight, o_weight, weight_sem)

    barrier = pltpu.get_barrier_semaphore()
    for device in (right, left, above, below, twin, across, beside):
        pl.semaphore_signal(barrier, inc=1, device_id=device, device_id_type=MESH)
    for i in range(2):

        @pl.when(jnp.logical_not(stays[i]))
        def _():
            pl.semaphore_signal(barrier, inc=1, device_id=givers[i], device_id_type=MESH)

    pl.semaphore_wait(barrier, 9 - jnp.where(stays[0], 1, 0) - jnp.where(stays[1], 1, 0))

    def post(source, target, sems, device):
        sent.append(send(source, target, sems, device))

    lane = lax.broadcasted_iota(jnp.int32, (length, HEAD_SIZE), 1)
    in_front = lane < HEAD_SIZE // 2
    is_lower = jnp.full((length, HEAD_SIZE), core) == 0
    kv_send[...] = proj[:, q_width:].astype(BF16)
    post(kv_send, kv_recv, (kv_sems.at[0], kv_sems.at[1]), twin)
    seg_col = jnp.transpose(jnp.broadcast_to(seg_row[...].astype(F32), (HEAD_SIZE, length)))[:, :1]
    seg_cols[...] = jnp.broadcast_to(seg_col, seg_cols.shape)

    @pl.loop(0, 2)
    def _(step):
        start = pl.multiple_of(step * tile, tile)
        part = pl.ds(start, tile)
        row = lax.broadcasted_iota(jnp.int32, (tile, length), 0) + start
        key = lax.broadcasted_iota(jnp.int32, (tile, length), 1)
        allowed = (key <= row) & (seg_cols[part, :1] == seg_row[...].astype(F32))
        bias[part, :] = jnp.where(allowed, 0.0, -jnp.inf)

    @pl.loop(0, q_width // HEAD_SIZE)
    def _(head):
        cols = pl.ds(pl.multiple_of(head * HEAD_SIZE, HEAD_SIZE), HEAD_SIZE)
        query = proj[:, cols]
        q_rot[:, cols] = (query * cosine[...] + swap_halves(query) * sine[...]).astype(BF16)

    arrived(kv_recv, kv_sems.at[1])
    own, other = kv_send[...].astype(F32), kv_recv[...].astype(F32)
    lower, upper = jnp.where(is_lower, own, other), jnp.where(is_lower, other, own)
    key = jnp.where(in_front, lower, swap_halves(upper))
    keys[...] = (key * cosine[...] + swap_halves(key) * sine[...]).astype(BF16)
    values[...] = jnp.where(in_front, swap_halves(lower), upper).astype(BF16)

    @pl.loop(0, q_width // HEAD_SIZE)
    def _(head):
        cols = pl.ds(pl.multiple_of(head * HEAD_SIZE, HEAD_SIZE), HEAD_SIZE)

        @pl.loop(0, 2)
        def _(step):
            part = pl.ds(pl.multiple_of(step * tile, tile), tile)
            scores = nt(q_rot[part, cols], keys[...]) * score_scale + bias[part, :]
            raised = jnp.exp(scores - jnp.max(scores, axis=1, keepdims=True))
            prob = raised / jnp.sum(raised, axis=1, keepdims=True)
            probs[head, part, :] = prob
            mixed_values = jnp.dot(prob.astype(BF16), values[...], preferred_element_type=F32)
            attn_all[0, part, cols] = mixed_values.astype(BF16)

    rings = (attn_all, grad_all)

    def hop(i, k, source, target, device):
        ring = rings[i]
        post(ring.at[source], ring.at[target], (ring_s.at[i, k], ring_r.at[i, k]), device)

    def ring_wait(i, k, target):
        arrived(rings[i].at[target], ring_r.at[i, k])

    def ring_across(i):
        hop(i, 0, 0, 4, across)

    def ring_start(i):
        hop(i, 1, 0, 1, right)
        hop(i, 2, 0, 3, left)

    def ring_side(i):
        ring_wait(i, 0, 4)
        hop(i, 3, 4, 5, right)
        hop(i, 4, 4, 7, left)

    def ring_pass(i):
        ring_wait(i, 1, 1)
        hop(i, 5, 1, 2, right)

    def ring_back(i):
        ring_wait(i, 4, 7)
        hop(i, 6, 7, 6, left)

    def ring_end(i):
        for k, target in ((2, 3), (3, 5), (5, 2), (6, 6)):
            ring_wait(i, k, target)

    ring_across(0)
    ring_start(0)

    key_sum[...] = jnp.zeros_like(key_sum)
    value_sum[...] = jnp.zeros_like(value_sum)

    @pl.loop(0, q_width // HEAD_SIZE)
    def _(head):
        cols = pl.ds(pl.multiple_of(head * HEAD_SIZE, HEAD_SIZE), HEAD_SIZE)

        @pl.loop(0, 2)
        def _(step):
            part = pl.ds(pl.multiple_of(step * tile, tile), tile)
            d_out = d_attn[part, cols]
            prob = probs[head, part, :]
            d_prob = nt(d_out, values[...])
            row_delta = jnp.sum(prob * d_prob, axis=1, keepdims=True)
            d_score = (prob * (d_prob - row_delta) * score_scale).astype(BF16)
            d_query = jnp.dot(d_score, keys[...], preferred_element_type=F32)
            d_query = d_query * cosine[part, :] - swap_halves(d_query) * sine[part, :]
            grad_all[0, part, cols] = d_query.astype(BF16)
            key_sum[...] += tn(d_score, q_rot[part, cols])
            value_sum[...] += tn(prob.astype(BF16), d_out)

    d_key = key_sum[...] * cosine[...] - swap_halves(key_sum[...]) * sine[...]
    d_key, d_value = d_key.astype(BF16).astype(F32), value_sum[...].astype(BF16).astype(F32)
    lower = jnp.where(in_front, d_key, swap_halves(d_value))
    upper = jnp.where(in_front, swap_halves(d_key), d_value)
    kv_grad_send[...] = jnp.where(is_lower, upper, lower).astype(BF16)
    post(kv_grad_send, kv_grad_recv, (kv_sems.at[2], kv_sems.at[3]), twin)
    own = jnp.where(is_lower, lower, upper)
    arrived(kv_grad_recv, kv_sems.at[3])
    grad_all[0, :, q_width:] = (own + kv_grad_recv[...].astype(F32)).astype(BF16)

    weights = (o_weight, in_weight)
    half = o_weight.shape[0] // 2

    def spot(dz, side):
        return (z + dz + 4) % 4 * 2 + side

    def term(i, dz, side, which, part):
        rows = pl.ds(pl.multiple_of(which * half, half), half)
        return nt(rings[i][spot(dz, side), part, :], weights[i][rows, :])

    def give_half(i):
        for q, dz in enumerate(LEVELS):
            if i:
                halves[q].wait_send()
            for side in range(2):

                @pl.loop(0, 2)
                def _(step):
                    part = pl.ds(pl.multiple_of(step * tile, tile), tile)
                    half_send[q, side, part, :] = term(i, dz, side, 1 - core, part).astype(BF16)

            sems = (half_s.at[i, q], half_r.at[i, q])
            halves.append(send(half_send.at[q], half_recv.at[i, q], sems, twin))

    def half_wait(i, q):
        arrived(half_recv.at[i, q], half_r.at[i, q])

    def add_up(i, q, side, target, first, count, terms):
        part = pl.ds(first, count)
        total = term(i, LEVELS[q], side, core, part)
        total = total + half_recv[i, q, side, part, :].astype(F32)
        for ref in terms:
            total = total + ref[...].astype(F32)
        target[...] = total.astype(target.dtype)

    few = tile // 2

    def level_hop(i, k, slot, device):
        sems = (level_s.at[i, k], level_r.at[i, slot])
        post(level_send.at[i, k], level_recv.at[i, slot], sems, device)

    def level_wait(i, slot):
        arrived(level_recv.at[i, slot], level_r.at[i, slot])

    def cross(i, q):
        add_up(i, q, 1 - low, cross_send.at[i, q], tile, tile, ())
        post(cross_send.at[i, q], cross_recv.at[i, q], (cross_s.at[i, q], cross_r.at[i, q]), beside)

    def cross_wait(i, q):
        arrived(cross_recv.at[i, q], cross_r.at[i, q])

    def slab(ref, which):
        return ref.at[pl.ds(which * few, few)]

    def far_level(i):
        half_wait(i, 0)
        cross(i, 0)
        add_up(i, 0, 0, level_send.at[i, 0], 0, tile, ())
        level_hop(i, 0, 0, below)
        add_up(i, 0, 1, level_send.at[i, 1], 0, tile, ())
        level_hop(i, 1, 1, above)

    def near_level(i):
        half_wait(i, 1)
        cross(i, 1)
        add_up(i, 1, 1, level_send.at[i, 2], 0, tile, ())
        level_hop(i, 2, 3, below)
        half_wait(i, 2)
        cross(i, 2)
        add_up(i, 2, 0, level_send.at[i, 3], 0, tile, ())
        level_hop(i, 3, 4, above)
        half_wait(i, 3)
        cross(i, 3)

    def far_plane(i):
        cross_wait(i, 0)
        add_up(i, 0, low, plane_send.at[i, 0], tile, tile, (cross_recv.at[i, 0],))
        for which, k, device in ((0, 0, below), (1, 3, above)):
            sems = (plane_s.at[i, k], plane_r.at[i, k])
            post(slab(plane_send.at[i, 0], which), slab(plane_recv.at[i, 0], which), sems, device)

    def pass_level(i):
        level_wait(i, 0)
        add_up(i, 1, 0, level_send.at[i, 4], 0, tile, (level_recv.at[i, 0],))
        level_hop(i, 4, 2, below)
        level_wait(i, 1)
        add_up(i, 2, 1, level_send.at[i, 5], 0, tile, (level_recv.at[i, 1],))
        level_hop(i, 5, 5, above)

    def pass_plane(i):
        for q, joins, k, device in ((1, 0, 0, below), (2, 1, 3, above)):
            cross_wait(i, q)
            arrived(slab(plane_recv.at[i, 0], joins), plane_r.at[i, k])
            for which in range(2):
                terms = [slab(cross_recv.at[i, q], which)]
                if which == joins:
                    terms.append(slab(plane_recv.at[i, 0], which))
                add_up(i, q, low, slab(plane_send.at[i, q], which), tile + which * few, few, terms)
            sems = (plane_s.at[i, q], plane_r.at[i, q])
            post(plane_send.at[i, q], plane_recv.at[i, q], sems, device)

    def own_level(i):
        for slot in range(2, 6):
            level_wait(i, slot)
        terms = (level_recv.at[i, 2 + 1 - low], level_recv.at[i, 4 + 1 - low])
        add_up(i, 3, 1 - low, side_send.at[i], 0, tile, terms)
        post(side_send.at[i], side_recv.at[i], (side_sems.at[i, 0], side_sems.at[i, 1]), beside)

    tp_width = half

    def columns(t):
        return mixed.at[:, pl.ds(pl.multiple_of(t * tp_width, tp_width), tp_width)]

    def tp_at(dz, dl, dc=0):
        level, side = (z + dz + 4) % 4, (low + dl) % 2
        owner = (h + level // 2) % 2 * 4 + (x + level % 2 * 2 + side) % 4
        return owner * 2 + (core + dc) % 2

    def last_target(i):
        return columns(tp_at(0, 0)) if i == 0 else last_recv

    def last_level(i):
        cross_wait(i, 3)
        for q in (1, 2):
            arrived(plane_recv.at[i, q], plane_r.at[i, q])
        terms = (cross_recv.at[i, 3], plane_recv.at[i, 1], plane_recv.at[i, 2])
        add_up(i, 3, low, last_send.at[i, pl.ds(tile, tile)], tile, tile, terms)
        arrived(side_recv.at[i], side_sems.at[i, 1])
        terms = (level_recv.at[i, 2 + low], level_recv.at[i, 4 + low], side_recv.at[i])
        add_up(i, 3, low, last_send.at[i, pl.ds(0, tile)], 0, tile, terms)
        there = columns(blk * 2 + core) if i == 0 else last_recv

        @pl.when(jnp.logical_not(stays[i]))
        def _():
            send(last_send.at[i], there, (hand_s.at[i], hand_r.at[i]), homes[i])

        @pl.when(stays[i])
        def _():
            pltpu.make_async_copy(last_send.at[i], last_target(i), hand_r.at[i]).start()

    def hand_end(i):
        arrived(last_target(i), hand_r.at[i])

    def hand_sent(i):
        @pl.when(jnp.logical_not(stays[i]))
        def _():
            arrived(last_send.at[i], hand_s.at[i])

    whole, top, bottom = (0, length), (0, tile), (tile, tile)
    quarters = ((tile, tile // 2), (tile + tile // 2, tile // 2))

    def cell(t, rows):
        return columns(t).at[pl.ds(*rows)]

    def mixed_hop(k, t, rows, device):
        post(cell(t, rows), cell(t, rows), (mixed_s.at[k], mixed_r.at[k]), device)

    def mixed_wait(k, t, rows):
        arrived(cell(t, rows), mixed_r.at[k])

    given = []

    def mixed_twin(dz, dl, rows):
        k, t = len(given), tp_at(dz, dl)
        given.append((tp_at(dz, dl, 1), rows))
        post(cell(t, rows), cell(t, rows), (twin_s.at[k], twin_r.at[k]), twin)

    def mixed_start():
        hand_end(0)
        mixed_hop(0, tp_at(0, 0), top, beside)
        mixed_hop(7, tp_at(0, 0), bottom, above)
        mixed_hop(8, tp_at(0, 0), bottom, below)
        mixed_hop(1, tp_at(0, 0), top, above)
        mixed_hop(2, tp_at(0, 0), top, below)
        mixed_hop(11, tp_at(0, 0), bottom, beside)
        mixed_twin(0, 0, whole)

    def mixed_side():
        mixed_wait(0, tp_at(0, 1), top)
        mixed_hop(3, tp_at(0, 1), top, above)
        mixed_hop(4, tp_at(0, 1), top, below)
        mixed_twin(0, 1, top)

    def mixed_bottom():
        mixed_wait(7, tp_at(-1, 0), bottom)
        mixed_hop(9, tp_at(-1, 0), quarters[0], above)
        mixed_hop(12, tp_at(-1, 0), bottom, beside)
        mixed_twin(-1, 0, bottom)
        mixed_wait(8, tp_at(1, 0), bottom)
        mixed_hop(10, tp_at(1, 0), quarters[1], below)
        mixed_hop(13, tp_at(1, 0), bottom, beside)
        mixed_twin(1, 0, bottom)

    def mixed_pass():
        mixed_wait(1, tp_at(-1, 0), top)
        mixed_hop(5, tp_at(-1, 0), top, above)
        mixed_twin(-1, 0, top)
        mixed_wait(2, tp_at(1, 0), top)
        mixed_twin(1, 0, top)

    def mixed_back():
        mixed_wait(4, tp_at(1, 1), top)
        mixed_hop(6, tp_at(1, 1), top, below)
        mixed_twin(1, 1, top)

    def mixed_far():
        mixed_wait(9, tp_at(2, 0), quarters[0])
        mixed_wait(10, tp_at(2, 0), quarters[1])
        mixed_hop(14, tp_at(2, 0), bottom, beside)
        mixed_twin(2, 0, bottom)
        mixed_wait(11, tp_at(0, 1), bottom)
        mixed_twin(0, 1, bottom)
        mixed_wait(12, tp_at(-1, 1), bottom)
        mixed_twin(-1, 1, bottom)
        mixed_wait(13, tp_at(1, 1), bottom)
        mixed_twin(1, 1, bottom)

    def mixed_end():
        for k, dz, dl, rows in ((3, -1, 1, top), (5, 2, 0, top), (6, 2, 1, top), (14, 2, 1, bottom)):
            mixed_wait(k, tp_at(dz, dl), rows)
            mixed_twin(dz, dl, rows)
        for k, (t, rows) in enumerate(given):
            arrived(cell(t, rows), twin_r.at[k])

    sources = (cot_blocks, token_blocks)
    order = (0, 4, 1, 3, 5, 7, 2, 6)
    steps = [(i, j) for i in range(2) for j in order]

    def load(n):
        i, j = steps[n]
        pltpu.make_async_copy(sources[i].at[j], column.at[n % 2], column_sem.at[n % 2]).start()

    def grad_step(n):
        i, j = steps[n]
        slot = n % 2
        arrived(column.at[slot], column_sem.at[slot])
        width = rings[i].shape[2]
        strip = 256

        @pl.loop(0, column.shape[2] // strip)
        def _(step):
            part = pl.ds(pl.multiple_of(step * strip, strip), strip)
            value = tn(column[slot, :, part], rings[i][j])
            if n % 8:
                value = value + grad_sum[part, :width]
            if n % 8 < 7:
                grad_sum[part, :width] = value
            elif i == 0:
                o_grad[part, :] = value.astype(BF16)
            else:
                q_grad[part, :] = value[:, :q_width].astype(BF16)
                kv_grad[part, :] = value[:, q_width:].astype(BF16)

        if n + 2 < len(steps):
            load(n + 2)

    load(0)
    load(1)
    ring_across(1)
    grad_step(0)
    ring_side(0)
    grad_step(1)
    ring_pass(0)
    grad_step(2)
    ring_back(0)
    ring_start(1)
    ring_side(1)
    ring_end(0)
    for held in loads:
        held.wait()
    give_half(0)
    far_level(0)
    near_level(0)
    ring_pass(1)
    far_plane(0)
    pass_level(0)
    grad_step(3)
    grad_step(4)
    pass_plane(0)
    grad_step(5)
    ring_back(1)
    own_level(0)
    grad_step(6)
    grad_step(7)
    last_level(0)
    ring_end(1)
    give_half(1)
    far_level(1)
    near_level(1)
    far_plane(1)
    pass_level(1)
    mixed_start()
    grad_step(8)
    grad_step(9)
    pass_plane(1)
    grad_step(10)
    mixed_side()
    grad_step(11)
    own_level(1)
    mixed_bottom()
    grad_step(12)
    mixed_pass()
    grad_step(13)
    grad_step(14)
    grad_step(15)
    last_level(1)
    mixed_far()
    mixed_back()
    mixed_end()
    hand_end(1)
    out = pltpu.make_async_copy(last_recv, d_tokens, out_sem)
    out.start()
    for copy in sent + halves[4:]:
        copy.wait_send()
    hand_sent(0)
    hand_sent(1)
    out.wait()


def finish(proj, d_attn, cosine, sine, segments, weights, blocks):
    length, q_width = d_attn.shape
    in_width = proj.shape[1]
    depth = weights[0].shape[0]
    half = depth // 2
    heads = q_width // HEAD_SIZE
    dma = pltpu.SemaphoreType.DMA
    vmem = pl.BlockSpec(memory_space=pltpu.VMEM)
    hbm = pl.BlockSpec(memory_space=pl.ANY)
    part = pltpu.VMEM((length, HEAD_SIZE), BF16)
    part_sum = pltpu.VMEM((length, HEAD_SIZE), F32)
    return pl.pallas_call(
        finish_kernel,
        out_shape=(
            jax.ShapeDtypeStruct((length, 16 * half), BF16),
            jax.ShapeDtypeStruct((length, half), BF16),
            jax.ShapeDtypeStruct((depth, q_width), BF16),
            jax.ShapeDtypeStruct((depth, in_width - q_width), BF16),
            jax.ShapeDtypeStruct((depth, q_width), BF16),
        ),
        in_specs=[vmem] * 5 + [hbm] * 5,
        out_specs=(hbm, hbm, vmem, vmem, vmem),
        scratch_shapes=[
            pltpu.VMEM((depth, in_width), BF16),
            pltpu.VMEM((depth, q_width), BF16),
            dma((3,)),
            pltpu.VMEM((8, length, q_width), BF16),
            pltpu.VMEM((8, length, in_width), BF16),
            pltpu.VMEM((length, q_width), BF16),
            pltpu.VMEM((heads, length, length), F32),
            pltpu.VMEM((length, length), F32),
            pltpu.VMEM((length, HEAD_SIZE), F32),
            part,
            part,
            part,
            part,
            part_sum,
            part_sum,
            part,
            part,
            pltpu.VMEM((4, 2, length, half), BF16),
            pltpu.VMEM((2, 4, 2, length, half), BF16),
            pltpu.VMEM((2, 6, length // 2, half), BF16),
            pltpu.VMEM((2, 6, length // 2, half), BF16),
            pltpu.VMEM((2, length // 2, half), BF16),
            pltpu.VMEM((2, length // 2, half), BF16),
            pltpu.VMEM((2, 4, length // 2, half), BF16),
            pltpu.VMEM((2, 4, length // 2, half), BF16),
            pltpu.VMEM((2, 3, length // 2, half), BF16),
            pltpu.VMEM((2, 3, length // 2, half), BF16),
            pltpu.VMEM((2, length, half), BF16),
            pltpu.VMEM((length, half), BF16),
            pltpu.VMEM((2, length, depth), BF16),
            pltpu.VMEM((depth, in_width), F32),
            dma((4,)),
            dma((2, 7)),
            dma((2, 7)),
            dma((2, 4)),
            dma((2, 4)),
            dma((2, 6)),
            dma((2, 6)),
            dma((2, 2)),
            dma((2, 4)),
            dma((2, 4)),
            dma((2, 4)),
            dma((2, 4)),
            dma((2,)),
            dma((2,)),
            dma((15,)),
            dma((15,)),
            dma((15,)),
            dma((15,)),
            dma((2,)),
            dma,
        ],
        compiler_params=pltpu.CompilerParams(
            collective_id=1, has_side_effects=True, vmem_limit_bytes=63 * MIB
        ),
        name="finish",
    )(
        proj, d_attn, cosine, sine, segments, *weights, *blocks
    )


def settle_kernel(*refs):
    count = (len(refs) - 2) // 3
    sources, targets, buffers = refs[:count], refs[count : 2 * count], refs[2 * count : 3 * count]
    in_sems, out_sems = refs[-2:]
    parts = []
    for source, target, buffer in zip(sources, targets, buffers, strict=True):
        pieces = 16 if source.shape[1] > 1024 else 2
        rows = source.shape[0] // pieces
        for piece in range(pieces):
            part = pl.ds(piece * rows, rows)
            parts.append((source.at[part], buffer.at[part], target.at[part]))
    ins = [pltpu.make_async_copy(a, b, in_sems.at[n]) for n, (a, b, _) in enumerate(parts)]
    outs = [pltpu.make_async_copy(b, c, out_sems.at[n]) for n, (_, b, c) in enumerate(parts)]
    for copy in ins:
        copy.start()
    for arrival, copy in zip(ins, outs, strict=True):
        arrival.wait()
        copy.start()
    for copy in outs:
        copy.wait()


def settle(arrays):
    hbm = pl.BlockSpec(memory_space=pl.ANY)
    return pl.pallas_call(
        settle_kernel,
        out_shape=tuple(jax.ShapeDtypeStruct(a.shape, a.dtype) for a in arrays),
        in_specs=[hbm] * len(arrays),
        out_specs=(hbm,) * len(arrays),
        scratch_shapes=[pltpu.VMEM(a.shape, a.dtype) for a in arrays]
        + [pltpu.SemaphoreType.DMA((24,)), pltpu.SemaphoreType.DMA((24,))],
        compiler_params=pltpu.CompilerParams(vmem_limit_bytes=63 * MIB),
        name="settle",
    )(*arrays)


def shards(tokens, segment_ids, q_weight, key_value_weight, o_weight, cotangent):
    weights = (q_weight, key_value_weight, o_weight)
    token_blocks, cot_blocks, proj, d_attn = project(tokens, cotangent, *weights)
    cosine, sine = rope_tables(tokens.shape[0], HEAD_SIZE)
    cosine = jnp.concatenate([cosine, cosine], axis=1)
    sine = jnp.concatenate([-sine, sine], axis=1)
    blocks = (token_blocks, cot_blocks)
    return settle(finish(proj, d_attn, cosine, sine, segment_ids, weights, blocks))


def solution(mesh):
    in_specs = (
        P("blk", None),
        P("blk", None),
        P("blk", "tp"),
        P("blk", "tp"),
        P("blk", "tp"),
        P("blk", None),
    )
    out_specs = (P("blk", None), P("blk", "tp"), P("blk", "tp"), P("blk", "tp"), P("blk", "tp"))
    return jax.shard_map(shards, mesh=mesh, in_specs=in_specs, out_specs=out_specs, check_vma=False)
```

```python
import math

import jax
import jax.numpy as jnp
from jax import lax
from jax.experimental import pallas as pl
from jax.experimental.pallas import tpu as pltpu
from jax.sharding import PartitionSpec as P

HEAD_SIZE = 128


THETA = 10000.0


def rope_tables(length, width):
    half_width = width // 2
    position = jnp.arange(length, dtype=jnp.float32)[:, None]
    channel = jnp.arange(half_width, dtype=jnp.float32)[None, :]
    angle = position * jnp.power(THETA, -2.0 * channel / width)
    return (jnp.cos(angle), jnp.sin(angle))


MESH = pl.DeviceIdType.MESH
BF16 = jnp.bfloat16
F32 = jnp.float32
MIB = 1 << 20


def here():
    blk, tp = lax.axis_index("blk"), lax.axis_index("tp")
    return blk // 4, blk % 4, tp // 4, tp // 2 % 2, tp % 2


def near(place, dh=0, dx=0, dz=0, dl=0, dc=0):
    h, x, z, low, core = place
    h, low, core = (h + dh) % 2, (low + dl) % 2, (core + dc) % 2
    x, z = (x + dx + 4) % 4, (z + dz + 4) % 4
    return h * 4 + x, z * 4 + low * 2 + core


def greet(devices):
    barrier = pltpu.get_barrier_semaphore()
    for device in devices:
        pl.semaphore_signal(barrier, inc=1, device_id=device, device_id_type=MESH)
    pl.semaphore_wait(barrier, len(devices))


def send(source, target, sems, device):
    copy = pltpu.make_async_remote_copy(
        src_ref=source,
        dst_ref=target,
        send_sem=sems[0],
        recv_sem=sems[1],
        device_id=device,
        device_id_type=MESH,
    )
    copy.start()
    return copy


def arrived(ref, sem):
    pltpu.make_async_copy(ref, ref, sem).wait()


def load_weights(q_weight, kv_weight, o_source, in_weight, o_weight, sems):
    width = q_weight.shape[1]
    kv_part = pl.ds(width, kv_weight.shape[1])
    loads = [
        pltpu.make_async_copy(q_weight, in_weight.at[:, pl.ds(0, width)], sems.at[0]),
        pltpu.make_async_copy(kv_weight, in_weight.at[:, kv_part], sems.at[1]),
        pltpu.make_async_copy(o_source, o_weight, sems.at[2]),
    ]
    for held in loads:
        held.start()
    return loads


CHUNKS = ((0, 2), (1, 2), (1, 1), (0, 3), (0, 1), (1, 3), (1, 0), (0, 0))


def project_kernel(
    tokens, cot, q_weight, kv_weight, o_source, token_out, cot_out, proj_out, d_attn_out,
    in_weight, o_weight, weight_sem, blocks, proj_send, proj_recv, cot_send, cot_recv,
    a2a_s, a2a_r, up_s, up_r, down_s, down_r, far_s, far_r, core_s, core_r, sum_s, sum_r, keep,
):
    place = here()
    h, x, z, low, core = place
    seat = z * 2 + core
    height = blocks.shape[2] // 8
    width = blocks.shape[3]
    right, left = near(place, dx=1), near(place, dx=-1)
    above, below = near(place, dz=1), near(place, dz=-1)
    twin, across = near(place, dc=1), near(place, dh=1)
    shifts = [shift for shift in CHUNKS if shift != (0, 0)]
    loads = load_weights(q_weight, kv_weight, o_source, in_weight, o_weight, weight_sem)
    greet([near(place, dh=dh, dx=dx) for dh, dx in shifts] + [above, below, twin])
    sent = []

    def rows(a, dh, dx, at):
        return blocks.at[a, dh * 4 + dx, pl.ds(pl.multiple_of(at * height, height), height)]

    def level(dz):
        return (z + dz + 4) % 4 * 2 + core

    def index(dh, dx):
        return dh * 4 + dx

    def start_blocks(a, source):
        for dh, dx in CHUNKS:
            target = near(place, dh=dh, dx=dx)
            piece = source.at[
                pl.ds(pl.multiple_of(seat * height, height), height),
                pl.ds(pl.multiple_of(target[0] * width, width), width),
            ]
            j = index(dh, dx)
            if j:
                sent.append(send(piece, rows(a, dh, dx, seat), (a2a_s.at[a, j], a2a_r.at[a, j]), target))
            else:
                pltpu.make_async_copy(piece, rows(a, 0, 0, seat), a2a_r.at[a, 0]).start()

    def to_twin(a, dh, dx, which, at):
        j = index(dh, dx)
        piece = rows(a, dh, dx, at)
        sent.append(send(piece, piece, (core_s.at[a, j, which], core_r.at[a, j, which]), twin))

    def first_stage(a, dh, dx):
        j = index(dh, dx)
        piece = rows(a, dh, dx, seat)
        arrived(piece, a2a_r.at[a, j])
        sent.append(send(piece, piece, (up_s.at[a, j], up_r.at[a, j]), above))
        sent.append(send(piece, piece, (down_s.at[a, j], down_r.at[a, j]), below))
        to_twin(a, dh, dx, 0, seat)

    def second_stage(a, dh, dx):
        j = index(dh, dx)
        sems = (far_s.at[a, j], far_r.at[a, j])
        lower, upper = rows(a, dh, dx, level(-1)), rows(a, dh, dx, level(1))
        arrived(lower, up_r.at[a, j])
        if dh == 0:
            sent.append(send(lower, lower, sems, above))
        to_twin(a, dh, dx, 1, level(-1))
        arrived(upper, down_r.at[a, j])
        if dh == 1:
            sent.append(send(upper, upper, sems, below))
        to_twin(a, dh, dx, 2, level(1))

    def third_stage(a, dh, dx):
        j = index(dh, dx)
        arrived(rows(a, dh, dx, level(2)), far_r.at[a, j])
        to_twin(a, dh, dx, 3, level(2))

    def complete(a, dh, dx):
        j = index(dh, dx)
        for which, dz in enumerate((0, -1, 1, 2)):
            seat_there = (z + dz + 4) % 4 * 2 + (1 - core)
            arrived(rows(a, dh, dx, seat_there), core_r.at[a, j, which])

    outs, keeps = (token_out, cot_out), []
    weights = (in_weight, o_weight)
    outgoing = (proj_send, cot_send)
    incoming = (proj_recv, cot_recv)
    results = (proj_out, d_attn_out)
    adds = {4: (0,), 5: (1,), 6: (2, 5), 7: (3, 4, 6)}
    ways = (left, right, left, right, left, right, across)

    def chunk(a, k):
        dh, dx = CHUNKS[k]
        j = index(dh, dx)
        complete(a, dh, dx)
        copy = pltpu.make_async_copy(blocks.at[a, j], outs[a].at[j], keep.at[a, j])
        copy.start()
        keeps.append(copy)
        terms = adds.get(k, ())
        for term in terms:
            arrived(incoming[a].at[term], sum_r.at[a, term])
        target = outgoing[a].at[k] if k < 7 else results[a]
        tile = blocks.shape[2] // 2

        @pl.loop(0, 2)
        def _(step):
            part = pl.ds(pl.multiple_of(step * tile, tile), tile)
            total = jnp.dot(blocks[a, j, part, :], weights[a][...], preferred_element_type=F32)
            for term in terms:
                total = total + incoming[a][term, part, :].astype(F32)
            target[part, :] = total.astype(target.dtype)

        if k < 7:
            sent.append(send(target, incoming[a].at[k], (sum_s.at[a, k], sum_r.at[a, k]), ways[k]))

    start_blocks(0, tokens)
    start_blocks(1, cot)
    pieces = [(a, k) for a in range(2) for k in range(8)]
    waiting = [(0, 0), (0, 1), (0, 2), (0, 3), (0, 4), (0, 5), (0, 6), (1, 0), (1, 1), (1, 2), (1, 3)]
    waiting += [(0, 7), (1, 4), (1, 5), (1, 6), (1, 7)]
    late = {(0, 6): 7, (0, 7): 9}
    for step in range(len(pieces) + 5):
        for stage, lag in ((first_stage, 0), (second_stage, 2), (third_stage, 4)):
            if 0 <= step - lag < len(pieces):
                a, k = pieces[step - lag]
                stage(a, *CHUNKS[k])
        if step == 4:
            for held in loads:
                held.wait()
        while waiting and pieces.index(waiting[0]) + late.get(waiting[0], 5) <= step:
            chunk(*waiting.pop(0))
    assert not waiting
    for copy in sent:
        copy.wait_send()
    for copy in keeps:
        copy.wait()


def project(tokens, cot, q_weight, kv_weight, o_weight):
    length = tokens.shape[0]
    width = tokens.shape[1] // 8
    in_width, o_width = q_weight.shape[1] + kv_weight.shape[1], o_weight.shape[1]
    depth = q_weight.shape[0]
    dma = pltpu.SemaphoreType.DMA
    pair = [dma((2, 8)), dma((2, 8))]
    block = jax.ShapeDtypeStruct((8, length, width), BF16)
    return pl.pallas_call(
        project_kernel,
        out_shape=(
            block,
            block,
            jax.ShapeDtypeStruct((length, in_width), F32),
            jax.ShapeDtypeStruct((length, o_width), BF16),
        ),
        in_specs=[pl.BlockSpec(memory_space=pl.ANY)] * 5,
        out_specs=(pl.BlockSpec(memory_space=pl.ANY),) * 2
        + (pl.BlockSpec(memory_space=pltpu.VMEM),) * 2,
        scratch_shapes=[
            pltpu.VMEM((depth, in_width), BF16),
            pltpu.VMEM((depth, o_width), BF16),
            dma((3,)),
            pltpu.VMEM((2, 8, length, width), BF16),
            pltpu.VMEM((7, length, in_width), BF16),
            pltpu.VMEM((7, length, in_width), BF16),
            pltpu.VMEM((7, length, o_width), BF16),
            pltpu.VMEM((7, length, o_width), BF16),
            *pair,
            *pair,
            *pair,
            *pair,
            dma((2, 8, 4)),
            dma((2, 8, 4)),
            dma((2, 7)),
            dma((2, 7)),
            dma((2, 8)),
        ],
        compiler_params=pltpu.CompilerParams(
            collective_id=0, has_side_effects=True, vmem_limit_bytes=56 * MIB
        ),
        name="project",
    )(tokens, cot, q_weight, kv_weight, o_weight)


def nt(left, right):
    return lax.dot_general(left, right, (((1,), (1,)), ((), ())), preferred_element_type=F32)


def tn(left, right):
    return lax.dot_general(left, right, (((0,), (0,)), ((), ())), preferred_element_type=F32)


def swap_halves(array):
    return pltpu.roll(array, array.shape[1] // 2, 1)


LEVELS = (2, -1, 1, 0)


def finish_kernel(
    proj, d_attn, cosine, sine, seg_row, q_weight, kv_weight, o_source, token_blocks, cot_blocks,
    mixed, d_tokens, q_grad, kv_grad, o_grad, in_weight, o_weight, weight_sem,
    attn_all, grad_all, q_rot, probs, bias, seg_cols, keys, values, kv_send, kv_recv, key_sum, value_sum,
    kv_grad_send, kv_grad_recv,
    half_send, half_recv, level_send, level_recv, side_send, side_recv, cross_send, cross_recv,
    plane_send, plane_recv, last_send, last_recv,
    column, grad_sum,
    kv_sems, ring_s, ring_r, half_s, half_r, level_s, level_r, side_sems, cross_s, cross_r,
    plane_s, plane_r, hand_s, hand_r,
    mixed_s, mixed_r, twin_s, twin_r, column_sem, out_sem,
):
    place = here()
    h, x, z, low, core = place
    blk = h * 4 + x
    length, q_width = d_attn.shape
    tile = length // 2
    score_scale = 1.0 / math.sqrt(HEAD_SIZE)
    right, left = near(place, dx=1), near(place, dx=-1)
    above, below = near(place, dz=1), near(place, dz=-1)
    twin, across, beside = near(place, dc=1), near(place, dh=1), near(place, dl=1)
    halves = []
    far_h, far_x = z // 2, z % 2 * 2 + low
    origin = z * 2 + low
    origin_h, origin_x = (origin // 4 + h) % 2, (origin % 4 - x + 4) % 4
    homes = (
        near(place, dh=far_h, dx=-far_x),
        (near(place, dh=far_h, dx=-far_x)[0], blk * 2 + core),
    )
    givers = (
        near(place, dh=far_h, dx=far_x),
        (origin, (origin_h * 2 + origin_x // 2) * 4 + origin_x % 2 * 2 + core),
    )
    stays = (z * 2 + low == 0, z * 2 + low + blk == 0)
    sent, halves = [], []
    loads = load_weights(q_weight, kv_weight, o_source, in_weight, o_weight, weight_sem)

    barrier = pltpu.get_barrier_semaphore()
    for device in (right, left, above, below, twin, across, beside):
        pl.semaphore_signal(barrier, inc=1, device_id=device, device_id_type=MESH)
    for i in range(2):

        @pl.when(jnp.logical_not(stays[i]))
        def _():
            pl.semaphore_signal(barrier, inc=1, device_id=givers[i], device_id_type=MESH)

    pl.semaphore_wait(barrier, 9 - jnp.where(stays[0], 1, 0) - jnp.where(stays[1], 1, 0))

    def post(source, target, sems, device):
        sent.append(send(source, target, sems, device))

    lane = lax.broadcasted_iota(jnp.int32, (length, HEAD_SIZE), 1)
    in_front = lane < HEAD_SIZE // 2
    is_lower = jnp.full((length, HEAD_SIZE), core) == 0
    kv_send[...] = proj[:, q_width:].astype(BF16)
    post(kv_send, kv_recv, (kv_sems.at[0], kv_sems.at[1]), twin)
    seg_col = jnp.transpose(jnp.broadcast_to(seg_row[...].astype(F32), (HEAD_SIZE, length)))[:, :1]
    seg_cols[...] = jnp.broadcast_to(seg_col, seg_cols.shape)

    @pl.loop(0, 2)
    def _(step):
        start = pl.multiple_of(step * tile, tile)
        part = pl.ds(start, tile)
        row = lax.broadcasted_iota(jnp.int32, (tile, length), 0) + start
        key = lax.broadcasted_iota(jnp.int32, (tile, length), 1)
        allowed = (key <= row) & (seg_cols[part, :1] == seg_row[...].astype(F32))
        bias[part, :] = jnp.where(allowed, 0.0, -jnp.inf)

    @pl.loop(0, q_width // HEAD_SIZE)
    def _(head):
        cols = pl.ds(pl.multiple_of(head * HEAD_SIZE, HEAD_SIZE), HEAD_SIZE)
        query = proj[:, cols]
        q_rot[:, cols] = (query * cosine[...] + swap_halves(query) * sine[...]).astype(BF16)

    arrived(kv_recv, kv_sems.at[1])
    own, other = kv_send[...].astype(F32), kv_recv[...].astype(F32)
    lower, upper = jnp.where(is_lower, own, other), jnp.where(is_lower, other, own)
    key = jnp.where(in_front, lower, swap_halves(upper))
    keys[...] = (key * cosine[...] + swap_halves(key) * sine[...]).astype(BF16)
    values[...] = jnp.where(in_front, swap_halves(lower), upper).astype(BF16)

    @pl.loop(0, q_width // HEAD_SIZE)
    def _(head):
        cols = pl.ds(pl.multiple_of(head * HEAD_SIZE, HEAD_SIZE), HEAD_SIZE)

        @pl.loop(0, 2)
        def _(step):
            part = pl.ds(pl.multiple_of(step * tile, tile), tile)
            scores = nt(q_rot[part, cols], keys[...]) * score_scale + bias[part, :]
            raised = jnp.exp(scores - jnp.max(scores, axis=1, keepdims=True))
            prob = raised / jnp.sum(raised, axis=1, keepdims=True)
            probs[head, part, :] = prob
            mixed_values = jnp.dot(prob.astype(BF16), values[...], preferred_element_type=F32)
            attn_all[0, part, cols] = mixed_values.astype(BF16)

    rings = (attn_all, grad_all)

    def hop(i, k, source, target, device):
        ring = rings[i]
        post(ring.at[source], ring.at[target], (ring_s.at[i, k], ring_r.at[i, k]), device)

    def ring_wait(i, k, target):
        arrived(rings[i].at[target], ring_r.at[i, k])

    def ring_across(i):
        hop(i, 0, 0, 4, across)

    def ring_start(i):
        hop(i, 1, 0, 1, right)
        hop(i, 2, 0, 3, left)

    def ring_side(i):
        ring_wait(i, 0, 4)
        hop(i, 3, 4, 5, right)
        hop(i, 4, 4, 7, left)

    def ring_pass(i):
        ring_wait(i, 1, 1)
        hop(i, 5, 1, 2, right)

    def ring_back(i):
        ring_wait(i, 4, 7)
        hop(i, 6, 7, 6, left)

    def ring_end(i):
        for k, target in ((2, 3), (3, 5), (5, 2), (6, 6)):
            ring_wait(i, k, target)

    ring_across(0)
    ring_start(0)

    key_sum[...] = jnp.zeros_like(key_sum)
    value_sum[...] = jnp.zeros_like(value_sum)

    @pl.loop(0, q_width // HEAD_SIZE)
    def _(head):
        cols = pl.ds(pl.multiple_of(head * HEAD_SIZE, HEAD_SIZE), HEAD_SIZE)

        @pl.loop(0, 2)
        def _(step):
            part = pl.ds(pl.multiple_of(step * tile, tile), tile)
            d_out = d_attn[part, cols]
            prob = probs[head, part, :]
            d_prob = nt(d_out, values[...])
            row_delta = jnp.sum(prob * d_prob, axis=1, keepdims=True)
            d_score = (prob * (d_prob - row_delta) * score_scale).astype(BF16)
            d_query = jnp.dot(d_score, keys[...], preferred_element_type=F32)
            d_query = d_query * cosine[part, :] - swap_halves(d_query) * sine[part, :]
            grad_all[0, part, cols] = d_query.astype(BF16)
            key_sum[...] += tn(d_score, q_rot[part, cols])
            value_sum[...] += tn(prob.astype(BF16), d_out)

    d_key = key_sum[...] * cosine[...] - swap_halves(key_sum[...]) * sine[...]
    d_key, d_value = d_key.astype(BF16).astype(F32), value_sum[...].astype(BF16).astype(F32)
    lower = jnp.where(in_front, d_key, swap_halves(d_value))
    upper = jnp.where(in_front, swap_halves(d_key), d_value)
    kv_grad_send[...] = jnp.where(is_lower, upper, lower).astype(BF16)
    post(kv_grad_send, kv_grad_recv, (kv_sems.at[2], kv_sems.at[3]), twin)
    own = jnp.where(is_lower, lower, upper)
    arrived(kv_grad_recv, kv_sems.at[3])
    grad_all[0, :, q_width:] = (own + kv_grad_recv[...].astype(F32)).astype(BF16)

    weights = (o_weight, in_weight)
    half = o_weight.shape[0] // 2

    def spot(dz, side):
        return (z + dz + 4) % 4 * 2 + side

    def term(i, dz, side, which, part):
        rows = pl.ds(pl.multiple_of(which * half, half), half)
        return nt(rings[i][spot(dz, side), part, :], weights[i][rows, :])

    def give_half(i):
        for q, dz in enumerate(LEVELS):
            if i:
                halves[q].wait_send()
            for side in range(2):

                @pl.loop(0, 2)
                def _(step):
                    part = pl.ds(pl.multiple_of(step * tile, tile), tile)
                    half_send[q, side, part, :] = term(i, dz, side, 1 - core, part).astype(BF16)

            sems = (half_s.at[i, q], half_r.at[i, q])
            halves.append(send(half_send.at[q], half_recv.at[i, q], sems, twin))

    def half_wait(i, q):
        arrived(half_recv.at[i, q], half_r.at[i, q])

    def add_up(i, q, side, target, first, count, terms):
        part = pl.ds(first, count)
        total = term(i, LEVELS[q], side, core, part)
        total = total + half_recv[i, q, side, part, :].astype(F32)
        for ref in terms:
            total = total + ref[...].astype(F32)
        target[...] = total.astype(target.dtype)

    few = tile // 2

    def level_hop(i, k, slot, device):
        sems = (level_s.at[i, k], level_r.at[i, slot])
        post(level_send.at[i, k], level_recv.at[i, slot], sems, device)

    def level_wait(i, slot):
        arrived(level_recv.at[i, slot], level_r.at[i, slot])

    def cross(i, q):
        add_up(i, q, 1 - low, cross_send.at[i, q], tile, tile, ())
        post(cross_send.at[i, q], cross_recv.at[i, q], (cross_s.at[i, q], cross_r.at[i, q]), beside)

    def cross_wait(i, q):
        arrived(cross_recv.at[i, q], cross_r.at[i, q])

    def slab(ref, which):
        return ref.at[pl.ds(which * few, few)]

    def far_level(i):
        half_wait(i, 0)
        cross(i, 0)
        add_up(i, 0, 0, level_send.at[i, 0], 0, tile, ())
        level_hop(i, 0, 0, below)
        add_up(i, 0, 1, level_send.at[i, 1], 0, tile, ())
        level_hop(i, 1, 1, above)

    def near_level(i):
        half_wait(i, 1)
        cross(i, 1)
        add_up(i, 1, 1, level_send.at[i, 2], 0, tile, ())
        level_hop(i, 2, 3, below)
        half_wait(i, 2)
        cross(i, 2)
        add_up(i, 2, 0, level_send.at[i, 3], 0, tile, ())
        level_hop(i, 3, 4, above)
        half_wait(i, 3)
        cross(i, 3)

    def far_plane(i):
        cross_wait(i, 0)
        add_up(i, 0, low, plane_send.at[i, 0], tile, tile, (cross_recv.at[i, 0],))
        for which, k, device in ((0, 0, below), (1, 3, above)):
            sems = (plane_s.at[i, k], plane_r.at[i, k])
            post(slab(plane_send.at[i, 0], which), slab(plane_recv.at[i, 0], which), sems, device)

    def pass_level(i):
        level_wait(i, 0)
        add_up(i, 1, 0, level_send.at[i, 4], 0, tile, (level_recv.at[i, 0],))
        level_hop(i, 4, 2, below)
        level_wait(i, 1)
        add_up(i, 2, 1, level_send.at[i, 5], 0, tile, (level_recv.at[i, 1],))
        level_hop(i, 5, 5, above)

    def pass_plane(i):
        for q, joins, k, device in ((1, 0, 0, below), (2, 1, 3, above)):
            cross_wait(i, q)
            arrived(slab(plane_recv.at[i, 0], joins), plane_r.at[i, k])
            for which in range(2):
                terms = [slab(cross_recv.at[i, q], which)]
                if which == joins:
                    terms.append(slab(plane_recv.at[i, 0], which))
                add_up(i, q, low, slab(plane_send.at[i, q], which), tile + which * few, few, terms)
            sems = (plane_s.at[i, q], plane_r.at[i, q])
            post(plane_send.at[i, q], plane_recv.at[i, q], sems, device)

    def own_level(i):
        for slot in range(2, 6):
            level_wait(i, slot)
        terms = (level_recv.at[i, 2 + 1 - low], level_recv.at[i, 4 + 1 - low])
        add_up(i, 3, 1 - low, side_send.at[i], 0, tile, terms)
        post(side_send.at[i], side_recv.at[i], (side_sems.at[i, 0], side_sems.at[i, 1]), beside)

    tp_width = half

    def columns(t):
        return mixed.at[:, pl.ds(pl.multiple_of(t * tp_width, tp_width), tp_width)]

    def tp_at(dz, dl, dc=0):
        level, side = (z + dz + 4) % 4, (low + dl) % 2
        owner = (h + level // 2) % 2 * 4 + (x + level % 2 * 2 + side) % 4
        return owner * 2 + (core + dc) % 2

    def last_target(i):
        return columns(tp_at(0, 0)) if i == 0 else last_recv

    def last_level(i):
        cross_wait(i, 3)
        for q in (1, 2):
            arrived(plane_recv.at[i, q], plane_r.at[i, q])
        terms = (cross_recv.at[i, 3], plane_recv.at[i, 1], plane_recv.at[i, 2])
        add_up(i, 3, low, last_send.at[i, pl.ds(tile, tile)], tile, tile, terms)
        arrived(side_recv.at[i], side_sems.at[i, 1])
        terms = (level_recv.at[i, 2 + low], level_recv.at[i, 4 + low], side_recv.at[i])
        add_up(i, 3, low, last_send.at[i, pl.ds(0, tile)], 0, tile, terms)
        there = columns(blk * 2 + core) if i == 0 else last_recv

        @pl.when(jnp.logical_not(stays[i]))
        def _():
            send(last_send.at[i], there, (hand_s.at[i], hand_r.at[i]), homes[i])

        @pl.when(stays[i])
        def _():
            pltpu.make_async_copy(last_send.at[i], last_target(i), hand_r.at[i]).start()

    def hand_end(i):
        arrived(last_target(i), hand_r.at[i])

    def hand_sent(i):
        @pl.when(jnp.logical_not(stays[i]))
        def _():
            arrived(last_send.at[i], hand_s.at[i])

    whole, top, bottom = (0, length), (0, tile), (tile, tile)
    quarters = ((tile, tile // 2), (tile + tile // 2, tile // 2))

    def cell(t, rows):
        return columns(t).at[pl.ds(*rows)]

    def mixed_hop(k, t, rows, device):
        post(cell(t, rows), cell(t, rows), (mixed_s.at[k], mixed_r.at[k]), device)

    def mixed_wait(k, t, rows):
        arrived(cell(t, rows), mixed_r.at[k])

    given = []

    def mixed_twin(dz, dl, rows):
        k, t = len(given), tp_at(dz, dl)
        given.append((tp_at(dz, dl, 1), rows))
        post(cell(t, rows), cell(t, rows), (twin_s.at[k], twin_r.at[k]), twin)

    def mixed_start():
        hand_end(0)
        mixed_hop(0, tp_at(0, 0), top, beside)
        mixed_hop(7, tp_at(0, 0), bottom, above)
        mixed_hop(8, tp_at(0, 0), bottom, below)
        mixed_hop(1, tp_at(0, 0), top, above)
        mixed_hop(2, tp_at(0, 0), top, below)
        mixed_hop(11, tp_at(0, 0), bottom, beside)
        mixed_twin(0, 0, whole)

    def mixed_side():
        mixed_wait(0, tp_at(0, 1), top)
        mixed_hop(3, tp_at(0, 1), top, above)
        mixed_hop(4, tp_at(0, 1), top, below)
        mixed_twin(0, 1, top)

    def mixed_bottom():
        mixed_wait(7, tp_at(-1, 0), bottom)
        mixed_hop(9, tp_at(-1, 0), quarters[0], above)
        mixed_hop(12, tp_at(-1, 0), bottom, beside)
        mixed_twin(-1, 0, bottom)
        mixed_wait(8, tp_at(1, 0), bottom)
        mixed_hop(10, tp_at(1, 0), quarters[1], below)
        mixed_hop(13, tp_at(1, 0), bottom, beside)
        mixed_twin(1, 0, bottom)

    def mixed_pass():
        mixed_wait(1, tp_at(-1, 0), top)
        mixed_hop(5, tp_at(-1, 0), top, above)
        mixed_twin(-1, 0, top)
        mixed_wait(2, tp_at(1, 0), top)
        mixed_twin(1, 0, top)

    def mixed_back():
        mixed_wait(4, tp_at(1, 1), top)
        mixed_hop(6, tp_at(1, 1), top, below)
        mixed_twin(1, 1, top)

    def mixed_far():
        mixed_wait(9, tp_at(2, 0), quarters[0])
        mixed_wait(10, tp_at(2, 0), quarters[1])
        mixed_hop(14, tp_at(2, 0), bottom, beside)
        mixed_twin(2, 0, bottom)
        mixed_wait(11, tp_at(0, 1), bottom)
        mixed_twin(0, 1, bottom)
        mixed_wait(12, tp_at(-1, 1), bottom)
        mixed_twin(-1, 1, bottom)
        mixed_wait(13, tp_at(1, 1), bottom)
        mixed_twin(1, 1, bottom)

    def mixed_end():
        for k, dz, dl, rows in ((3, -1, 1, top), (5, 2, 0, top), (6, 2, 1, top), (14, 2, 1, bottom)):
            mixed_wait(k, tp_at(dz, dl), rows)
            mixed_twin(dz, dl, rows)
        for k, (t, rows) in enumerate(given):
            arrived(cell(t, rows), twin_r.at[k])

    sources = (cot_blocks, token_blocks)
    order = (0, 4, 1, 3, 5, 7, 2, 6)
    steps = [(i, j) for i in range(2) for j in order]

    def load(n):
        i, j = steps[n]
        pltpu.make_async_copy(sources[i].at[j], column.at[n % 2], column_sem.at[n % 2]).start()

    def grad_step(n):
        i, j = steps[n]
        slot = n % 2
        arrived(column.at[slot], column_sem.at[slot])
        width = rings[i].shape[2]
        strip = 256

        @pl.loop(0, column.shape[2] // strip)
        def _(step):
            part = pl.ds(pl.multiple_of(step * strip, strip), strip)
            value = tn(column[slot, :, part], rings[i][j])
            if n % 8:
                value = value + grad_sum[part, :width]
            if n % 8 < 7:
                grad_sum[part, :width] = value
            elif i == 0:
                o_grad[part, :] = value.astype(BF16)
            else:
                q_grad[part, :] = value[:, :q_width].astype(BF16)
                kv_grad[part, :] = value[:, q_width:].astype(BF16)

        if n + 2 < len(steps):
            load(n + 2)

    load(0)
    load(1)
    ring_across(1)
    grad_step(0)
    ring_side(0)
    grad_step(1)
    ring_pass(0)
    grad_step(2)
    ring_back(0)
    ring_start(1)
    ring_side(1)
    ring_end(0)
    for held in loads:
        held.wait()
    give_half(0)
    far_level(0)
    near_level(0)
    ring_pass(1)
    far_plane(0)
    pass_level(0)
    grad_step(3)
    grad_step(4)
    pass_plane(0)
    grad_step(5)
    ring_back(1)
    own_level(0)
    grad_step(6)
    grad_step(7)
    last_level(0)
    ring_end(1)
    give_half(1)
    far_level(1)
    near_level(1)
    far_plane(1)
    pass_level(1)
    mixed_start()
    grad_step(8)
    grad_step(9)
    pass_plane(1)
    grad_step(10)
    mixed_side()
    grad_step(11)
    own_level(1)
    mixed_bottom()
    grad_step(12)
    mixed_pass()
    grad_step(13)
    grad_step(14)
    grad_step(15)
    last_level(1)
    mixed_far()
    mixed_back()
    mixed_end()
    hand_end(1)
    out = pltpu.make_async_copy(last_recv, d_tokens, out_sem)
    out.start()
    for copy in sent + halves[4:]:
        copy.wait_send()
    hand_sent(0)
    hand_sent(1)
    out.wait()


def finish(proj, d_attn, cosine, sine, segments, weights, blocks):
    length, q_width = d_attn.shape
    in_width = proj.shape[1]
    depth = weights[0].shape[0]
    half = depth // 2
    heads = q_width // HEAD_SIZE
    dma = pltpu.SemaphoreType.DMA
    vmem = pl.BlockSpec(memory_space=pltpu.VMEM)
    hbm = pl.BlockSpec(memory_space=pl.ANY)
    part = pltpu.VMEM((length, HEAD_SIZE), BF16)
    part_sum = pltpu.VMEM((length, HEAD_SIZE), F32)
    return pl.pallas_call(
        finish_kernel,
        out_shape=(
            jax.ShapeDtypeStruct((length, 16 * half), BF16),
            jax.ShapeDtypeStruct((length, half), BF16),
            jax.ShapeDtypeStruct((depth, q_width), BF16),
            jax.ShapeDtypeStruct((depth, in_width - q_width), BF16),
            jax.ShapeDtypeStruct((depth, q_width), BF16),
        ),
        in_specs=[vmem] * 5 + [hbm] * 5,
        out_specs=(hbm, hbm, vmem, vmem, vmem),
        scratch_shapes=[
            pltpu.VMEM((depth, in_width), BF16),
            pltpu.VMEM((depth, q_width), BF16),
            dma((3,)),
            pltpu.VMEM((8, length, q_width), BF16),
            pltpu.VMEM((8, length, in_width), BF16),
            pltpu.VMEM((length, q_width), BF16),
            pltpu.VMEM((heads, length, length), F32),
            pltpu.VMEM((length, length), F32),
            pltpu.VMEM((length, HEAD_SIZE), F32),
            part,
            part,
            part,
            part,
            part_sum,
            part_sum,
            part,
            part,
            pltpu.VMEM((4, 2, length, half), BF16),
            pltpu.VMEM((2, 4, 2, length, half), BF16),
            pltpu.VMEM((2, 6, length // 2, half), BF16),
            pltpu.VMEM((2, 6, length // 2, half), BF16),
            pltpu.VMEM((2, length // 2, half), BF16),
            pltpu.VMEM((2, length // 2, half), BF16),
            pltpu.VMEM((2, 4, length // 2, half), BF16),
            pltpu.VMEM((2, 4, length // 2, half), BF16),
            pltpu.VMEM((2, 3, length // 2, half), BF16),
            pltpu.VMEM((2, 3, length // 2, half), BF16),
            pltpu.VMEM((2, length, half), BF16),
            pltpu.VMEM((length, half), BF16),
            pltpu.VMEM((2, length, depth), BF16),
            pltpu.VMEM((depth, in_width), F32),
            dma((4,)),
            dma((2, 7)),
            dma((2, 7)),
            dma((2, 4)),
            dma((2, 4)),
            dma((2, 6)),
            dma((2, 6)),
            dma((2, 2)),
            dma((2, 4)),
            dma((2, 4)),
            dma((2, 4)),
            dma((2, 4)),
            dma((2,)),
            dma((2,)),
            dma((15,)),
            dma((15,)),
            dma((15,)),
            dma((15,)),
            dma((2,)),
            dma,
        ],
        compiler_params=pltpu.CompilerParams(
            collective_id=1, has_side_effects=True, vmem_limit_bytes=63 * MIB
        ),
        name="finish",
    )(
        proj, d_attn, cosine, sine, segments, *weights, *blocks
    )


def settle_kernel(*refs):
    count = (len(refs) - 2) // 3
    sources, targets, buffers = refs[:count], refs[count : 2 * count], refs[2 * count : 3 * count]
    in_sems, out_sems = refs[-2:]
    parts = []
    for source, target, buffer in zip(sources, targets, buffers, strict=True):
        pieces = 16 if source.shape[1] > 1024 else 2
        rows = source.shape[0] // pieces
        for piece in range(pieces):
            part = pl.ds(piece * rows, rows)
            parts.append((source.at[part], buffer.at[part], target.at[part]))
    ins = [pltpu.make_async_copy(a, b, in_sems.at[n]) for n, (a, b, _) in enumerate(parts)]
    outs = [pltpu.make_async_copy(b, c, out_sems.at[n]) for n, (_, b, c) in enumerate(parts)]
    for copy in ins:
        copy.start()
    for arrival, copy in zip(ins, outs, strict=True):
        arrival.wait()
        copy.start()
    for copy in outs:
        copy.wait()


def settle(arrays):
    hbm = pl.BlockSpec(memory_space=pl.ANY)
    return pl.pallas_call(
        settle_kernel,
        out_shape=tuple(jax.ShapeDtypeStruct(a.shape, a.dtype) for a in arrays),
        in_specs=[hbm] * len(arrays),
        out_specs=(hbm,) * len(arrays),
        scratch_shapes=[pltpu.VMEM(a.shape, a.dtype) for a in arrays]
        + [pltpu.SemaphoreType.DMA((24,)), pltpu.SemaphoreType.DMA((24,))],
        compiler_params=pltpu.CompilerParams(vmem_limit_bytes=63 * MIB),
        name="settle",
    )(*arrays)


def shards(tokens, segment_ids, q_weight, key_value_weight, o_weight, cotangent):
    weights = (q_weight, key_value_weight, o_weight)
    token_blocks, cot_blocks, proj, d_attn = project(tokens, cotangent, *weights)
    cosine, sine = rope_tables(tokens.shape[0], HEAD_SIZE)
    cosine = jnp.concatenate([cosine, cosine], axis=1)
    sine = jnp.concatenate([-sine, sine], axis=1)
    blocks = (token_blocks, cot_blocks)
    return settle(finish(proj, d_attn, cosine, sine, segment_ids, weights, blocks))


def solution(mesh):
    in_specs = (
        P("blk", None),
        P("blk", None),
        P("blk", "tp"),
        P("blk", "tp"),
        P("blk", "tp"),
        P("blk", None),
    )
    out_specs = (P("blk", None), P("blk", "tp"), P("blk", "tp"), P("blk", "tp"), P("blk", "tp"))
    return jax.shard_map(shards, mesh=mesh, in_specs=in_specs, out_specs=out_specs, check_vma=False)
```
